256 devices in a mesh: src: 64 (over z, y_lo, x), rcv: 4 (over y_hi, core).
Axes of the slice: x: 4, y: 4 (y_hi: 2, y_lo: 2; y = y_hi * 2 + y_lo), z: 8, core: 2. Of those that a mesh axis runs over, the one named last changes fastest.
Arguments:
- probes: bfloat16 [256, 1024, 256], P('rcv', 'src'), may hold values from -6 to 6
- kappa: float32 [1024, 256], P('src'), may hold values from 0.02 to 0.24
- footprint: bfloat16 [64, 4, 192, 128, 128], P('src', 'rcv'), may hold values from -0.0390625 to 0.0390625
- block_source: int32 [64, 4, 192], P('src', 'rcv'), may hold values from 0 to 31
- block_receptor: int32 [64, 4, 192], P('src', 'rcv'), may hold values from 0 to 15
- block_count: int32 [64, 4], P('src', 'rcv'), may hold values from 1 to 192, as said below
- obs_weight: float32 [8192], P('rcv'), may hold values from 1 to 8
Outputs:
- hessian_probe: float32 [256, 1024, 256], P('rcv', 'src')
The draws below stay inside these ranges and needn't reach their ends.
Inputs may be any that keep to these rules, and one draw needn't show every extreme that they name: Slots 0 to block_count - 1 of a tile and group hold its footprint blocks, later slots are unused; some tile and group uses all 192 slots.
All inputs are finite; a program needn't handle non-finite values.
Results may differ from the reference program's by a relative error of at most 0.006.
Values may be sent and summed in bfloat16 or wider, within the bound.
A program may use at most 64 MiB of HBM per device.

```python
import math
import jax
import jax.numpy as jnp
from jax import lax

BLK = 128
NLON = 256
RB_LOC = 16
NB = 192
SMOOTH = 4
SB = 32
NLAT = 1024
P_SIZE = 256
NREC = 8192
N_SRC = 64
N_RCV = 4


def draw_block_count(key, part):
    first_key, second_key, third_key = jax.random.split(key, 3)
    factor_one = jax.random.randint(first_key, (N_SRC, N_RCV), 0, NB)
    factor_two = jax.random.randint(second_key, (N_SRC, N_RCV), 0, NB)
    counts = factor_one * factor_two // NB + 1
    busiest = jax.random.randint(third_key, (), 0, N_SRC * N_RCV)
    flat_counts = jnp.where(jnp.arange(N_SRC * N_RCV) == busiest, NB, counts.reshape(-1))
    return flat_counts.reshape(N_SRC, N_RCV).astype(jnp.int32)


def touch_ends(drawn, own_key, smallest, largest):
    index_at = [jax.random.randint(jax.random.fold_in(own_key, axis), (), 0, length) for axis, length in enumerate(drawn.shape)]
    longest = drawn.shape.index(max(drawn.shape))
    neighbour = index_at[:longest] + [(index_at[longest] + 1) % drawn.shape[longest]] + index_at[longest + 1:]
    return drawn.at[tuple(index_at)].set(smallest).at[tuple(neighbour)].set(largest)


def shard_levels(rng, shape, shards, low, high):
    level, own = 1.0, jax.random.fold_in(rng, 6)
    for position, blocks in shards:
        heights = jnp.exp(jax.random.uniform(jax.random.fold_in(own, position), (blocks,), jnp.float32, low / len(shards), high / len(shards)))
        level = level * jnp.repeat(heights, shape[position] // blocks).reshape([-1 if axis == position else 1 for axis in range(len(shape))])
    return level


def centred(key, shape, spread, limit, cuts=(), kind=jnp.bfloat16):
    gain = shard_levels(key, shape, cuts, -0.22, 0.18) if cuts else 1.0
    entries = jax.random.normal(key, shape, jnp.float32) * spread * gain
    return jnp.minimum(jnp.maximum(entries, -limit), limit).astype(kind)


def setup_inputs(seed: int = 0) -> dict:
    key_list = jax.random.split(jax.random.key(seed), 8)
    probes = centred(key_list[0], (P_SIZE, NLAT, NLON), 1.0, 6.0, ((0, 4), (1, 64)))
    kappa = jnp.clip(jnp.exp(math.log(0.24) - 2.4849066 * jax.random.uniform(key_list[1], (NLAT, NLON), jnp.float32) ** shard_levels(key_list[1], (NLAT, NLON), ((0, 64),), -0.2, 0.2)), 0.02, 0.24)
    footprint = centred(key_list[2], (N_SRC, N_RCV, NB, BLK, BLK), (N_SRC * NB * BLK // (4 * RB_LOC)) ** -0.5, 0.0390625, ((0, 64), (1, 4)))
    block_source = touch_ends(jax.random.randint(key_list[3], (N_SRC, N_RCV, NB), 0, SB), jax.random.fold_in(key_list[3], 1), 0, SB - 1).astype(jnp.int32)
    block_receptor = touch_ends(jax.random.randint(key_list[4], (N_SRC, N_RCV, NB), 0, RB_LOC), jax.random.fold_in(key_list[4], 1), 0, RB_LOC - 1).astype(jnp.int32)
    block_count = draw_block_count(jax.random.fold_in(key_list[7], 71), 0)
    obs_weight = jnp.clip(jnp.exp(math.log(8.0) - 2.0794415 * jax.random.uniform(key_list[6], (NREC,), jnp.float32) ** shard_levels(key_list[6], (NREC,), ((0, 4),), -0.2, 0.2)), 1.0, 8.0)
    return {"probes": probes, "kappa": kappa, "footprint": footprint, "block_source": block_source, "block_receptor": block_receptor, "block_count": block_count, "obs_weight": obs_weight}


def laplacian_operator(emission_source_field):
    padded = jnp.pad(emission_source_field, ((0, 0), (1, 1), (1, 1)))
    return padded[:, 2:, 1:-1] + padded[:, :-2, 1:-1] + padded[:, 1:-1, 2:] + padded[:, 1:-1, :-2] - 4.0 * emission_source_field


def device_forward(blocks, sources, receptors, used_slots, tile_field):
    selected_entries = jnp.take(tile_field, sources, axis=0).astype(jnp.float32)
    hessian_result = jnp.einsum("nrc,ncp->nrp", blocks.astype(jnp.float32), selected_entries)
    in_use = jnp.arange(blocks.shape[0], dtype=jnp.int32) < used_slots
    onehot = ((receptors[:, None] == jnp.arange(RB_LOC, dtype=jnp.int32)[None, :]) & in_use[:, None]).astype(jnp.float32)
    return jnp.einsum("nrp,nb->brp", hessian_result, onehot, precision=lax.Precision.HIGHEST)


def device_adjoint(blocks, sources, receptors, used_slots, weighted_group):
    selected_entries = jnp.take(weighted_group, receptors, axis=0).astype(jnp.float32)
    hessian_result = jnp.einsum("nrc,nrp->ncp", blocks.astype(jnp.float32), selected_entries)
    in_use = jnp.arange(blocks.shape[0], dtype=jnp.int32) < used_slots
    onehot = ((sources[:, None] == jnp.arange(SB, dtype=jnp.int32)[None, :]) & in_use[:, None]).astype(jnp.float32)
    return jnp.einsum("ncp,ns->scp", hessian_result, onehot, precision=lax.Precision.HIGHEST)


def reference(probes, kappa, footprint, block_source, block_receptor, block_count, obs_weight):
    smoothed = probes.astype(jnp.float32)
    for repeat in range(SMOOTH):
        smoothed = smoothed + kappa * laplacian_operator(smoothed)
    truncated_field = lax.optimization_barrier(smoothed.astype(jnp.bfloat16))
    tile_fields = truncated_field.reshape(P_SIZE, N_SRC, SB, BLK).transpose(1, 2, 3, 0)

    def forward_tile(running, inputs):
        blocks, sources, receptors, counts, tile_field = inputs
        block_terms = jax.vmap(device_forward, in_axes=(0, 0, 0, 0, None))(blocks, sources, receptors, counts, tile_field)
        return running + block_terms, None

    initial = jnp.zeros((N_RCV, RB_LOC, BLK, P_SIZE), jnp.float32)
    evolved, unused = lax.scan(forward_tile, initial, (footprint, block_source, block_receptor, block_count, tile_fields))
    weighted = lax.optimization_barrier((obs_weight.reshape(N_RCV, RB_LOC, BLK, 1) * evolved).astype(jnp.bfloat16))

    def adjoint_tile(running, inputs):
        blocks, sources, receptors, counts = inputs
        block_terms = jax.vmap(device_adjoint)(blocks, sources, receptors, counts, weighted)
        rounded = lax.optimization_barrier(block_terms.astype(jnp.bfloat16))
        return running, jnp.sum(rounded.astype(jnp.float32), axis=0)

    dummy = jnp.zeros((), jnp.float32)
    dummy, adjoint_pass = lax.scan(adjoint_tile, dummy, (footprint, block_source, block_receptor, block_count))
    adjoint_pass = adjoint_pass.transpose(3, 0, 1, 2).reshape(P_SIZE, NLAT, NLON)
    back = adjoint_pass
    for repeat in range(SMOOTH):
        back = back + laplacian_operator(kappa * back)
    return probes.astype(jnp.float32) + back
```

```python
import functools

import jax
import jax.numpy as jnp
from jax import lax
from jax.experimental import pallas as pl
from jax.experimental.pallas import tpu as pltpu
from jax.sharding import PartitionSpec as P

BLK = 128
RB_LOC = 16
SMOOTH = 4
PLANE = 8
SLAB = 16
FETCH = 16
MESH = pl.DeviceIdType.MESH
VMEM = pltpu.VMEM
F32 = jnp.float32
BF16 = jnp.bfloat16
VMEM_LIMIT = 56 * 1024 * 1024


def barrier_with(devices):
    barrier = pltpu.get_barrier_semaphore()
    for device in devices:
        pl.semaphore_signal(barrier, inc=1, device_id=device, device_id_type=MESH)
    pl.semaphore_wait(barrier, len(devices))


def remote(src, dst, send_sem, recv_sem, device):
    return pltpu.make_async_remote_copy(
        src_ref=src,
        dst_ref=dst,
        send_sem=send_sem,
        recv_sem=recv_sem,
        device_id=device,
        device_id_type=MESH,
    )


def neighbours(n_src):
    me = lax.axis_index("src")
    group = lax.axis_index("rcv")
    high, core = group // 2, group % 2
    before = (lax.rem(me + n_src - 1, n_src), group)
    after = (lax.rem(me + 1, n_src), group)
    twin = high * 2 + (1 - core)
    opposite = (1 - high) * 2 + core
    return me, group, before, after, twin, opposite


def beside(centre):
    lanes = centre.shape[-1]
    lane = lax.broadcasted_iota(jnp.int32, centre.shape, centre.ndim - 1)
    west = jnp.where(lane == 0, 0.0, pltpu.roll(centre, 1, centre.ndim - 1))
    east = jnp.where(lane == lanes - 1, 0.0, pltpu.roll(centre, lanes - 1, centre.ndim - 1))
    return west + east


def spread_kappa(n_src, me, kext_ref, kwide):
    rows = kwide.shape[0]
    for row in range(rows):
        value = kext_ref[8 - SMOOTH + row : 8 - SMOOTH + row + 1, :]
        if row < SMOOTH:
            value = jnp.where(me == 0, 0.0, value)
        if row >= rows - SMOOTH:
            value = jnp.where(me == n_src - 1, 0.0, value)
        kwide[row] = jnp.broadcast_to(value, kwide.shape[1:])


def smooth_kernel(
    n_src, probes_ref, kappa_ref, field_ref, kext_ref, halo, wide, kwide, edge_send, edge_recv, send, recv
):
    me, group, before, after, twin, opposite = neighbours(n_src)
    lat, loc, lon = probes_ref.shape
    slabs = loc // SLAB
    src = me
    barrier_with([before, after, (src, twin), (src, opposite)])

    edges = [
        remote(probes_ref.at[pl.ds(lat - SMOOTH, SMOOTH)], halo.at[0], edge_send.at[0], edge_recv.at[0], after),
        remote(probes_ref.at[pl.ds(0, SMOOTH)], halo.at[1], edge_send.at[1], edge_recv.at[1], before),
        remote(kappa_ref.at[pl.ds(lat - 8, 8)], kext_ref.at[pl.ds(0, 8)], edge_send.at[2], edge_recv.at[2], after),
        remote(kappa_ref.at[pl.ds(0, 8)], kext_ref.at[pl.ds(lat + 8, 8)], edge_send.at[3], edge_recv.at[3], before),
    ]
    for copy in edges:
        copy.start()
    kext_ref[8 : lat + 8, :] = kappa_ref[...]
    wide[SMOOTH : lat + SMOOTH] = probes_ref[...].astype(F32)
    for copy in edges:
        copy.wait()
    wide[0:SMOOTH] = jnp.where(me == 0, 0.0, halo[0].astype(F32))
    wide[lat + SMOOTH :] = jnp.where(me == n_src - 1, 0.0, halo[1].astype(F32))
    spread_kappa(n_src, me, kext_ref, kwide)

    def place(owner, slab):
        return field_ref.at[:, pl.ds(pl.multiple_of(owner * loc + slab * SLAB, SLAB), SLAB), :]

    def to_twin(slab):
        return remote(place(group, slab), place(group, slab), send.at[0, slab], recv.at[0, slab], (src, twin))

    def to_opposite(slab):
        return remote(place(group, slab), place(group, slab), send.at[1, slab], recv.at[1, slab], (src, opposite))

    def relay(slab):
        return remote(place(opposite, slab), place(opposite, slab), send.at[2, slab], recv.at[2, slab], (src, twin))

    def one_slab(slab, carry):
        for half in range(SLAB // 8):
            some = pl.ds(pl.multiple_of(slab * SLAB + half * 8, 8), 8)
            value = wide[:, some, :]
            for step in range(SMOOTH):
                centre = value[1:-1]
                lap = value[:-2] + value[2:] + beside(centre) - 4.0 * centre
                value = centre + kwide[step + 1 : lat + 2 * SMOOTH - 1 - step] * lap
            wide[SMOOTH : lat + SMOOTH, some, :] = value
        some = pl.ds(pl.multiple_of(slab * SLAB, SLAB), SLAB)
        mine = pl.ds(pl.multiple_of(group * loc + slab * SLAB, SLAB), SLAB)
        field_ref[:, mine, :] = wide[SMOOTH : lat + SMOOTH, some, :].astype(BF16)
        to_opposite(slab).start()
        to_twin(slab).start()
        return carry

    lax.fori_loop(0, slabs, one_slab, 0)

    def pass_on(slab, carry):
        to_opposite(slab).wait_recv()
        relay(slab).start()
        return carry

    lax.fori_loop(0, slabs, pass_on, 0)

    def finish(slab, carry):
        to_opposite(slab).wait_send()
        to_twin(slab).wait()
        relay(slab).wait()
        return carry

    lax.fori_loop(0, slabs, finish, 0)


def smooth_and_gather(n_src, n_rcv, probes, kappa):
    lat, loc, lon = probes.shape
    slabs = loc // SLAB
    return pl.pallas_call(
        functools.partial(smooth_kernel, n_src),
        out_shape=(
            jax.ShapeDtypeStruct((lat, loc * n_rcv, lon), BF16),
            jax.ShapeDtypeStruct((lat + 16, lon), F32),
        ),
        in_specs=[pl.BlockSpec(memory_space=VMEM)] * 2,
        out_specs=(pl.BlockSpec(memory_space=VMEM),) * 2,
        scratch_shapes=[
            VMEM((2, SMOOTH, loc, lon), BF16),
            VMEM((lat + 2 * SMOOTH, loc, lon), F32),
            VMEM((lat + 2 * SMOOTH, 8, lon), F32),
            pltpu.SemaphoreType.DMA((4,)),
            pltpu.SemaphoreType.DMA((4,)),
            pltpu.SemaphoreType.DMA((3, slabs)),
            pltpu.SemaphoreType.DMA((3, slabs)),
        ],
        compiler_params=pltpu.CompilerParams(
            collective_id=0, has_side_effects=True, vmem_limit_bytes=VMEM_LIMIT
        ),
        name="smooth_and_gather",
    )(probes, kappa)


def each_used_block(count, blocks_ref, held, sems, work):
    fetches = (count + FETCH - 1) // FETCH

    def fetch(index):
        part = pl.ds(pl.multiple_of(index * FETCH, FETCH), FETCH)
        return pltpu.make_async_copy(blocks_ref.at[part], held.at[part], sems.at[index])

    def begin(index, carry):
        fetch(index).start()
        return carry

    def consume(index, carry):
        fetch(index).wait()
        first = index * FETCH
        here = jnp.minimum(count - first, FETCH)

        def several(turn, inner):
            work([first + turn * 4 + step for step in range(4)])
            return inner

        def single(turn, inner):
            work([first + turn])
            return inner

        lax.fori_loop(0, here // 4, several, 0)
        lax.fori_loop(here // 4 * 4, here, single, 0)
        return carry

    return (
        lambda: lax.fori_loop(0, fetches, begin, 0),
        lambda: lax.fori_loop(0, fetches, consume, 0),
    )


def forward_kernel(source_ref, receptor_ref, count_ref, field_ref, blocks_ref, out_ref, total, held, sems):
    def work(slots):
        products = []
        for slot in slots:
            source = source_ref[slot]
            half = pl.ds(pl.multiple_of(source % 2 * BLK, BLK), BLK)
            products.append(
                lax.dot_general(
                    field_ref[source // 2, :, half],
                    held[slot],
                    (((1,), (1,)), ((), ())),
                    preferred_element_type=F32,
                )
            )
        for slot, product in zip(slots, products):
            total[receptor_ref[slot]] += product

    begin, consume = each_used_block(count_ref[0], blocks_ref, held, sems, work)
    begin()
    total[...] = jnp.zeros_like(total)
    consume()
    out_ref[...] = total[...].astype(BF16)


def adjoint_kernel(source_ref, receptor_ref, count_ref, weighted_ref, blocks_ref, out_ref, total, held, sems):
    def work(slots):
        products = [
            jnp.dot(weighted_ref[receptor_ref[slot]], held[slot], preferred_element_type=F32) for slot in slots
        ]
        for slot, product in zip(slots, products):
            total[source_ref[slot]] += product

    begin, consume = each_used_block(count_ref[0], blocks_ref, held, sems, work)
    begin()
    total[...] = jnp.zeros_like(total)
    consume()
    for row in range(out_ref.shape[0]):
        for half in range(2):
            out_ref[row, :, half * BLK : (half + 1) * BLK] = total[2 * row + half].astype(BF16)


def block_products(kernel, name, out_shape, total_shape, sources, receptors, count, dense, blocks):
    slots = blocks.shape[0]
    fetches = (slots + FETCH - 1) // FETCH
    smem = pl.BlockSpec(memory_space=pltpu.SMEM)
    return pl.pallas_call(
        kernel,
        out_shape=jax.ShapeDtypeStruct(out_shape, BF16),
        in_specs=[smem, smem, smem, pl.BlockSpec(memory_space=VMEM), pl.BlockSpec(memory_space=pl.ANY)],
        out_specs=pl.BlockSpec(memory_space=VMEM),
        scratch_shapes=[
            VMEM(total_shape, F32),
            VMEM(blocks.shape, BF16),
            pltpu.SemaphoreType.DMA((fetches,)),
        ],
        compiler_params=pltpu.CompilerParams(vmem_limit_bytes=VMEM_LIMIT),
        name=name,
    )(sources, receptors, count, dense, blocks)


def reduce_kernel(planes, probes, weight_ref, mine_ref, out_ref, first, part, second, *sems):
    me = lax.axis_index("src")
    group = lax.axis_index("rcv")
    plane, spot = me // PLANE, me % PLANE
    send1, recv1, send2, recv2, send3, recv3, send4, recv4 = sems
    rows = mine_ref.shape[2]

    def spot_of(distance):
        return lax.rem(spot + distance, PLANE)

    def plane_of(distance):
        return lax.rem(plane + distance, planes)

    def in_plane(distance):
        return (plane * PLANE + spot_of(distance), group)

    def in_line(distance):
        return (plane_of(distance) * PLANE + spot, group)

    def scatter_plane(d):
        return remote(mine_ref.at[spot_of(d)], first.at[d - 1], send1.at[d - 1], recv1.at[d - 1], in_plane(d))

    def scatter_line(d):
        return remote(part.at[plane_of(d)], second.at[d - 1], send2.at[d - 1], recv2.at[d - 1], in_line(d))

    def gather_line(d):
        return remote(out_ref.at[spot, plane], out_ref.at[spot, plane], send3.at[d - 1], recv3.at[d - 1], in_line(d))

    def gather_plane(d):
        return remote(out_ref.at[spot], out_ref.at[spot], send4.at[d - 1], recv4.at[d - 1], in_plane(d))

    barrier_with(
        [in_plane(d) for d in range(1, PLANE)] + [in_line(d) for d in range(1, planes)]
    )
    for d in range(1, PLANE):
        scatter_plane(d).start()
    for d in range(1, PLANE):
        scatter_plane(d).wait_recv()
    for d in list(range(1, planes)) + [0]:
        piece = plane_of(d)
        total = mine_ref[spot, piece].astype(F32)
        for other in range(PLANE - 1):
            total = total + first[other, piece].astype(F32)
        part[piece] = total.astype(BF16)
        if d:
            scatter_line(d).start()
    for d in range(1, planes):
        scatter_line(d).wait_recv()
    total = part[plane].astype(F32)
    for other in range(planes - 1):
        total = total + second[other].astype(F32)
    block = spot * (RB_LOC // PLANE) + plane * rows // probes
    out_ref[spot, plane] = (total * weight_ref[pl.ds(block, 1), :]).astype(BF16)
    for d in range(1, planes):
        gather_line(d).start()
    for d in range(1, planes):
        gather_line(d).wait_recv()
    for d in range(1, PLANE):
        gather_plane(d).start()
    for d in range(1, PLANE):
        scatter_plane(d).wait_send()
        gather_plane(d).wait()
    for d in range(1, planes):
        scatter_line(d).wait_send()
        gather_line(d).wait_send()


def reduce_and_weigh(n_src, evolved, weight):
    blocks, probes, receptors = evolved.shape
    planes = n_src // PLANE
    rows = blocks * probes // (PLANE * planes)
    dma = pltpu.SemaphoreType.DMA
    out = pl.pallas_call(
        functools.partial(reduce_kernel, planes, probes),
        out_shape=jax.ShapeDtypeStruct((PLANE, planes, rows, receptors), BF16),
        in_specs=[pl.BlockSpec(memory_space=VMEM)] * 2,
        out_specs=pl.BlockSpec(memory_space=VMEM),
        scratch_shapes=[
            VMEM((PLANE - 1, planes, rows, receptors), BF16),
            VMEM((planes, rows, receptors), BF16),
            VMEM((planes - 1, rows, receptors), BF16),
            dma((PLANE - 1,)),
            dma((PLANE - 1,)),
            dma((planes - 1,)),
            dma((planes - 1,)),
            dma((planes - 1,)),
            dma((planes - 1,)),
            dma((PLANE - 1,)),
            dma((PLANE - 1,)),
        ],
        compiler_params=pltpu.CompilerParams(
            collective_id=1, has_side_effects=True, vmem_limit_bytes=VMEM_LIMIT
        ),
        name="reduce_and_weigh",
    )(weight, evolved.reshape(PLANE, planes, rows, receptors))
    return out.reshape(blocks, probes, receptors)


def back_kernel(
    n_src, terms_ref, probes_ref, kext_ref, out_ref, pair, relayed, joined, far, edge, halo, wide, kwide,
    edge_send, edge_recv, send, recv,
):
    me, group, before, after, twin, opposite = neighbours(n_src)
    lat, loc, lon = probes_ref.shape
    diagonal = 3 - group
    order = (0, lat // SMOOTH - 1) + tuple(range(1, lat // SMOOTH - 1))
    barrier_with([before, after, (me, twin), (me, opposite)])

    def term(owner, piece):
        return terms_ref.at[
            pl.ds(piece * SMOOTH, SMOOTH), pl.ds(pl.multiple_of(owner * loc, loc), loc), :
        ]

    def for_relay(k):
        return remote(term(diagonal, k), relayed.at[k], send.at[0, k], recv.at[0, k], (me, twin))

    def for_twin(k):
        return remote(term(twin, k), pair.at[k], send.at[1, k], recv.at[1, k], (me, twin))

    def across(k):
        return remote(joined.at[k], far.at[k], send.at[2, k], recv.at[2, k], (me, opposite))

    edges = [
        remote(edge.at[0], halo.at[1], edge_send.at[0], edge_recv.at[0], before),
        remote(edge.at[1], halo.at[0], edge_send.at[1], edge_recv.at[1], after),
    ]
    for k in order:
        for_relay(k).start()
    for k in order:
        for_twin(k).start()
    for k in order:
        for_relay(k).wait_recv()
        joined[k] = (term(opposite, k)[...].astype(F32) + relayed[k].astype(F32)).astype(BF16)
        across(k).start()
    spread_kappa(n_src, me, kext_ref, kwide)
    for k in order:
        for_twin(k).wait_recv()
        across(k).wait_recv()
        total = term(group, k)[...].astype(F32) + pair[k].astype(F32) + far[k].astype(F32)
        wide[SMOOTH + k * SMOOTH : 2 * SMOOTH + k * SMOOTH] = total
        if k == 0:
            edge[0] = total.astype(BF16)
            edges[0].start()
        if k == lat // SMOOTH - 1:
            edge[1] = total.astype(BF16)
            edges[1].start()
    for copy in edges:
        copy.wait()
    wide[0:SMOOTH] = halo[0].astype(F32)
    wide[lat + SMOOTH :] = halo[1].astype(F32)

    def one_slab(slab, carry):
        for half in range(SLAB // 8):
            some = pl.ds(pl.multiple_of(slab * SLAB + half * 8, 8), 8)
            value = wide[:, some, :]
            for step in range(SMOOTH):
                scaled = kwide[step : lat + 2 * SMOOTH - step] * value
                centre = scaled[1:-1]
                lap = scaled[:-2] + scaled[2:] + beside(centre) - 4.0 * centre
                value = value[1:-1] + lap
            out_ref[:, some, :] = value
        some = pl.ds(pl.multiple_of(slab * SLAB, SLAB), SLAB)
        out_ref[:, some, :] += probes_ref[:, some, :].astype(F32)
        return carry

    lax.fori_loop(0, loc // SLAB, one_slab, 0)
    for k in order:
        for_relay(k).wait_send()
        for_twin(k).wait_send()
        across(k).wait_send()


def scatter_and_smooth(n_src, terms, probes, kext):
    lat, loc, lon = probes.shape
    pieces = lat // SMOOTH
    landing = VMEM((pieces, SMOOTH, loc, lon), BF16)
    dma = pltpu.SemaphoreType.DMA
    return pl.pallas_call(
        functools.partial(back_kernel, n_src),
        out_shape=jax.ShapeDtypeStruct((lat, loc, lon), F32),
        in_specs=[pl.BlockSpec(memory_space=VMEM)] * 3,
        out_specs=pl.BlockSpec(memory_space=VMEM),
        scratch_shapes=[
            landing,
            landing,
            landing,
            landing,
            VMEM((2, SMOOTH, loc, lon), BF16),
            VMEM((2, SMOOTH, loc, lon), BF16),
            VMEM((lat + 2 * SMOOTH, loc, lon), F32),
            VMEM((lat + 2 * SMOOTH, 8, lon), F32),
            dma((2,)),
            dma((2,)),
            dma((3, pieces)),
            dma((3, pieces)),
        ],
        compiler_params=pltpu.CompilerParams(
            collective_id=2, has_side_effects=True, vmem_limit_bytes=VMEM_LIMIT
        ),
        name="scatter_and_smooth",
    )(terms, probes, kext)


def per_device(probes, kappa, footprint, block_source, block_receptor, block_count, obs_weight):
    n_src, n_rcv = lax.axis_size("src"), lax.axis_size("rcv")
    rows_first = probes.transpose(1, 0, 2)
    lat, loc, lon = rows_first.shape
    total = loc * n_rcv
    blocks = footprint.reshape(footprint.shape[2:])
    sources = block_source.reshape(-1)
    receptors = block_receptor.reshape(-1)
    count = block_count.reshape(1)
    field, kext = smooth_and_gather(n_src, n_rcv, rows_first, kappa)
    evolved = block_products(
        forward_kernel, "forward", (RB_LOC, total, BLK), (RB_LOC, total, BLK),
        sources, receptors, count, field, blocks,
    )
    weighted = reduce_and_weigh(n_src, evolved, obs_weight.reshape(RB_LOC, BLK))
    terms = block_products(
        adjoint_kernel, "adjoint", (lat, total, lon), (lat * lon // BLK, total, BLK),
        sources, receptors, count, weighted, blocks,
    )
    out = scatter_and_smooth(n_src, terms, rows_first, kext)
    return out.transpose(1, 0, 2)


def solution(mesh):
    placed = (
        P("rcv", "src", None),
        P("src", None),
        P("src", "rcv", None, None, None),
        P("src", "rcv", None),
        P("src", "rcv", None),
        P("src", "rcv"),
        P("rcv"),
    )
    return jax.shard_map(
        per_device, mesh=mesh, in_specs=placed, out_specs=P("rcv", "src", None), check_vma=False
    )
```

```python
import functools

import jax
import jax.numpy as jnp
from jax import lax
from jax.experimental import pallas as pl
from jax.experimental.pallas import tpu as pltpu
from jax.sharding import PartitionSpec as P

BLK = 128
RB_LOC = 16
SMOOTH = 4
PLANE = 8
SLAB = 16
TOGETHER = 16
MESH = pl.DeviceIdType.MESH
VMEM = pltpu.VMEM
F32 = jnp.float32
BF16 = jnp.bfloat16
VMEM_LIMIT = 24 * 1024 * 1024


def announce(devices):
    barrier = pltpu.get_barrier_semaphore()
    for device in devices:
        pl.semaphore_signal(barrier, inc=1, device_id=device, device_id_type=MESH)


def await_all(devices):
    pl.semaphore_wait(pltpu.get_barrier_semaphore(), len(devices))


def remote(src, dst, send_sem, recv_sem, device):
    return pltpu.make_async_remote_copy(
        src_ref=src,
        dst_ref=dst,
        send_sem=send_sem,
        recv_sem=recv_sem,
        device_id=device,
        device_id_type=MESH,
    )


def neighbours(n_src):
    me = lax.axis_index("src")
    group = lax.axis_index("rcv")
    high, core = group // 2, group % 2
    before = (lax.rem(me + n_src - 1, n_src), group)
    after = (lax.rem(me + 1, n_src), group)
    twin = high * 2 + (1 - core)
    opposite = (1 - high) * 2 + core
    return me, group, before, after, twin, opposite


def beside(centre):
    lanes = centre.shape[-1]
    lane = lax.broadcasted_iota(jnp.int32, centre.shape, centre.ndim - 1)
    west = jnp.where(lane == 0, 0.0, pltpu.roll(centre, 1, centre.ndim - 1))
    east = jnp.where(lane == lanes - 1, 0.0, pltpu.roll(centre, lanes - 1, centre.ndim - 1))
    return west + east


def spread_kappa(n_src, me, kext_ref, kwide, rows):
    for row in rows:
        value = kext_ref[8 - SMOOTH + row : 8 - SMOOTH + row + 1, :]
        if row < SMOOTH:
            value = jnp.where(me == 0, 0.0, value)
        if row >= kwide.shape[0] - SMOOTH:
            value = jnp.where(me == n_src - 1, 0.0, value)
        kwide[row] = jnp.broadcast_to(value, kwide.shape[1:])


def smooth_kernel(
    n_src, probes_ref, kappa_ref, field_ref, kext_ref, flat, halo, edge, wide, kwide, edge_send, edge_recv, send, recv
):
    me, group, before, after, twin, opposite = neighbours(n_src)
    lat, lon = kappa_ref.shape
    loc = probes_ref.shape[0] // lat
    slabs = loc // SLAB
    partners = [before, after, (me, twin), (me, opposite)]
    announce(partners)

    top, bottom = range(SMOOTH), range(lat - SMOOTH, lat)
    for side in range(lon // BLK):
        flat[side] = probes_ref[:, side * BLK : (side + 1) * BLK].astype(F32)

    def of_row(row):
        return jnp.concatenate([flat[side, pl.ds(row, loc, stride=lat), :] for side in range(lon // BLK)], axis=1)

    for side, rows in enumerate((top, bottom)):
        for place, row in enumerate(rows):
            value = of_row(row)
            wide[SMOOTH + row] = value
            edge[side, place] = value.astype(BF16)
    await_all(partners)
    edges = [
        remote(edge.at[1], halo.at[0], edge_send.at[0], edge_recv.at[0], after),
        remote(edge.at[0], halo.at[1], edge_send.at[1], edge_recv.at[1], before),
        remote(kappa_ref.at[pl.ds(lat - 8, 8)], kext_ref.at[pl.ds(0, 8)], edge_send.at[2], edge_recv.at[2], after),
        remote(kappa_ref.at[pl.ds(0, 8)], kext_ref.at[pl.ds(lat + 8, 8)], edge_send.at[3], edge_recv.at[3], before),
    ]
    for copy in edges:
        copy.start()
    for row in range(SMOOTH, lat - SMOOTH):
        wide[SMOOTH + row] = of_row(row)
    kext_ref[8 : lat + 8, :] = kappa_ref[...]
    spread_kappa(n_src, me, kext_ref, kwide, range(SMOOTH, lat + SMOOTH))

    parts = ((SMOOTH, lat - SMOOTH), (0, SMOOTH), (lat - SMOOTH, lat))

    def place(owner, part, slab):
        first, last = parts[part]
        return field_ref.at[
            pl.ds(first, last - first), pl.ds(pl.multiple_of(owner * loc + slab * SLAB, SLAB), SLAB), :
        ]

    def to_twin(part, slab):
        where = place(group, part, slab)
        return remote(where, where, send.at[0, part, slab], recv.at[0, part, slab], (me, twin))

    def to_opposite(part, slab):
        where = place(group, part, slab)
        return remote(where, where, send.at[1, part, slab], recv.at[1, part, slab], (me, opposite))

    def relay(part, slab):
        where = place(opposite, part, slab)
        return remote(where, where, send.at[2, part, slab], recv.at[2, part, slab], (me, twin))

    def smooth_part(part, slab):
        first, last = parts[part]
        halves = []
        for half in range(SLAB // 8):
            some = pl.ds(pl.multiple_of(slab * SLAB + half * 8, 8), 8)
            value = wide[first : last + 2 * SMOOTH, some, :]
            for step in range(SMOOTH):
                centre = value[1:-1]
                lap = value[:-2] + value[2:] + beside(centre) - 4.0 * centre
                value = centre + kwide[first + step + 1 : last + 2 * SMOOTH - 1 - step] * lap
            halves.append(value)
        mine = pl.ds(pl.multiple_of(group * loc + slab * SLAB, SLAB), SLAB)
        field_ref[first:last, mine, :] = jnp.concatenate(halves, axis=1).astype(BF16)
        to_opposite(part, slab).start()
        to_twin(part, slab).start()

    def inner(slab, carry):
        smooth_part(0, slab)
        return carry

    def outer(slab, carry):
        smooth_part(1, slab)
        smooth_part(2, slab)
        return carry

    lax.fori_loop(0, slabs, inner, 0)
    for copy in edges:
        copy.wait()
    wide[0:SMOOTH] = jnp.where(me == 0, 0.0, halo[0].astype(F32))
    wide[lat + SMOOTH :] = jnp.where(me == n_src - 1, 0.0, halo[1].astype(F32))
    spread_kappa(n_src, me, kext_ref, kwide, [*range(SMOOTH), *range(lat + SMOOTH, lat + 2 * SMOOTH)])
    lax.fori_loop(0, slabs, outer, 0)

    def pass_on(parts_here):
        def one(slab, carry):
            for part in parts_here:
                to_opposite(part, slab).wait_recv()
                relay(part, slab).start()
            return carry

        lax.fori_loop(0, slabs, one, 0)

    pass_on((0,))
    pass_on((1, 2))

    def finish(slab, carry):
        for part in range(3):
            to_opposite(part, slab).wait_send()
            to_twin(part, slab).wait()
            relay(part, slab).wait()
        return carry

    lax.fori_loop(0, slabs, finish, 0)


def smooth_and_gather(n_src, n_rcv, probes, kappa):
    lat, lon = kappa.shape
    loc = probes.shape[0] // lat
    slabs = loc // SLAB
    dma = pltpu.SemaphoreType.DMA
    return pl.pallas_call(
        functools.partial(smooth_kernel, n_src),
        out_shape=(
            jax.ShapeDtypeStruct((lat, loc * n_rcv, lon), BF16),
            jax.ShapeDtypeStruct((lat + 16, lon), F32),
        ),
        in_specs=[pl.BlockSpec(memory_space=VMEM)] * 2,
        out_specs=(pl.BlockSpec(memory_space=VMEM),) * 2,
        scratch_shapes=[
            VMEM((lon // BLK, loc * lat, BLK), F32),
            VMEM((2, SMOOTH, loc, lon), BF16),
            VMEM((2, SMOOTH, loc, lon), BF16),
            VMEM((lat + 2 * SMOOTH, loc, lon), F32),
            VMEM((lat + 2 * SMOOTH, 8, lon), F32),
            dma((4,)),
            dma((4,)),
            dma((3, 3, slabs)),
            dma((3, 3, slabs)),
        ],
        compiler_params=pltpu.CompilerParams(
            collective_id=0, has_side_effects=True, vmem_limit_bytes=VMEM_LIMIT
        ),
        cost_estimate=pl.CostEstimate(flops=20_000_000_000, bytes_accessed=64_000_000, transcendentals=0),
        name="smooth_and_gather",
    )(probes, kappa)


def each_used_block(count, work):
    def some(index, carry):
        work([index * TOGETHER + step for step in range(TOGETHER)])
        return carry

    lax.fori_loop(0, (count + TOGETHER - 1) // TOGETHER, some, 0)


def forward_kernel(source_ref, receptor_ref, count_ref, field_ref, blocks_ref, out_ref, total):
    count = count_ref[0]

    def work(slots):
        products = []
        for slot in slots:
            source = source_ref[slot]
            half = pl.ds(pl.multiple_of(source % 2 * BLK, BLK), BLK)
            products.append(
                lax.dot_general(
                    field_ref[source // 2, :, half],
                    blocks_ref[slot],
                    (((1,), (1,)), ((), ())),
                    preferred_element_type=F32,
                )
            )
        for slot, product in zip(slots, products):
            total[jnp.where(slot < count, receptor_ref[slot], RB_LOC)] += product

    total[...] = jnp.zeros_like(total)
    each_used_block(count, work)
    out_ref[...] = total[0:RB_LOC].astype(BF16)


def adjoint_kernel(source_ref, receptor_ref, count_ref, weighted_ref, blocks_ref, out_ref, total):
    count, spare = count_ref[0], total.shape[0] - 1

    def work(slots):
        products = [
            jnp.dot(weighted_ref[receptor_ref[slot]], blocks_ref[slot], preferred_element_type=F32) for slot in slots
        ]
        for slot, product in zip(slots, products):
            total[jnp.where(slot < count, source_ref[slot], spare)] += product

    total[...] = jnp.zeros_like(total)
    each_used_block(count, work)
    for row in range(out_ref.shape[0]):
        for half in range(2):
            out_ref[row, :, half * BLK : (half + 1) * BLK] = total[2 * row + half].astype(BF16)


def block_products(kernel, name, out_shape, total_shape, sources, receptors, count, dense, blocks):
    smem = pl.BlockSpec(memory_space=pltpu.SMEM)
    return pl.pallas_call(
        kernel,
        out_shape=jax.ShapeDtypeStruct(out_shape, BF16),
        in_specs=[smem, smem, smem, pl.BlockSpec(memory_space=VMEM), pl.BlockSpec(memory_space=VMEM)],
        out_specs=pl.BlockSpec(memory_space=VMEM),
        scratch_shapes=[VMEM(total_shape, F32)],
        compiler_params=pltpu.CompilerParams(vmem_limit_bytes=VMEM_LIMIT),
        name=name,
    )(sources, receptors, count, dense, blocks)


def reduce_kernel(planes, probes, weight_ref, mine_ref, out_ref, first, part, second, line, mixed, last, *sems):
    me = lax.axis_index("src")
    group = lax.axis_index("rcv")
    plane, spot = me // PLANE, me % PLANE
    pairs = iter(sems)
    a_plane, a_line, c_line, c_plane, ga_line, ga_plane, gc_plane, gc_line = zip(pairs, pairs)
    rows = mine_ref.shape[2]
    cut = rows * 3 // 4
    upper, lower = pl.ds(0, cut), pl.ds(cut, rows - cut)
    half_planes = planes // 2
    in_planes = range(1, PLANE)
    in_lines = range(1, planes)

    def spot_of(distance):
        return lax.rem(spot + distance, PLANE)

    def plane_of(distance):
        return lax.rem(plane + distance, planes)

    def in_plane(distance):
        return (plane * PLANE + spot_of(distance), group)

    def in_line(distance):
        return (plane_of(distance) * PLANE + spot, group)

    def copy(pair, index, src, dst, device):
        return remote(src, dst, pair[0].at[index], pair[1].at[index], device)

    def some(half):
        return pl.ds(half * half_planes, half_planes)

    def scatter_a_plane(d, half):
        return copy(
            a_plane, (d - 1, half), mine_ref.at[spot_of(d), some(half), upper], first.at[d - 1, some(half)], in_plane(d)
        )

    def scatter_a_line(piece):
        d = lax.rem(piece + planes - plane, planes)
        return copy(a_line, (d - 1,), part.at[piece], second.at[d - 1], (piece * PLANE + spot, group))

    def scatter_c_line(d):
        return copy(c_line, (d - 1,), mine_ref.at[:, plane_of(d), lower], line.at[d - 1], in_line(d))

    def scatter_c_plane(d):
        return copy(c_plane, (d - 1,), mixed.at[spot_of(d)], last.at[d - 1], in_plane(d))

    def gather_a_line(d):
        where = out_ref.at[spot, plane, upper]
        return copy(ga_line, (d - 1,), where, where, in_line(d))

    def gather_a_plane(d, half):
        where = out_ref.at[spot, some(half), upper]
        return copy(ga_plane, (d - 1, half), where, where, in_plane(d))

    def gather_c_plane(d):
        where = out_ref.at[spot, plane, lower]
        return copy(gc_plane, (d - 1,), where, where, in_plane(d))

    def gather_c_line(d):
        where = out_ref.at[:, plane, lower]
        return copy(gc_line, (d - 1,), where, where, in_line(d))

    partners = [in_plane(d) for d in in_planes] + [in_line(d) for d in in_lines]
    announce(partners)
    await_all(partners)
    for d in in_planes:
        scatter_a_plane(d, 0).start()
    for d in in_lines:
        scatter_c_line(d).start()
    for d in in_planes:
        scatter_a_plane(d, 1).start()
    weight = weight_ref[pl.ds(spot * (RB_LOC // PLANE) + plane * rows // probes, 1), :]

    def finish_half(half):
        for d in in_planes:
            scatter_a_plane(d, half).wait_recv()
        for index in range(half_planes):
            piece = half * half_planes + index
            total = mine_ref[spot, piece, 0:cut].astype(F32)
            for other in range(PLANE - 1):
                total = total + first[other, piece].astype(F32)
            part[piece] = total.astype(BF16)

            @pl.when(piece != plane)
            def _():
                scatter_a_line(piece).start()

    finish_half(0)
    for d in in_lines:
        scatter_c_line(d).wait_recv()
    for d in [*in_planes, 0]:
        piece = spot_of(d)
        total = mine_ref[piece, plane, cut:rows].astype(F32)
        for other in range(planes - 1):
            total = total + line[other, piece].astype(F32)
        mixed[piece] = total.astype(BF16)
        if d:
            scatter_c_plane(d).start()
    finish_half(1)
    for d in in_planes:
        scatter_c_plane(d).wait_recv()
    total = mixed[spot].astype(F32)
    for other in range(PLANE - 1):
        total = total + last[other].astype(F32)
    out_ref[spot, plane, cut:rows] = (total * weight).astype(BF16)
    for d in in_planes:
        gather_c_plane(d).start()

    def landed(piece):
        return lax.rem(plane + planes - piece, planes) - 1

    for d in in_lines:
        copy(a_line, (d - 1,), part.at[plane], second.at[d - 1], in_line(d)).wait_recv()
    total = part[plane].astype(F32)
    for other in range(planes - 1):
        total = total + second[other].astype(F32)
    out_ref[spot, plane, 0:cut] = (total * weight).astype(BF16)
    for d in in_lines:
        gather_a_line(d).start()
    for d in in_planes:
        gather_c_plane(d).wait_recv()
    for d in in_lines:
        gather_c_line(d).start()
    near = plane // half_planes
    for half in (near, 1 - near):
        for index in range(half_planes):
            piece = half * half_planes + index

            @pl.when(piece != plane)
            def _():
                where = out_ref.at[spot, piece, upper]
                copy(ga_line, (landed(piece),), where, where, in_line(1)).wait_recv()

        for d in in_planes:
            gather_a_plane(d, half).start()
    for d in in_planes:
        for half in (0, 1):
            gather_a_plane(d, half).wait()
            scatter_a_plane(d, half).wait_send()
        scatter_c_plane(d).wait_send()
        gather_c_plane(d).wait_send()
    for d in in_lines:
        gather_c_line(d).wait()
        gather_a_line(d).wait_send()
        scatter_c_line(d).wait_send()
        copy(a_line, (d - 1,), part.at[plane], second.at[d - 1], in_line(d)).wait_send()


def reduce_and_weigh(n_src, evolved, weight):
    blocks, probes, receptors = evolved.shape
    planes = n_src // PLANE
    rows = blocks * probes // (PLANE * planes)
    cut = rows * 3 // 4
    dma = pltpu.SemaphoreType.DMA
    per_spot, per_plane, halves = (PLANE - 1,), (planes - 1,), (PLANE - 1, 2)
    counts = (halves, per_plane, per_plane, per_spot, per_plane, halves, per_spot, per_plane)
    out = pl.pallas_call(
        functools.partial(reduce_kernel, planes, probes),
        out_shape=jax.ShapeDtypeStruct((PLANE, planes, rows, receptors), BF16),
        in_specs=[pl.BlockSpec(memory_space=VMEM)] * 2,
        out_specs=pl.BlockSpec(memory_space=VMEM),
        scratch_shapes=[
            VMEM((PLANE - 1, planes, cut, receptors), BF16),
            VMEM((planes, cut, receptors), BF16),
            VMEM((planes - 1, cut, receptors), BF16),
            VMEM((planes - 1, PLANE, rows - cut, receptors), BF16),
            VMEM((PLANE, rows - cut, receptors), BF16),
            VMEM((PLANE - 1, rows - cut, receptors), BF16),
        ]
        + [dma(count) for count in counts for _ in range(2)],
        compiler_params=pltpu.CompilerParams(
            collective_id=1, has_side_effects=True, vmem_limit_bytes=VMEM_LIMIT
        ),
        name="reduce_and_weigh",
    )(weight, evolved.reshape(PLANE, planes, rows, receptors))
    return out.reshape(blocks, probes, receptors)


def back_kernel(
    n_src, terms_ref, probes_ref, kext_ref, out_ref, pair, relayed, joined, far, edge, halo, wide, kwide, flat,
    edge_send, edge_recv, send, recv,
):
    me, group, before, after, twin, opposite = neighbours(n_src)
    lat = kext_ref.shape[0] - 16
    loc, lon = probes_ref.shape[0] // lat, probes_ref.shape[1]
    diagonal = 3 - group
    order = (0, lat // SMOOTH - 1) + tuple(range(1, lat // SMOOTH - 1))
    partners = [before, after, (me, twin), (me, opposite)]
    announce(partners)
    await_all(partners)

    def term(owner, piece):
        return terms_ref.at[
            pl.ds(piece * SMOOTH, SMOOTH), pl.ds(pl.multiple_of(owner * loc, loc), loc), :
        ]

    def for_relay(k):
        return remote(term(diagonal, k), relayed.at[k], send.at[0, k], recv.at[0, k], (me, twin))

    def for_twin(k):
        return remote(term(twin, k), pair.at[k], send.at[1, k], recv.at[1, k], (me, twin))

    def across(k):
        return remote(joined.at[k], far.at[k], send.at[2, k], recv.at[2, k], (me, opposite))

    edges = [
        remote(edge.at[0], halo.at[1], edge_send.at[0], edge_recv.at[0], before),
        remote(edge.at[1], halo.at[0], edge_send.at[1], edge_recv.at[1], after),
    ]
    for k in order:
        for_relay(k).start()
    for k in order:
        for_twin(k).start()
    for k in order:
        for_relay(k).wait_recv()
        joined[k] = (term(opposite, k)[...].astype(F32) + relayed[k].astype(F32)).astype(BF16)
        across(k).start()
    spread_kappa(n_src, me, kext_ref, kwide, range(lat + 2 * SMOOTH))
    for k in order:
        for_twin(k).wait_recv()
        across(k).wait_recv()
        total = term(group, k)[...].astype(F32) + pair[k].astype(F32) + far[k].astype(F32)
        wide[SMOOTH + k * SMOOTH : 2 * SMOOTH + k * SMOOTH] = total
        if k == 0:
            edge[0] = total.astype(BF16)
            edges[0].start()
        if k == lat // SMOOTH - 1:
            edge[1] = total.astype(BF16)
            edges[1].start()
    for copy in edges:
        copy.wait()
    wide[0:SMOOTH] = halo[0].astype(F32)
    wide[lat + SMOOTH :] = halo[1].astype(F32)

    def one_slab(slab, carry):
        for half in range(SLAB // 8):
            some = pl.ds(pl.multiple_of(slab * SLAB + half * 8, 8), 8)
            value = wide[:, some, :]
            for step in range(SMOOTH):
                scaled = kwide[step : lat + 2 * SMOOTH - step] * value
                centre = scaled[1:-1]
                lap = scaled[:-2] + scaled[2:] + beside(centre) - 4.0 * centre
                value = value[1:-1] + lap
            for row in range(lat):
                for side in range(lon // BLK):
                    flat[side, pl.ds(half * 8 * lat + row, 8, stride=lat), :] = value[
                        row, :, side * BLK : (side + 1) * BLK
                    ]
        some = pl.ds(pl.multiple_of(slab * SLAB * lat, SLAB * lat), SLAB * lat)
        for side in range(lon // BLK):
            lanes = slice(side * BLK, (side + 1) * BLK)
            out_ref[some, lanes] = flat[side] + probes_ref[some, lanes].astype(F32)
        return carry

    lax.fori_loop(0, loc // SLAB, one_slab, 0)
    for k in order:
        for_relay(k).wait_send()
        for_twin(k).wait_send()
        across(k).wait_send()


def scatter_and_smooth(n_src, terms, probes, kext):
    lat = kext.shape[0] - 16
    loc, lon = probes.shape[0] // lat, probes.shape[1]
    pieces = lat // SMOOTH
    landing = VMEM((pieces, SMOOTH, loc, lon), BF16)
    dma = pltpu.SemaphoreType.DMA
    return pl.pallas_call(
        functools.partial(back_kernel, n_src),
        out_shape=jax.ShapeDtypeStruct(probes.shape, F32),
        in_specs=[pl.BlockSpec(memory_space=VMEM)] * 3,
        out_specs=pl.BlockSpec(memory_space=VMEM),
        scratch_shapes=[
            landing,
            landing,
            landing,
            landing,
            VMEM((2, SMOOTH, loc, lon), BF16),
            VMEM((2, SMOOTH, loc, lon), BF16),
            VMEM((lat + 2 * SMOOTH, loc, lon), F32),
            VMEM((lat + 2 * SMOOTH, 8, lon), F32),
            VMEM((lon // BLK, SLAB * lat, BLK), F32),
            dma((2,)),
            dma((2,)),
            dma((3, pieces)),
            dma((3, pieces)),
        ],
        compiler_params=pltpu.CompilerParams(
            collective_id=2, has_side_effects=True, vmem_limit_bytes=VMEM_LIMIT
        ),
        name="scatter_and_smooth",
    )(terms, probes, kext)


def per_device(probes, kappa, footprint, block_source, block_receptor, block_count, obs_weight):
    n_src, n_rcv = lax.axis_size("src"), lax.axis_size("rcv")
    loc, lat, lon = probes.shape
    flat = probes.reshape(loc * lat, lon)
    total = loc * n_rcv
    blocks = footprint.reshape(footprint.shape[2:])
    sources = block_source.reshape(-1)
    receptors = block_receptor.reshape(-1)
    count = block_count.reshape(1)
    field, kext = smooth_and_gather(n_src, n_rcv, flat, kappa)
    evolved = block_products(
        forward_kernel, "forward", (RB_LOC, total, BLK), (RB_LOC + 1, total, BLK),
        sources, receptors, count, field, blocks,
    )
    weighted = reduce_and_weigh(n_src, evolved, obs_weight.reshape(RB_LOC, BLK))
    terms = block_products(
        adjoint_kernel, "adjoint", (lat, total, lon), (lat * lon // BLK + 1, total, BLK),
        sources, receptors, count, weighted, blocks,
    )
    out = scatter_and_smooth(n_src, terms, flat, kext)
    return out.reshape(loc, lat, lon)


def solution(mesh):
    placed = (
        P("rcv", "src", None),
        P("src", None),
        P("src", "rcv", None, None, None),
        P("src", "rcv", None),
        P("src", "rcv", None),
        P("src", "rcv"),
        P("rcv"),
    )
    return jax.shard_map(
        per_device, mesh=mesh, in_specs=placed, out_specs=P("rcv", "src", None), check_vma=False
    )
```

```python
import functools

import jax
import jax.numpy as jnp
from jax import lax
from jax.experimental import pallas as pl
from jax.experimental.pallas import tpu as pltpu
from jax.sharding import PartitionSpec as P

BLK = 128
RB_LOC = 16
SMOOTH = 4
PLANE = 8
REDUCE_GROUPS = 4
SLAB = 16
TOGETHER = 32
MESH = pl.DeviceIdType.MESH
VMEM = pltpu.VMEM
F32 = jnp.float32
BF16 = jnp.bfloat16
VMEM_LIMIT = 24 * 1024 * 1024


def announce(devices):
    barrier = pltpu.get_barrier_semaphore()
    for device in devices:
        pl.semaphore_signal(barrier, inc=1, device_id=device, device_id_type=MESH)


def await_all(devices):
    pl.semaphore_wait(pltpu.get_barrier_semaphore(), len(devices))


def remote(src, dst, send_sem, recv_sem, device):
    return pltpu.make_async_remote_copy(
        src_ref=src,
        dst_ref=dst,
        send_sem=send_sem,
        recv_sem=recv_sem,
        device_id=device,
        device_id_type=MESH,
    )


def neighbours(n_src):
    me = lax.axis_index("src")
    group = lax.axis_index("rcv")
    high, core = group // 2, group % 2
    before = (lax.rem(me + n_src - 1, n_src), group)
    after = (lax.rem(me + 1, n_src), group)
    twin = high * 2 + (1 - core)
    opposite = (1 - high) * 2 + core
    return me, group, before, after, twin, opposite


def beside(west_half, east_half):
    axis = west_half.ndim - 1
    lane = lax.broadcasted_iota(jnp.int32, west_half.shape, axis)
    first, last = lane == 0, lane == BLK - 1
    up_w, up_e = pltpu.roll(west_half, 1, axis), pltpu.roll(east_half, 1, axis)
    down_w, down_e = pltpu.roll(west_half, BLK - 1, axis), pltpu.roll(east_half, BLK - 1, axis)
    return (
        jnp.where(first, 0.0, up_w) + jnp.where(last, down_e, down_w),
        jnp.where(first, up_w, up_e) + jnp.where(last, 0.0, down_e),
    )


def halves_of(ref, rows, *middle):
    return [ref[(rows, *middle, slice(side * BLK, (side + 1) * BLK))] for side in range(2)]


def spread_kappa(n_src, me, kext_ref, kwide, keep, rows):
    for row in rows:
        value = kext_ref[8 - SMOOTH + row : 8 - SMOOTH + row + 1, :]
        if row < SMOOTH:
            value = jnp.where(me == 0, 0.0, value)
        if row >= kwide.shape[0] - SMOOTH:
            value = jnp.where(me == n_src - 1, 0.0, value)
        wide = jnp.broadcast_to(value, kwide.shape[1:])
        kwide[row] = wide
        keep[row] = 1.0 - 4.0 * wide


def smooth_kernel(
    n_src, probes_ref, kappa_ref, field_ref, kext_ref, flat, halo, edge, wide, kwide, keep,
    edge_send, edge_recv, send, recv,
):
    me, group, before, after, twin, opposite = neighbours(n_src)
    lat, lon = kappa_ref.shape
    loc = probes_ref.shape[0] // lat
    slabs = loc // SLAB
    partners = [before, after, (me, twin), (me, opposite)]
    announce(partners)

    top, bottom = range(SMOOTH), range(lat - SMOOTH, lat)
    for side in range(lon // BLK):
        flat[side] = probes_ref[:, side * BLK : (side + 1) * BLK].astype(F32)

    def of_row(row):
        return jnp.concatenate([flat[side, pl.ds(row, loc, stride=lat), :] for side in range(lon // BLK)], axis=1)

    for side, rows in enumerate((top, bottom)):
        for place, row in enumerate(rows):
            value = of_row(row)
            wide[SMOOTH + row] = value
            edge[side, place] = value.astype(BF16)
    for row in range(SMOOTH, lat - SMOOTH):
        wide[SMOOTH + row] = of_row(row)
    kext_ref[8 : lat + 8, :] = kappa_ref[...]
    spread_kappa(n_src, me, kext_ref, kwide, keep, range(SMOOTH, lat + SMOOTH))
    edges = [
        remote(edge.at[1], halo.at[0], edge_send.at[0], edge_recv.at[0], after),
        remote(edge.at[0], halo.at[1], edge_send.at[1], edge_recv.at[1], before),
        remote(kappa_ref.at[pl.ds(lat - 8, 8)], kext_ref.at[pl.ds(0, 8)], edge_send.at[2], edge_recv.at[2], after),
        remote(kappa_ref.at[pl.ds(0, 8)], kext_ref.at[pl.ds(lat + 8, 8)], edge_send.at[3], edge_recv.at[3], before),
    ]

    parts = ((SMOOTH, lat - SMOOTH), (0, SMOOTH), (lat - SMOOTH, lat))

    def place(owner, part, slab):
        first, last = parts[part]
        return field_ref.at[
            pl.ds(first, last - first), pl.ds(pl.multiple_of(owner * loc + slab * SLAB, SLAB), SLAB), :
        ]

    def to_twin(part, slab):
        where = place(group, part, slab)
        return remote(where, where, send.at[0, part, slab], recv.at[0, part, slab], (me, twin))

    def to_opposite(part, slab):
        where = place(group, part, slab)
        return remote(where, where, send.at[1, part, slab], recv.at[1, part, slab], (me, opposite))

    def relay(part, slab):
        where = place(opposite, part, slab)
        return remote(where, where, send.at[2, part, slab], recv.at[2, part, slab], (me, twin))

    def smooth_part(part, slab):
        first, last = parts[part]
        groups = []
        for half in range(SLAB // 8):
            some = pl.ds(pl.multiple_of(slab * SLAB + half * 8, 8), 8)
            value = halves_of(wide, slice(first, last + 2 * SMOOTH), some)
            for step in range(SMOOTH):
                rows = slice(first + step + 1, last + 2 * SMOOTH - 1 - step)
                centre = [v[1:-1] for v in value]
                around = beside(*centre)
                value = [
                    c * k + w * (v[:-2] + v[2:] + a)
                    for c, k, w, v, a in zip(
                        centre, halves_of(keep, rows, slice(None)), halves_of(kwide, rows, slice(None)), value, around
                    )
                ]
            groups.append(value)
        mine = pl.ds(pl.multiple_of(group * loc + slab * SLAB, SLAB), SLAB)
        for side in range(2):
            field_ref[first:last, mine, side * BLK : (side + 1) * BLK] = jnp.concatenate(
                [g[side] for g in groups], axis=1
            ).astype(BF16)

    def post(part, slab):
        to_opposite(part, slab).start()
        to_twin(part, slab).start()

    def inner(slab, carry):
        smooth_part(0, slab)
        post(0, slab)
        return carry

    def outer(slab, carry):
        for part in (1, 2):
            smooth_part(part, slab)
            post(part, slab)
        return carry

    smooth_part(0, 0)
    await_all(partners)
    post(0, 0)
    for copy in edges:
        copy.start()
    lax.fori_loop(1, slabs, inner, 0)
    for copy in edges:
        copy.wait()
    wide[0:SMOOTH] = jnp.where(me == 0, 0.0, halo[0].astype(F32))
    wide[lat + SMOOTH :] = jnp.where(me == n_src - 1, 0.0, halo[1].astype(F32))
    spread_kappa(n_src, me, kext_ref, kwide, keep, [*range(SMOOTH), *range(lat + SMOOTH, lat + 2 * SMOOTH)])
    lax.fori_loop(0, slabs, outer, 0)

    def pass_on(parts_here):
        def one(slab, carry):
            for part in parts_here:
                to_opposite(part, slab).wait_recv()
                relay(part, slab).start()
            return carry

        lax.fori_loop(0, slabs, one, 0)

    pass_on((0,))
    pass_on((1, 2))

    def finish(slab, carry):
        for part in range(3):
            to_opposite(part, slab).wait_send()
            to_twin(part, slab).wait()
            relay(part, slab).wait()
        return carry

    lax.fori_loop(0, slabs, finish, 0)


def smooth_and_gather(n_src, n_rcv, probes, kappa):
    lat, lon = kappa.shape
    loc = probes.shape[0] // lat
    slabs = loc // SLAB
    dma = pltpu.SemaphoreType.DMA
    return pl.pallas_call(
        functools.partial(smooth_kernel, n_src),
        out_shape=(
            jax.ShapeDtypeStruct((lat, loc * n_rcv, lon), BF16),
            jax.ShapeDtypeStruct((lat + 16, lon), F32),
        ),
        in_specs=[pl.BlockSpec(memory_space=VMEM)] * 2,
        out_specs=(pl.BlockSpec(memory_space=VMEM),) * 2,
        scratch_shapes=[
            VMEM((lon // BLK, loc * lat, BLK), F32),
            VMEM((2, SMOOTH, loc, lon), BF16),
            VMEM((2, SMOOTH, loc, lon), BF16),
            VMEM((lat + 2 * SMOOTH, loc, lon), F32),
            VMEM((lat + 2 * SMOOTH, 8, lon), F32),
            VMEM((lat + 2 * SMOOTH, 8, lon), F32),
            dma((4,)),
            dma((4,)),
            dma((3, 3, slabs)),
            dma((3, 3, slabs)),
        ],
        compiler_params=pltpu.CompilerParams(
            collective_id=0, has_side_effects=True, vmem_limit_bytes=VMEM_LIMIT
        ),
        cost_estimate=pl.CostEstimate(flops=20_000_000_000, bytes_accessed=64_000_000, transcendentals=0),
        name="smooth_and_gather",
    )(probes, kappa)


def each_used_block(count, work):
    def some(index, carry):
        work([index * TOGETHER + step for step in range(TOGETHER)])
        return carry

    lax.fori_loop(0, (count + TOGETHER - 1) // TOGETHER, some, 0)


def forward_kernel(source_ref, receptor_ref, count_ref, field_ref, blocks_ref, out_ref, total):
    count = count_ref[0]

    def work(slots):
        products = []
        for slot in slots:
            source = source_ref[slot]
            half = pl.ds(pl.multiple_of(source % 2 * BLK, BLK), BLK)
            products.append(
                lax.dot_general(
                    field_ref[source // 2, :, half],
                    blocks_ref[slot],
                    (((1,), (1,)), ((), ())),
                    preferred_element_type=F32,
                )
            )
        for slot, product in zip(slots, products):
            total[jnp.where(slot < count, receptor_ref[slot], RB_LOC)] += product

    total[...] = jnp.zeros_like(total)
    each_used_block(count, work)
    out_ref[...] = total[0:RB_LOC].astype(BF16)


def adjoint_kernel(source_ref, receptor_ref, count_ref, weighted_ref, blocks_ref, out_ref, total):
    count, spare = count_ref[0], total.shape[0] - 1

    def work(slots):
        products = [
            jnp.dot(weighted_ref[receptor_ref[slot]], blocks_ref[slot], preferred_element_type=F32) for slot in slots
        ]
        for slot, product in zip(slots, products):
            total[jnp.where(slot < count, source_ref[slot], spare)] += product

    total[...] = jnp.zeros_like(total)
    each_used_block(count, work)
    for row in range(out_ref.shape[0]):
        for half in range(2):
            out_ref[row, :, half * BLK : (half + 1) * BLK] = total[2 * row + half].astype(BF16)


def block_products(kernel, name, out_shape, total_shape, sources, receptors, count, dense, blocks):
    smem = pl.BlockSpec(memory_space=pltpu.SMEM)
    return pl.pallas_call(
        kernel,
        out_shape=jax.ShapeDtypeStruct(out_shape, BF16),
        in_specs=[smem, smem, smem, pl.BlockSpec(memory_space=VMEM), pl.BlockSpec(memory_space=VMEM)],
        out_specs=pl.BlockSpec(memory_space=VMEM),
        scratch_shapes=[VMEM(total_shape, F32)],
        compiler_params=pltpu.CompilerParams(vmem_limit_bytes=VMEM_LIMIT),
        name=name,
    )(sources, receptors, count, dense, blocks)


def reduce_kernel(planes, probes, weight_ref, mine_ref, out_ref, first, part, second, line, mixed, last, *sems):
    me = lax.axis_index("src")
    group = lax.axis_index("rcv")
    plane, spot = me // PLANE, me % PLANE
    pairs = iter(sems)
    a_plane, a_line, c_line, c_plane, ga_line, ga_plane, gc_plane, gc_line = zip(pairs, pairs)
    rows = mine_ref.shape[2]
    cut = rows * 3 // 4
    upper, lower = pl.ds(0, cut), pl.ds(cut, rows - cut)
    groups = min(REDUCE_GROUPS, planes)
    size = planes // groups
    in_planes = range(1, PLANE)
    in_lines = range(1, planes)

    def spot_of(distance):
        return lax.rem(spot + distance, PLANE)

    def plane_of(distance):
        return lax.rem(plane + distance, planes)

    def in_plane(distance):
        return (plane * PLANE + spot_of(distance), group)

    def in_line(distance):
        return (plane_of(distance) * PLANE + spot, group)

    def copy(pair, index, src, dst, device):
        return remote(src, dst, pair[0].at[index], pair[1].at[index], device)

    def some(g):
        return pl.ds(g * size, size)

    def scatter_a_plane(d, g):
        return copy(
            a_plane, (d - 1, g), mine_ref.at[spot_of(d), some(g), upper], first.at[d - 1, some(g)], in_plane(d)
        )

    def scatter_a_line(piece):
        d = lax.rem(piece + planes - plane, planes)
        return copy(a_line, (d - 1,), part.at[piece], second.at[d - 1], (piece * PLANE + spot, group))

    def scatter_c_line(d):
        return copy(c_line, (d - 1,), mine_ref.at[:, plane_of(d), lower], line.at[d - 1], in_line(d))

    def scatter_c_plane(d):
        return copy(c_plane, (d - 1,), mixed.at[spot_of(d)], last.at[d - 1], in_plane(d))

    def gather_a_line(d):
        where = out_ref.at[spot, plane, upper]
        return copy(ga_line, (d - 1,), where, where, in_line(d))

    def gather_a_plane(d, g):
        where = out_ref.at[spot, some(g), upper]
        return copy(ga_plane, (d - 1, g), where, where, in_plane(d))

    def gather_c_plane(d):
        where = out_ref.at[spot, plane, lower]
        return copy(gc_plane, (d - 1,), where, where, in_plane(d))

    def gather_c_line(d):
        where = out_ref.at[:, plane, lower]
        return copy(gc_line, (d - 1,), where, where, in_line(d))

    weight = weight_ref[pl.ds(spot * (RB_LOC // PLANE) + plane * rows // probes, 1), :]

    def begin_group(g):
        for d in in_planes:
            scatter_a_plane(d, g).start()

    def plane_sums(g):
        for d in in_planes:
            scatter_a_plane(d, g).wait_recv()
        if g + 2 < groups:
            begin_group(g + 2)
        for index in range(size):
            piece = g * size + index
            total = mine_ref[spot, piece, 0:cut].astype(F32)
            for other in range(PLANE - 1):
                total = total + first[other, piece].astype(F32)
            part[piece] = total.astype(BF16)

            @pl.when(piece != plane)
            def _():
                scatter_a_line(piece).start()

    def own_rows(g):
        @pl.when(plane // size == g)
        def _():
            for d in in_lines:
                copy(a_line, (d - 1,), part.at[plane], second.at[d - 1], in_line(d)).wait_recv()
            total = part[plane].astype(F32)
            for other in range(planes - 1):
                total = total + second[other].astype(F32)
            out_ref[spot, plane, 0:cut] = (total * weight).astype(BF16)
            for d in in_lines:
                gather_a_line(d).start()

    def spread_group(g):
        for index in range(size):
            piece = g * size + index

            @pl.when(piece != plane)
            def _():
                where = out_ref.at[spot, piece, upper]
                sender = lax.rem(plane + planes - piece, planes) - 1
                copy(ga_line, (sender,), where, where, in_line(1)).wait_recv()

        for d in in_planes:
            gather_a_plane(d, g).start()

    def line_sums():
        for d in in_lines:
            scatter_c_line(d).wait_recv()
        for d in [*in_planes, 0]:
            piece = spot_of(d)
            total = mine_ref[piece, plane, cut:rows].astype(F32)
            for other in range(planes - 1):
                total = total + line[other, piece].astype(F32)
            mixed[piece] = total.astype(BF16)
            if d:
                scatter_c_plane(d).start()

    def own_lower_rows():
        for d in in_planes:
            scatter_c_plane(d).wait_recv()
        total = mixed[spot].astype(F32)
        for other in range(PLANE - 1):
            total = total + last[other].astype(F32)
        out_ref[spot, plane, cut:rows] = (total * weight).astype(BF16)
        for d in in_planes:
            gather_c_plane(d).start()

    def spread_lower_rows():
        for d in in_planes:
            gather_c_plane(d).wait_recv()
        for d in in_lines:
            gather_c_line(d).start()

    partners = [in_plane(d) for d in in_planes] + [in_line(d) for d in in_lines]
    announce(partners)
    await_all(partners)
    begin_group(0)
    for d in in_lines:
        scatter_c_line(d).start()
    if groups > 1:
        begin_group(1)
    steps = [(2.6, line_sums), (6.3, own_lower_rows), (10.0, spread_lower_rows)]
    for g in range(groups):
        steps.append((2.5 * g, functools.partial(plane_sums, g)))
        steps.append((2.5 * g + 3.5, functools.partial(own_rows, g)))
        steps.append((2.5 * g + 7.0, functools.partial(spread_group, g)))
    for _, step in sorted(steps, key=lambda pair: pair[0]):
        step()
    for d in in_planes:
        for g in range(groups):
            gather_a_plane(d, g).wait()
            scatter_a_plane(d, g).wait_send()
        scatter_c_plane(d).wait_send()
        gather_c_plane(d).wait_send()
    for d in in_lines:
        gather_c_line(d).wait()
        gather_a_line(d).wait_send()
        scatter_c_line(d).wait_send()
        copy(a_line, (d - 1,), part.at[plane], second.at[d - 1], in_line(d)).wait_send()


def reduce_and_weigh(n_src, evolved, weight):
    blocks, probes, receptors = evolved.shape
    planes = n_src // PLANE
    rows = blocks * probes // (PLANE * planes)
    cut = rows * 3 // 4
    dma = pltpu.SemaphoreType.DMA
    per_spot, per_plane, parts = (PLANE - 1,), (planes - 1,), (PLANE - 1, min(REDUCE_GROUPS, planes))
    counts = (parts, per_plane, per_plane, per_spot, per_plane, parts, per_spot, per_plane)
    out = pl.pallas_call(
        functools.partial(reduce_kernel, planes, probes),
        out_shape=jax.ShapeDtypeStruct((PLANE, planes, rows, receptors), BF16),
        in_specs=[pl.BlockSpec(memory_space=VMEM)] * 2,
        out_specs=pl.BlockSpec(memory_space=VMEM),
        scratch_shapes=[
            VMEM((PLANE - 1, planes, cut, receptors), BF16),
            VMEM((planes, cut, receptors), BF16),
            VMEM((planes - 1, cut, receptors), BF16),
            VMEM((planes - 1, PLANE, rows - cut, receptors), BF16),
            VMEM((PLANE, rows - cut, receptors), BF16),
            VMEM((PLANE - 1, rows - cut, receptors), BF16),
        ]
        + [dma(count) for count in counts for _ in range(2)],
        compiler_params=pltpu.CompilerParams(
            collective_id=1, has_side_effects=True, vmem_limit_bytes=VMEM_LIMIT
        ),
        name="reduce_and_weigh",
    )(weight, evolved.reshape(PLANE, planes, rows, receptors))
    return out.reshape(blocks, probes, receptors)


def back_kernel(
    n_src, terms_ref, probes_ref, kext_ref, out_ref, pair, relayed, joined, far, edge, halo, wide, kwide, keep, flat,
    edge_send, edge_recv, send, recv,
):
    me, group, before, after, twin, opposite = neighbours(n_src)
    lat = kext_ref.shape[0] - 16
    loc, lon = probes_ref.shape[0] // lat, probes_ref.shape[1]
    slabs = loc // SLAB
    diagonal = 3 - group
    partners = [before, after, (me, twin), (me, opposite)]
    announce(partners)
    await_all(partners)

    def view(ref, k, offset=0):
        if isinstance(k, int) and k < 2:
            return ref.at[pl.ds(k * (lat - SMOOTH), SMOOTH), pl.ds(pl.multiple_of(offset, loc), loc), :]
        start = pl.multiple_of(offset + (k - 2) * SLAB, SLAB)
        return ref.at[pl.ds(SMOOTH, lat - 2 * SMOOTH), pl.ds(start, SLAB), :]

    def term(owner, k):
        return view(terms_ref, k, owner * loc)

    def for_relay(k):
        return remote(term(diagonal, k), view(relayed, k), send.at[0, k], recv.at[0, k], (me, twin))

    def for_twin(k):
        return remote(term(twin, k), view(pair, k), send.at[1, k], recv.at[1, k], (me, twin))

    def across(k):
        return remote(view(joined, k), view(far, k), send.at[2, k], recv.at[2, k], (me, opposite))

    def each(work):
        work(0)
        work(1)
        lax.fori_loop(2, slabs + 2, lambda k, carry: (work(k), carry)[1], 0)

    def join(k):
        for_relay(k).wait_recv()
        view(joined, k)[...] = (term(opposite, k)[...].astype(F32) + view(relayed, k)[...].astype(F32)).astype(BF16)
        across(k).start()

    def total(k):
        for_twin(k).wait_recv()
        across(k).wait_recv()
        return term(group, k)[...].astype(F32) + view(pair, k)[...].astype(F32) + view(far, k)[...].astype(F32)

    edges = [
        remote(edge.at[0], halo.at[1], edge_send.at[0], edge_recv.at[0], before),
        remote(edge.at[1], halo.at[0], edge_send.at[1], edge_recv.at[1], after),
    ]
    each(lambda k: for_relay(k).start())
    each(lambda k: for_twin(k).start())
    each(join)
    spread_kappa(n_src, me, kext_ref, kwide, keep, range(lat + 2 * SMOOTH))
    for k, row in ((0, SMOOTH), (1, lat)):
        rows = total(k)
        wide[row : row + SMOOTH] = rows
        edge[k] = rows.astype(BF16)
        edges[k].start()

    def one_slab(slab, carry):
        probes_here = pl.ds(pl.multiple_of(slab * SLAB, SLAB), SLAB)
        wide[2 * SMOOTH : lat, probes_here, :] = total(slab + 2)

        @pl.when(slab == 0)
        def _():
            for copy in edges:
                copy.wait()
            wide[0:SMOOTH] = halo[0].astype(F32)
            wide[lat + SMOOTH :] = halo[1].astype(F32)

        for half in range(SLAB // 8):
            some = pl.ds(pl.multiple_of(slab * SLAB + half * 8, 8), 8)
            value = halves_of(wide, slice(None), some)
            for step in range(SMOOTH):
                rows = slice(step, lat + 2 * SMOOTH - step)
                scaled = [w * v for w, v in zip(halves_of(kwide, rows, slice(None)), value)]
                around = beside(*[v[1:-1] for v in scaled])
                inner = slice(step + 1, lat + 2 * SMOOTH - 1 - step)
                value = [
                    v[1:-1] * k + (g[:-2] + g[2:] + a)
                    for v, k, g, a in zip(value, halves_of(keep, inner, slice(None)), scaled, around)
                ]
            for side in range(2):
                for row in range(lat):
                    flat[side, pl.ds(half * 8 * lat + row, 8, stride=lat), :] = value[side][row]
        some = pl.ds(pl.multiple_of(slab * SLAB * lat, SLAB * lat), SLAB * lat)
        for side in range(2):
            lanes = slice(side * BLK, (side + 1) * BLK)
            out_ref[some, lanes] = flat[side] + probes_ref[some, lanes].astype(F32)
        return carry

    lax.fori_loop(0, slabs, one_slab, 0)

    def finish(k):
        for_relay(k).wait_send()
        for_twin(k).wait_send()
        across(k).wait_send()

    each(finish)


def scatter_and_smooth(n_src, terms, probes, kext):
    lat = kext.shape[0] - 16
    loc, lon = probes.shape[0] // lat, probes.shape[1]
    pieces = loc // SLAB + 2
    landing = VMEM((lat, loc, lon), BF16)
    dma = pltpu.SemaphoreType.DMA
    return pl.pallas_call(
        functools.partial(back_kernel, n_src),
        out_shape=jax.ShapeDtypeStruct(probes.shape, F32),
        in_specs=[pl.BlockSpec(memory_space=VMEM)] * 3,
        out_specs=pl.BlockSpec(memory_space=VMEM),
        scratch_shapes=[
            landing,
            landing,
            landing,
            landing,
            VMEM((2, SMOOTH, loc, lon), BF16),
            VMEM((2, SMOOTH, loc, lon), BF16),
            VMEM((lat + 2 * SMOOTH, loc, lon), F32),
            VMEM((lat + 2 * SMOOTH, 8, lon), F32),
            VMEM((lat + 2 * SMOOTH, 8, lon), F32),
            VMEM((lon // BLK, SLAB * lat, BLK), F32),
            dma((2,)),
            dma((2,)),
            dma((3, pieces)),
            dma((3, pieces)),
        ],
        compiler_params=pltpu.CompilerParams(
            collective_id=2, has_side_effects=True, vmem_limit_bytes=VMEM_LIMIT
        ),
        name="scatter_and_smooth",
    )(terms, probes, kext)


def per_device(probes, kappa, footprint, block_source, block_receptor, block_count, obs_weight):
    n_src, n_rcv = lax.axis_size("src"), lax.axis_size("rcv")
    loc, lat, lon = probes.shape
    flat = probes.reshape(loc * lat, lon)
    total = loc * n_rcv
    blocks = footprint.reshape(footprint.shape[2:])
    sources = block_source.reshape(-1)
    receptors = block_receptor.reshape(-1)
    count = block_count.reshape(1)
    field, kext = smooth_and_gather(n_src, n_rcv, flat, kappa)
    evolved = block_products(
        forward_kernel, "forward", (RB_LOC, total, BLK), (RB_LOC + 1, total, BLK),
        sources, receptors, count, field, blocks,
    )
    weighted = reduce_and_weigh(n_src, evolved, obs_weight.reshape(RB_LOC, BLK))
    terms = block_products(
        adjoint_kernel, "adjoint", (lat, total, lon), (lat * lon // BLK + 1, total, BLK),
        sources, receptors, count, weighted, blocks,
    )
    out = scatter_and_smooth(n_src, terms, flat, kext)
    return out.reshape(loc, lat, lon)


def solution(mesh):
    placed = (
        P("rcv", "src", None),
        P("src", None),
        P("src", "rcv", None, None, None),
        P("src", "rcv", None),
        P("src", "rcv", None),
        P("src", "rcv"),
        P("rcv"),
    )
    return jax.shard_map(
        per_device, mesh=mesh, in_specs=placed, out_specs=P("rcv", "src", None), check_vma=False
    )
```

```python
import functools

import jax
import jax.numpy as jnp
from jax import lax
from jax.experimental import pallas as pl
from jax.experimental.pallas import tpu as pltpu
from jax.sharding import PartitionSpec as P

BLK = 128
RB_LOC = 16
SMOOTH = 4
PLANE = 8
SLAB = 16
TOGETHER = 32
MESH = pl.DeviceIdType.MESH
VMEM = pltpu.VMEM
F32 = jnp.float32
BF16 = jnp.bfloat16
VMEM_LIMIT = 24 * 1024 * 1024


def announce(devices):
    barrier = pltpu.get_barrier_semaphore()
    for device in devices:
        pl.semaphore_signal(barrier, inc=1, device_id=device, device_id_type=MESH)


def await_all(devices):
    pl.semaphore_wait(pltpu.get_barrier_semaphore(), len(devices))


def remote(src, dst, send_sem, recv_sem, device):
    return pltpu.make_async_remote_copy(
        src_ref=src,
        dst_ref=dst,
        send_sem=send_sem,
        recv_sem=recv_sem,
        device_id=device,
        device_id_type=MESH,
    )


def neighbours(n_src):
    me = lax.axis_index("src")
    group = lax.axis_index("rcv")
    high, core = group // 2, group % 2
    before = (lax.rem(me + n_src - 1, n_src), group)
    after = (lax.rem(me + 1, n_src), group)
    twin = high * 2 + (1 - core)
    opposite = (1 - high) * 2 + core
    return me, group, before, after, twin, opposite


def beside(west_half, east_half):
    axis = west_half.ndim - 1
    lane = lax.broadcasted_iota(jnp.int32, west_half.shape, axis)
    first, last = lane == 0, lane == BLK - 1
    up_w, up_e = pltpu.roll(west_half, 1, axis), pltpu.roll(east_half, 1, axis)
    down_w, down_e = pltpu.roll(west_half, BLK - 1, axis), pltpu.roll(east_half, BLK - 1, axis)
    return (
        jnp.where(first, 0.0, up_w) + jnp.where(last, down_e, down_w),
        jnp.where(first, up_w, up_e) + jnp.where(last, 0.0, down_e),
    )


def halves_of(ref, rows, *middle):
    return [ref[(rows, *middle, slice(side * BLK, (side + 1) * BLK))] for side in range(2)]


def spread_kappa(n_src, me, kext_ref, kwide, keep, rows):
    for row in rows:
        value = kext_ref[8 - SMOOTH + row : 8 - SMOOTH + row + 1, :]
        if row < SMOOTH:
            value = jnp.where(me == 0, 0.0, value)
        if row >= kwide.shape[0] - SMOOTH:
            value = jnp.where(me == n_src - 1, 0.0, value)
        wide = jnp.broadcast_to(value, kwide.shape[1:])
        kwide[row] = wide
        keep[row] = 1.0 - 4.0 * wide


def make_plan(source_ref, receptor_ref, count_ref, plan_ref):
    slots, lanes = source_ref.shape[1], plan_ref.shape[1]
    row_of = lax.broadcasted_iota(jnp.int32, (slots, slots), 0)
    lane_of = lax.broadcasted_iota(jnp.int32, (slots, slots), 1)
    place = lax.broadcasted_iota(jnp.int32, (slots, lanes), 1)
    slot = lax.broadcasted_iota(jnp.int32, (1, slots), 1)
    used = slot < count_ref[...]

    def place_of(receptor):
        return receptor // 2 * 4 + receptor % 2

    def column(row):
        return jnp.sum(jnp.where(row_of == lane_of, row, 0.0), axis=1, keepdims=True)

    first_lane = lax.broadcasted_iota(jnp.int32, (1, lanes), 1) == 0
    for base, key_ref, other in ((0, receptor_ref, source_ref[...]), (8, source_ref, place_of(receptor_ref[...]))):
        key = jnp.where(used, key_ref[...] * 256 + slot, 64 * 256 + slot).astype(F32)
        tall = column(key)
        rank = jnp.sum(jnp.where(key < tall, 1.0, 0.0), axis=1, keepdims=True)
        here = rank.astype(jnp.int32) == place

        def ordered(values):
            return jnp.sum(jnp.where(here, values, 0.0), axis=0, keepdims=True).astype(jnp.int32)

        keys = ordered(tall)
        block = keys // 256
        ends = jnp.sum(
            jnp.where(tall < ((place + 1) * 256).astype(F32), 1.0, 0.0), axis=0, keepdims=True
        ).astype(jnp.int32)
        start = jnp.where(first_lane, 0, pltpu.roll(ends, 1, 1))
        same = (block == pltpu.roll(block, 1, 1)) & jnp.logical_not(first_lane)
        plan_ref[base : base + 1, :] = keys - block * 256
        plan_ref[base + 1 : base + 2, :] = ordered(column(other.astype(F32)))
        plan_ref[base + 2 : base + 3, :] = same.astype(jnp.int32)
        plan_ref[base + 3 : base + 4, :] = jnp.maximum(ends - 1, 0)
        plan_ref[base + 4 : base + 5, :] = (ends > start).astype(jnp.int32)


def smooth_kernel(
    n_src, probes_ref, kappa_ref, source_ref, receptor_ref, count_ref, field_ref, kext_ref, plan_ref, flat, halo, edge, wide, kwide, keep,
    edge_send, edge_recv, send, recv,
):
    me, group, before, after, twin, opposite = neighbours(n_src)
    lat, lon = kappa_ref.shape
    loc = probes_ref.shape[0] // lat
    slabs = loc // SLAB
    partners = [before, after, (me, twin), (me, opposite)]
    announce(partners)

    top, bottom = range(SMOOTH), range(lat - SMOOTH, lat)
    for side in range(lon // BLK):
        flat[side] = probes_ref[:, side * BLK : (side + 1) * BLK].astype(F32)

    def of_row(row):
        return jnp.concatenate([flat[side, pl.ds(row, loc, stride=lat), :] for side in range(lon // BLK)], axis=1)

    for side, rows in enumerate((top, bottom)):
        for place, row in enumerate(rows):
            value = of_row(row)
            wide[SMOOTH + row] = value
            edge[side, place] = value.astype(BF16)
    for row in range(SMOOTH, lat - SMOOTH):
        wide[SMOOTH + row] = of_row(row)
    kext_ref[8 : lat + 8, :] = kappa_ref[...]
    spread_kappa(n_src, me, kext_ref, kwide, keep, range(SMOOTH, lat + SMOOTH))
    edges = [
        remote(edge.at[1], halo.at[0], edge_send.at[0], edge_recv.at[0], after),
        remote(edge.at[0], halo.at[1], edge_send.at[1], edge_recv.at[1], before),
        remote(kappa_ref.at[pl.ds(lat - 8, 8)], kext_ref.at[pl.ds(0, 8)], edge_send.at[2], edge_recv.at[2], after),
        remote(kappa_ref.at[pl.ds(0, 8)], kext_ref.at[pl.ds(lat + 8, 8)], edge_send.at[3], edge_recv.at[3], before),
    ]

    parts = ((SMOOTH, lat - SMOOTH), (0, SMOOTH), (lat - SMOOTH, lat))

    def place(owner, part, slab):
        first, last = parts[part]
        return field_ref.at[
            pl.ds(2 * first, 2 * (last - first)), pl.ds(pl.multiple_of(owner * loc + slab * SLAB, SLAB), SLAB), :
        ]

    def to_twin(part, slab):
        where = place(group, part, slab)
        return remote(where, where, send.at[0, part, slab], recv.at[0, part, slab], (me, twin))

    def to_opposite(part, slab):
        where = place(group, part, slab)
        return remote(where, where, send.at[1, part, slab], recv.at[1, part, slab], (me, opposite))

    def relay(part, slab):
        where = place(opposite, part, slab)
        return remote(where, where, send.at[2, part, slab], recv.at[2, part, slab], (me, twin))

    def smooth_part(part, slab):
        first, last = parts[part]
        groups = []
        for half in range(SLAB // 8):
            some = pl.ds(pl.multiple_of(slab * SLAB + half * 8, 8), 8)
            value = halves_of(wide, slice(first, last + 2 * SMOOTH), some)
            for step in range(SMOOTH):
                rows = slice(first + step + 1, last + 2 * SMOOTH - 1 - step)
                centre = [v[1:-1] for v in value]
                around = beside(*centre)
                value = [
                    c * k + w * (v[:-2] + v[2:] + a)
                    for c, k, w, v, a in zip(
                        centre, halves_of(keep, rows, slice(None)), halves_of(kwide, rows, slice(None)), value, around
                    )
                ]
            groups.append(value)
        mine = pl.ds(pl.multiple_of(group * loc + slab * SLAB, SLAB), SLAB)
        for side in range(2):
            smoothed = jnp.concatenate([g[side] for g in groups], axis=1).astype(BF16)
            for row in range(first, last):
                field_ref[2 * row + side, mine, :] = smoothed[row - first]

    def post(part, slab):
        to_opposite(part, slab).start()
        to_twin(part, slab).start()

    def inner(slab, carry):
        smooth_part(0, slab)
        post(0, slab)
        return carry

    def outer(slab, carry):
        for part in (1, 2):
            smooth_part(part, slab)
            post(part, slab)
        return carry

    smooth_part(0, 0)
    await_all(partners)
    post(0, 0)
    for copy in edges:
        copy.start()
    lax.fori_loop(1, slabs, inner, 0)
    for copy in edges:
        copy.wait()
    wide[0:SMOOTH] = jnp.where(me == 0, 0.0, halo[0].astype(F32))
    wide[lat + SMOOTH :] = jnp.where(me == n_src - 1, 0.0, halo[1].astype(F32))
    spread_kappa(n_src, me, kext_ref, kwide, keep, [*range(SMOOTH), *range(lat + SMOOTH, lat + 2 * SMOOTH)])
    lax.fori_loop(0, slabs, outer, 0)
    make_plan(source_ref, receptor_ref, count_ref, plan_ref)

    def pass_on(parts_here):
        def one(slab, carry):
            for part in parts_here:
                to_opposite(part, slab).wait_recv()
                relay(part, slab).start()
            return carry

        lax.fori_loop(0, slabs, one, 0)

    pass_on((0,))
    pass_on((1, 2))

    def finish(slab, carry):
        for part in range(3):
            to_opposite(part, slab).wait_send()
            to_twin(part, slab).wait()
            relay(part, slab).wait()
        return carry

    lax.fori_loop(0, slabs, finish, 0)


def smooth_and_gather(n_src, n_rcv, probes, kappa, sources, receptors, count):
    lat, lon = kappa.shape
    loc = probes.shape[0] // lat
    slabs = loc // SLAB
    dma = pltpu.SemaphoreType.DMA
    return pl.pallas_call(
        functools.partial(smooth_kernel, n_src),
        out_shape=(
            jax.ShapeDtypeStruct((lat * lon // BLK, loc * n_rcv, BLK), BF16),
            jax.ShapeDtypeStruct((lat + 16, lon), F32),
            jax.ShapeDtypeStruct((16, 256), jnp.int32),
        ),
        in_specs=[pl.BlockSpec(memory_space=VMEM)] * 5,
        out_specs=(pl.BlockSpec(memory_space=VMEM),) * 3,
        scratch_shapes=[
            VMEM((lon // BLK, loc * lat, BLK), F32),
            VMEM((2, SMOOTH, loc, lon), BF16),
            VMEM((2, SMOOTH, loc, lon), BF16),
            VMEM((lat + 2 * SMOOTH, loc, lon), F32),
            VMEM((lat + 2 * SMOOTH, 8, lon), F32),
            VMEM((lat + 2 * SMOOTH, 8, lon), F32),
            dma((4,)),
            dma((4,)),
            dma((3, 3, slabs)),
            dma((3, 3, slabs)),
        ],
        compiler_params=pltpu.CompilerParams(
            collective_id=0, has_side_effects=True, vmem_limit_bytes=VMEM_LIMIT
        ),
        cost_estimate=pl.CostEstimate(flops=20_000_000_000, bytes_accessed=64_000_000, transcendentals=0),
        name="smooth_and_gather",
    )(probes, kappa, sources, receptors, count)


def running_sums(plan_ref, base, slots, product, products, sums):
    together = products.shape[0]

    def several(turn, total):
        for step in range(together):
            k = turn * together + step
            products[step] = product(plan_ref[base, k], plan_ref[base + 1, k])
        for step in range(together):
            k = turn * together + step
            total = products[step] + total * plan_ref[base + 2, k].astype(F32)
            sums[k] = total.astype(BF16)
        return total

    lax.fori_loop(0, slots // together, several, jnp.zeros(sums.shape[1:], F32))


def block_sum(plan_ref, base, block, sums):
    value = sums[plan_ref[base + 3, block]]
    return (value.astype(F32) * plan_ref[base + 4, block].astype(F32)).astype(BF16)


def reduce_kernel(
    planes, plan_ref, field_ref, blocks_ref, weight_ref, out_ref, products, sums, mine_ref, first, part, second, line, mixed, last, *sems
):
    me = lax.axis_index("src")
    group = lax.axis_index("rcv")
    plane, spot = me // PLANE, me % PLANE
    pairs = iter(sems)
    a_plane, a_line, c_line, c_plane, ga_line, ga_plane, gc_plane, gc_line = zip(pairs, pairs)
    rows = mine_ref.shape[2]
    cut = rows * 3 // 4
    upper, lower = pl.ds(0, cut), pl.ds(cut, rows - cut)
    half_probes = field_ref.shape[1] // 2
    groups = 2
    size = planes // groups
    in_planes = range(1, PLANE)
    in_lines = range(1, planes)

    def spot_of(distance):
        return lax.rem(spot + distance, PLANE)

    def plane_of(distance):
        return lax.rem(plane + distance, planes)

    def in_plane(distance):
        return (plane * PLANE + spot_of(distance), group)

    def in_line(distance):
        return (plane_of(distance) * PLANE + spot, group)

    def copy(pair, index, src, dst, device):
        return remote(src, dst, pair[0].at[index], pair[1].at[index], device)

    def some(g):
        return pl.ds(g * size, size)

    def scatter_a_plane(d, g):
        return copy(
            a_plane, (d - 1, g), mine_ref.at[spot_of(d), some(g), upper], first.at[d - 1, some(g)], in_plane(d)
        )

    def scatter_a_line(piece):
        d = lax.rem(piece + planes - plane, planes)
        return copy(a_line, (d - 1,), part.at[piece], second.at[d - 1], (piece * PLANE + spot, group))

    def scatter_c_line(d):
        return copy(c_line, (d - 1,), mine_ref.at[:, plane_of(d), lower], line.at[d - 1], in_line(d))

    def scatter_c_plane(d):
        return copy(c_plane, (d - 1,), mixed.at[spot_of(d)], last.at[d - 1], in_plane(d))

    def gather_a_line(d):
        where = out_ref.at[spot, plane, upper]
        return copy(ga_line, (d - 1,), where, where, in_line(d))

    def gather_a_plane(d, g):
        where = out_ref.at[spot, some(g), upper]
        return copy(ga_plane, (d - 1, g), where, where, in_plane(d))

    def gather_c_plane(d):
        where = out_ref.at[spot, plane, lower]
        return copy(gc_plane, (d - 1,), where, where, in_plane(d))

    def gather_c_line(d):
        where = out_ref.at[:, plane, lower]
        return copy(gc_line, (d - 1,), where, where, in_line(d))

    per_block = max(1, half_probes // rows)
    weight = jnp.concatenate(
        [
            jnp.broadcast_to(
                weight_ref[pl.ds(spot * (RB_LOC // PLANE) + plane % size // per_block + extra, 1), :],
                (min(rows, half_probes), BLK),
            )
            for extra in range(max(1, rows // half_probes))
        ],
        axis=0,
    )

    def forward(half):
        def product(slot, source):
            return lax.dot_general(
                field_ref[source, half * half_probes : (half + 1) * half_probes, :],
                blocks_ref[slot],
                (((1,), (1,)), ((), ())),
                preferred_element_type=F32,
            )

        running_sums(plan_ref, 0, blocks_ref.shape[0], product, products, sums)
        step = min(rows, half_probes)
        for block in range(RB_LOC):
            value = block_sum(plan_ref, 0, block, sums)
            for inner in range(half_probes // step):
                at = block % 2 * half_probes + inner * step
                mine_ref[block // 2, half * size + at // rows, at % rows : at % rows + step] = value[
                    inner * step : (inner + 1) * step
                ]

    def begin_group(g):
        for d in in_planes:
            scatter_a_plane(d, g).start()

    def plane_sums(g):
        for d in in_planes:
            scatter_a_plane(d, g).wait_recv()
        for index in range(size):
            piece = g * size + index
            total = mine_ref[spot, piece, 0:cut].astype(F32)
            for other in range(PLANE - 1):
                total = total + first[other, piece].astype(F32)
            part[piece] = total.astype(BF16)

            @pl.when(piece != plane)
            def _():
                scatter_a_line(piece).start()

    def own_rows(g):
        @pl.when(plane // size == g)
        def _():
            for d in in_lines:
                copy(a_line, (d - 1,), part.at[plane], second.at[d - 1], in_line(d)).wait_recv()
            total = part[plane].astype(F32)
            for other in range(planes - 1):
                total = total + second[other].astype(F32)
            out_ref[spot, plane, 0:cut] = (total * weight[0:cut]).astype(BF16)
            for d in in_lines:
                gather_a_line(d).start()

    def spread_group(g):
        for index in range(size):
            piece = g * size + index

            @pl.when(piece != plane)
            def _():
                where = out_ref.at[spot, piece, upper]
                sender = lax.rem(plane + planes - piece, planes) - 1
                copy(ga_line, (sender,), where, where, in_line(1)).wait_recv()

        for d in in_planes:
            gather_a_plane(d, g).start()

    def line_sums():
        for d in in_lines:
            scatter_c_line(d).wait_recv()
        for d in [*in_planes, 0]:
            piece = spot_of(d)
            total = mine_ref[piece, plane, cut:rows].astype(F32)
            for other in range(planes - 1):
                total = total + line[other, piece].astype(F32)
            mixed[piece] = total.astype(BF16)
            if d:
                scatter_c_plane(d).start()

    def own_lower_rows():
        for d in in_planes:
            scatter_c_plane(d).wait_recv()
        total = mixed[spot].astype(F32)
        for other in range(PLANE - 1):
            total = total + last[other].astype(F32)
        out_ref[spot, plane, cut:rows] = (total * weight[cut:rows]).astype(BF16)
        for d in in_planes:
            gather_c_plane(d).start()

    def spread_lower_rows():
        for d in in_planes:
            gather_c_plane(d).wait_recv()
        for d in in_lines:
            gather_c_line(d).start()

    partners = [in_plane(d) for d in in_planes] + [in_line(d) for d in in_lines]
    announce(partners)
    forward(0)
    await_all(partners)
    begin_group(0)
    forward(1)
    for d in in_lines:
        scatter_c_line(d).start()
    begin_group(1)
    plane_sums(0)
    line_sums()
    plane_sums(1)
    own_lower_rows()
    own_rows(0)
    own_rows(1)
    spread_group(0)
    spread_lower_rows()
    spread_group(1)
    for d in in_planes:
        for g in range(groups):
            gather_a_plane(d, g).wait()
            scatter_a_plane(d, g).wait_send()
        scatter_c_plane(d).wait_send()
        gather_c_plane(d).wait_send()
    for d in in_lines:
        gather_c_line(d).wait()
        gather_a_line(d).wait_send()
        scatter_c_line(d).wait_send()
        copy(a_line, (d - 1,), part.at[plane], second.at[d - 1], in_line(d)).wait_send()


def reduce_and_weigh(n_src, plan, field, blocks, weight):
    probes = field.shape[1]
    slots = blocks.shape[0]
    planes = n_src // PLANE
    rows = RB_LOC * probes // (PLANE * planes)
    cut = rows * 3 // 4
    dma = pltpu.SemaphoreType.DMA
    per_spot, per_plane, parts = (PLANE - 1,), (planes - 1,), (PLANE - 1, 2)
    counts = (parts, per_plane, per_plane, per_spot, per_plane, parts, per_spot, per_plane)
    return pl.pallas_call(
        functools.partial(reduce_kernel, planes),
        out_shape=jax.ShapeDtypeStruct((PLANE, planes, rows, BLK), BF16),
        in_specs=[pl.BlockSpec(memory_space=pltpu.SMEM)] + [pl.BlockSpec(memory_space=VMEM)] * 3,
        out_specs=pl.BlockSpec(memory_space=VMEM),
        scratch_shapes=[
            VMEM((min(TOGETHER, slots), probes // 2, BLK), F32),
            VMEM((slots, probes // 2, BLK), BF16),
            VMEM((PLANE, planes, rows, BLK), BF16),
            VMEM((PLANE - 1, planes, cut, BLK), BF16),
            VMEM((planes, cut, BLK), BF16),
            VMEM((planes - 1, cut, BLK), BF16),
            VMEM((planes - 1, PLANE, rows - cut, BLK), BF16),
            VMEM((PLANE, rows - cut, BLK), BF16),
            VMEM((PLANE - 1, rows - cut, BLK), BF16),
        ]
        + [dma(count) for count in counts for _ in range(2)],
        compiler_params=pltpu.CompilerParams(
            collective_id=1, has_side_effects=True, vmem_limit_bytes=VMEM_LIMIT
        ),
        name="reduce_and_weigh",
    )(plan, field, blocks, weight)


def back_kernel(
    n_src, plan_ref, weighted_ref, blocks_ref, probes_ref, kext_ref, out_ref, products, sums, terms_far, terms_near, pair, relayed, joined, far, edge, halo, wide, kwide, keep, flat,
    edge_send, edge_recv, send, recv,
):
    me, group, before, after, twin, opposite = neighbours(n_src)
    lat = kext_ref.shape[0] - 16
    loc, lon = probes_ref.shape[0] // lat, probes_ref.shape[1]
    slabs = loc // SLAB
    high, core = group // 2, group % 2
    partners = [before, after, (me, twin), (me, opposite)]
    announce(partners)

    def view(ref, k, offset=0):
        if isinstance(k, int) and k < 2:
            return ref.at[pl.ds(k * (lat - SMOOTH), SMOOTH), pl.ds(pl.multiple_of(offset, loc), loc), :]
        start = pl.multiple_of(offset + (k - 2) * SLAB, SLAB)
        return ref.at[pl.ds(SMOOTH, lat - 2 * SMOOTH), pl.ds(start, SLAB), :]

    def term(terms, core_of, k):
        return view(terms, k, core_of * loc)

    def adjoint(half, terms):
        def product(slot, place):
            block = weighted_ref[place + half * 2]
            return jnp.dot(block, blocks_ref[slot], preferred_element_type=F32)

        running_sums(plan_ref, 8, blocks_ref.shape[0], product, products, sums)
        for row in range(lat):
            for side in range(2):
                terms[row, :, side * BLK : (side + 1) * BLK] = block_sum(plan_ref, 8, 2 * row + side, sums)

    def for_relay(k):
        return remote(term(terms_far, 1 - core, k), view(relayed, k), send.at[0, k], recv.at[0, k], (me, twin))

    def for_twin(k):
        return remote(term(terms_near, 1 - core, k), view(pair, k), send.at[1, k], recv.at[1, k], (me, twin))

    def across(k):
        return remote(view(joined, k), view(far, k), send.at[2, k], recv.at[2, k], (me, opposite))

    def each(work):
        work(0)
        work(1)
        lax.fori_loop(2, slabs + 2, lambda k, carry: (work(k), carry)[1], 0)

    def join(k):
        for_relay(k).wait_recv()
        view(joined, k)[...] = (
            term(terms_far, core, k)[...].astype(F32) + view(relayed, k)[...].astype(F32)
        ).astype(BF16)
        across(k).start()

    def total(k):
        for_twin(k).wait_recv()
        across(k).wait_recv()
        return term(terms_near, core, k)[...].astype(F32) + view(pair, k)[...].astype(F32) + view(far, k)[...].astype(F32)

    edges = [
        remote(edge.at[0], halo.at[1], edge_send.at[0], edge_recv.at[0], before),
        remote(edge.at[1], halo.at[0], edge_send.at[1], edge_recv.at[1], after),
    ]
    adjoint(1 - high, terms_far)
    await_all(partners)
    each(lambda k: for_relay(k).start())
    spread_kappa(n_src, me, kext_ref, kwide, keep, range(lat + 2 * SMOOTH))
    each(join)
    adjoint(high, terms_near)
    each(lambda k: for_twin(k).start())
    for k, row in ((0, SMOOTH), (1, lat)):
        rows = total(k)
        wide[row : row + SMOOTH] = rows
        edge[k] = rows.astype(BF16)
        edges[k].start()

    def one_slab(slab, carry):
        probes_here = pl.ds(pl.multiple_of(slab * SLAB, SLAB), SLAB)
        wide[2 * SMOOTH : lat, probes_here, :] = total(slab + 2)

        @pl.when(slab == 0)
        def _():
            for copy in edges:
                copy.wait()
            wide[0:SMOOTH] = halo[0].astype(F32)
            wide[lat + SMOOTH :] = halo[1].astype(F32)

        for half in range(SLAB // 8):
            some = pl.ds(pl.multiple_of(slab * SLAB + half * 8, 8), 8)
            value = halves_of(wide, slice(None), some)
            for step in range(SMOOTH):
                rows = slice(step, lat + 2 * SMOOTH - step)
                scaled = [w * v for w, v in zip(halves_of(kwide, rows, slice(None)), value)]
                around = beside(*[v[1:-1] for v in scaled])
                inner = slice(step + 1, lat + 2 * SMOOTH - 1 - step)
                value = [
                    v[1:-1] * k + (g[:-2] + g[2:] + a)
                    for v, k, g, a in zip(value, halves_of(keep, inner, slice(None)), scaled, around)
                ]
            for side in range(2):
                for row in range(lat):
                    flat[side, pl.ds(half * 8 * lat + row, 8, stride=lat), :] = value[side][row]
        some = pl.ds(pl.multiple_of(slab * SLAB * lat, SLAB * lat), SLAB * lat)
        for side in range(2):
            lanes = slice(side * BLK, (side + 1) * BLK)
            out_ref[some, lanes] = flat[side] + probes_ref[some, lanes].astype(F32)
        return carry

    lax.fori_loop(0, slabs, one_slab, 0)

    def finish(k):
        for_relay(k).wait_send()
        for_twin(k).wait_send()
        across(k).wait_send()

    each(finish)


def scatter_and_smooth(n_src, plan, weighted, blocks, probes, kext):
    lat = kext.shape[0] - 16
    loc, lon = probes.shape[0] // lat, probes.shape[1]
    pieces = loc // SLAB + 2
    landing = VMEM((lat, loc, lon), BF16)
    dma = pltpu.SemaphoreType.DMA
    return pl.pallas_call(
        functools.partial(back_kernel, n_src),
        out_shape=jax.ShapeDtypeStruct(probes.shape, F32),
        in_specs=[pl.BlockSpec(memory_space=pltpu.SMEM)] + [pl.BlockSpec(memory_space=VMEM)] * 4,
        out_specs=pl.BlockSpec(memory_space=VMEM),
        scratch_shapes=[
            VMEM((min(TOGETHER, blocks.shape[0]), 2 * loc, BLK), F32),
            VMEM((blocks.shape[0], 2 * loc, BLK), BF16),
            VMEM((lat, 2 * loc, lon), BF16),
            VMEM((lat, 2 * loc, lon), BF16),
            landing,
            landing,
            landing,
            landing,
            VMEM((2, SMOOTH, loc, lon), BF16),
            VMEM((2, SMOOTH, loc, lon), BF16),
            VMEM((lat + 2 * SMOOTH, loc, lon), F32),
            VMEM((lat + 2 * SMOOTH, 8, lon), F32),
            VMEM((lat + 2 * SMOOTH, 8, lon), F32),
            VMEM((lon // BLK, SLAB * lat, BLK), F32),
            dma((2,)),
            dma((2,)),
            dma((3, pieces)),
            dma((3, pieces)),
        ],
        compiler_params=pltpu.CompilerParams(
            collective_id=2, has_side_effects=True, vmem_limit_bytes=VMEM_LIMIT
        ),
        name="scatter_and_smooth",
    )(plan, weighted, blocks, probes, kext)


def per_device(probes, kappa, footprint, block_source, block_receptor, block_count, obs_weight):
    n_src, n_rcv = lax.axis_size("src"), lax.axis_size("rcv")
    loc, lat, lon = probes.shape
    flat = probes.reshape(loc * lat, lon)
    blocks = footprint.reshape(footprint.shape[2:])
    slots = blocks.shape[0]
    field, kext, plan = smooth_and_gather(
        n_src, n_rcv, flat, kappa, block_source.reshape(1, slots), block_receptor.reshape(1, slots), block_count.reshape(1, 1)
    )
    weighted = reduce_and_weigh(n_src, plan, field, blocks, obs_weight.reshape(RB_LOC, BLK))
    weighted = weighted.reshape(2 * RB_LOC, loc * n_rcv // 2, BLK)
    out = scatter_and_smooth(n_src, plan, weighted, blocks, flat, kext)
    return out.reshape(loc, lat, lon)


def solution(mesh):
    placed = (
        P("rcv", "src", None),
        P("src", None),
        P("src", "rcv", None, None, None),
        P("src", "rcv", None),
        P("src", "rcv", None),
        P("src", "rcv"),
        P("rcv"),
    )
    return jax.shard_map(
        per_device, mesh=mesh, in_specs=placed, out_specs=P("rcv", "src", None), check_vma=False
    )
```

```python
import functools

import jax
import jax.numpy as jnp
from jax import lax
from jax.experimental import pallas as pl
from jax.experimental.pallas import tpu as pltpu
from jax.sharding import PartitionSpec as P

BLK = 128
RB_LOC = 16
SMOOTH = 4
PLANE = 8
SLAB = 16
SLOT_BASE = 64
TOGETHER = 32
MESH = pl.DeviceIdType.MESH
VMEM = pltpu.VMEM
F32 = jnp.float32
BF16 = jnp.bfloat16
VMEM_LIMIT = 32 * 1024 * 1024


def announce(devices):
    barrier = pltpu.get_barrier_semaphore()
    for device in devices:
        pl.semaphore_signal(barrier, inc=1, device_id=device, device_id_type=MESH)


def await_all(devices):
    pl.semaphore_wait(pltpu.get_barrier_semaphore(), len(devices))


def remote(src, dst, send_sem, recv_sem, device):
    return pltpu.make_async_remote_copy(
        src_ref=src,
        dst_ref=dst,
        send_sem=send_sem,
        recv_sem=recv_sem,
        device_id=device,
        device_id_type=MESH,
    )


def neighbours(n_src):
    me = lax.axis_index("src")
    group = lax.axis_index("rcv")
    high, core = group // 2, group % 2
    before = (lax.rem(me + n_src - 1, n_src), group)
    after = (lax.rem(me + 1, n_src), group)
    twin = high * 2 + (1 - core)
    opposite = (1 - high) * 2 + core
    return me, group, before, after, twin, opposite


def beside(west_half, east_half):
    axis = west_half.ndim - 1
    lane = lax.broadcasted_iota(jnp.int32, west_half.shape, axis)
    first, last = lane == 0, lane == BLK - 1
    up_w, up_e = pltpu.roll(west_half, 1, axis), pltpu.roll(east_half, 1, axis)
    down_w, down_e = pltpu.roll(west_half, BLK - 1, axis), pltpu.roll(east_half, BLK - 1, axis)
    return (
        jnp.where(first, 0.0, up_w) + jnp.where(last, down_e, down_w),
        jnp.where(first, up_w, up_e) + jnp.where(last, 0.0, down_e),
    )


def halves_of(ref, rows, *middle):
    return [ref[(rows, *middle, slice(side * BLK, (side + 1) * BLK))] for side in range(2)]


def spread_kappa(n_src, me, kext_ref, kwide, keep, rows):
    for row in rows:
        value = kext_ref[8 - SMOOTH + row : 8 - SMOOTH + row + 1, :]
        if row < SMOOTH:
            value = jnp.where(me == 0, 0.0, value)
        if row >= kwide.shape[0] - SMOOTH:
            value = jnp.where(me == n_src - 1, 0.0, value)
        wide = jnp.broadcast_to(value, kwide.shape[1:])
        kwide[row] = wide
        keep[row] = 1.0 - 4.0 * wide


def make_plan(packed, plan_ref):
    slots, lanes = packed.shape[1], plan_ref.shape[1]
    sources, receptors = packed % SLOT_BASE, packed // SLOT_BASE % SLOT_BASE
    row_of = lax.broadcasted_iota(jnp.int32, (slots, slots), 0)
    lane_of = lax.broadcasted_iota(jnp.int32, (slots, slots), 1)
    place = lax.broadcasted_iota(jnp.int32, (slots, lanes), 1)
    slot = lax.broadcasted_iota(jnp.int32, (1, slots), 1)
    used = packed < SLOT_BASE * SLOT_BASE

    def place_of(receptor):
        return receptor // 2 * 4 + receptor % 2

    def column(row):
        return jnp.sum(jnp.where(row_of == lane_of, row, 0.0), axis=1, keepdims=True)

    first_lane = lax.broadcasted_iota(jnp.int32, (1, lanes), 1) == 0
    for base, owner, other in ((0, receptors, sources), (8, sources, place_of(receptors))):
        key = jnp.where(used, owner * 256 + slot, 64 * 256 + slot).astype(F32)
        tall = column(key)
        rank = jnp.sum(jnp.where(key < tall, 1.0, 0.0), axis=1, keepdims=True)
        here = rank.astype(jnp.int32) == place

        def ordered(values):
            return jnp.sum(jnp.where(here, values, 0.0), axis=0, keepdims=True).astype(jnp.int32)

        keys = ordered(tall)
        block = keys // 256
        ends = jnp.sum(
            jnp.where(tall < ((place + 1) * 256).astype(F32), 1.0, 0.0), axis=0, keepdims=True
        ).astype(jnp.int32)
        start = jnp.where(first_lane, 0, pltpu.roll(ends, 1, 1))
        same = (block == pltpu.roll(block, 1, 1)) & jnp.logical_not(first_lane)
        plan_ref[base : base + 1, :] = keys - block * 256
        plan_ref[base + 1 : base + 2, :] = ordered(column(other.astype(F32)))
        plan_ref[base + 2 : base + 3, :] = same.astype(jnp.int32)
        plan_ref[base + 3 : base + 4, :] = jnp.maximum(ends - 1, 0)
        plan_ref[base + 4 : base + 5, :] = (ends > start).astype(jnp.int32)


def smooth_kernel(
    n_src, probes_ref, kappa_ref, slots_ref, field_ref, kext_ref, plan_ref, flat, halo, edge, wide, kwide, keep,
    edge_send, edge_recv, send, recv,
):
    me, group, before, after, twin, opposite = neighbours(n_src)
    lat, lon = kappa_ref.shape
    loc = probes_ref.shape[0] // lat
    slabs = loc // SLAB
    partners = [before, after, (me, twin), (me, opposite)]
    announce(partners)

    top, bottom = range(SMOOTH), range(lat - SMOOTH, lat)
    for side in range(lon // BLK):
        flat[side] = probes_ref[:, side * BLK : (side + 1) * BLK].astype(F32)

    def of_row(row):
        return jnp.concatenate([flat[side, pl.ds(row, loc, stride=lat), :] for side in range(lon // BLK)], axis=1)

    for side, rows in enumerate((top, bottom)):
        for place, row in enumerate(rows):
            value = of_row(row)
            wide[SMOOTH + row] = value
            edge[side, place] = value.astype(BF16)
    for row in range(SMOOTH, lat - SMOOTH):
        wide[SMOOTH + row] = of_row(row)
    kext_ref[8 : lat + 8, :] = kappa_ref[...]
    spread_kappa(n_src, me, kext_ref, kwide, keep, range(SMOOTH, lat + SMOOTH))
    edges = [
        remote(edge.at[1], halo.at[0], edge_send.at[0], edge_recv.at[0], after),
        remote(edge.at[0], halo.at[1], edge_send.at[1], edge_recv.at[1], before),
        remote(kappa_ref.at[pl.ds(lat - 8, 8)], kext_ref.at[pl.ds(0, 8)], edge_send.at[2], edge_recv.at[2], after),
        remote(kappa_ref.at[pl.ds(0, 8)], kext_ref.at[pl.ds(lat + 8, 8)], edge_send.at[3], edge_recv.at[3], before),
    ]

    parts = ((SMOOTH, lat - SMOOTH), (0, SMOOTH), (lat - SMOOTH, lat))

    def place(owner, part, slab):
        first, last = parts[part]
        return field_ref.at[
            pl.ds(2 * first, 2 * (last - first)), pl.ds(pl.multiple_of(owner * loc + slab * SLAB, SLAB), SLAB), :
        ]

    def to_twin(part, slab):
        where = place(group, part, slab)
        return remote(where, where, send.at[0, part, slab], recv.at[0, part, slab], (me, twin))

    def to_opposite(part, slab):
        where = place(group, part, slab)
        return remote(where, where, send.at[1, part, slab], recv.at[1, part, slab], (me, opposite))

    def relay(part, slab):
        where = place(opposite, part, slab)
        return remote(where, where, send.at[2, part, slab], recv.at[2, part, slab], (me, twin))

    def smooth_part(part, slab):
        first, last = parts[part]
        groups = []
        for half in range(SLAB // 8):
            some = pl.ds(pl.multiple_of(slab * SLAB + half * 8, 8), 8)
            value = halves_of(wide, slice(first, last + 2 * SMOOTH), some)
            for step in range(SMOOTH):
                rows = slice(first + step + 1, last + 2 * SMOOTH - 1 - step)
                centre = [v[1:-1] for v in value]
                around = beside(*centre)
                value = [
                    c * k + w * (v[:-2] + v[2:] + a)
                    for c, k, w, v, a in zip(
                        centre, halves_of(keep, rows, slice(None)), halves_of(kwide, rows, slice(None)), value, around
                    )
                ]
            groups.append(value)
        mine = pl.ds(pl.multiple_of(group * loc + slab * SLAB, SLAB), SLAB)
        for side in range(2):
            smoothed = jnp.concatenate([g[side] for g in groups], axis=1).astype(BF16)
            for row in range(first, last):
                field_ref[2 * row + side, mine, :] = smoothed[row - first]

    def post(part, slab):
        to_opposite(part, slab).start()
        to_twin(part, slab).start()

    def inner(slab, carry):
        smooth_part(0, slab)
        post(0, slab)
        return carry

    def outer(slab, carry):
        for part in (1, 2):
            smooth_part(part, slab)
            post(part, slab)
        return carry

    smooth_part(0, 0)
    await_all(partners)
    post(0, 0)
    for copy in edges:
        copy.start()
    lax.fori_loop(1, slabs, inner, 0)
    for copy in edges:
        copy.wait()
    wide[0:SMOOTH] = jnp.where(me == 0, 0.0, halo[0].astype(F32))
    wide[lat + SMOOTH :] = jnp.where(me == n_src - 1, 0.0, halo[1].astype(F32))
    spread_kappa(n_src, me, kext_ref, kwide, keep, [*range(SMOOTH), *range(lat + SMOOTH, lat + 2 * SMOOTH)])
    lax.fori_loop(0, slabs, outer, 0)
    make_plan(slots_ref[...], plan_ref)

    def pass_on(parts_here):
        def one(slab, carry):
            for part in parts_here:
                to_opposite(part, slab).wait_recv()
                relay(part, slab).start()
            return carry

        lax.fori_loop(0, slabs, one, 0)

    pass_on((0,))
    pass_on((1, 2))

    def finish(slab, carry):
        for part in range(3):
            to_opposite(part, slab).wait_send()
            to_twin(part, slab).wait()
            relay(part, slab).wait()
        return carry

    lax.fori_loop(0, slabs, finish, 0)


def smooth_and_gather(n_src, n_rcv, probes, kappa, packed):
    lat, lon = kappa.shape
    loc = probes.shape[0] // lat
    slabs = loc // SLAB
    dma = pltpu.SemaphoreType.DMA
    return pl.pallas_call(
        functools.partial(smooth_kernel, n_src),
        out_shape=(
            jax.ShapeDtypeStruct((lat * lon // BLK, loc * n_rcv, BLK), BF16),
            jax.ShapeDtypeStruct((lat + 16, lon), F32),
            jax.ShapeDtypeStruct((16, 256), jnp.int32),
        ),
        in_specs=[pl.BlockSpec(memory_space=VMEM)] * 3,
        out_specs=(pl.BlockSpec(memory_space=VMEM),) * 3,
        scratch_shapes=[
            VMEM((lon // BLK, loc * lat, BLK), F32),
            VMEM((2, SMOOTH, loc, lon), BF16),
            VMEM((2, SMOOTH, loc, lon), BF16),
            VMEM((lat + 2 * SMOOTH, loc, lon), F32),
            VMEM((lat + 2 * SMOOTH, 8, lon), F32),
            VMEM((lat + 2 * SMOOTH, 8, lon), F32),
            dma((4,)),
            dma((4,)),
            dma((3, 3, slabs)),
            dma((3, 3, slabs)),
        ],
        compiler_params=pltpu.CompilerParams(
            collective_id=0, has_side_effects=True, vmem_limit_bytes=VMEM_LIMIT
        ),
        cost_estimate=pl.CostEstimate(flops=20_000_000_000, bytes_accessed=64_000_000, transcendentals=0),
        name="smooth_and_gather",
    )(probes, kappa, packed)


def running_sums(plan_ref, base, slots, product, products, sums):
    together = products.shape[0]

    def several(turn, total):
        for step in range(together):
            k = turn * together + step
            products[step] = product(plan_ref[base, k], plan_ref[base + 1, k])
        for step in range(together):
            k = turn * together + step
            total = products[step] + total * plan_ref[base + 2, k].astype(F32)
            sums[k] = total.astype(BF16)
        return total

    lax.fori_loop(0, slots // together, several, jnp.zeros(sums.shape[1:], F32))


def block_sum(plan_ref, base, block, sums):
    value = sums[plan_ref[base + 3, block]]
    return (value.astype(F32) * plan_ref[base + 4, block].astype(F32)).astype(BF16)


def reduce_kernel(
    planes, plan_ref, field_ref, blocks_ref, weight_ref, out_ref, products, sums, mine_ref, first, part, second, line, mixed, last, *sems
):
    me = lax.axis_index("src")
    group = lax.axis_index("rcv")
    plane, spot = me // PLANE, me % PLANE
    pairs = iter(sems)
    a_plane, a_line, c_line, c_plane, ga_line, ga_plane, gc_plane, gc_line = zip(pairs, pairs)
    rows = mine_ref.shape[2]
    cut = rows * 3 // 4
    upper, lower = pl.ds(0, cut), pl.ds(cut, rows - cut)
    half_probes = field_ref.shape[1] // 2
    groups = 2
    size = planes // groups
    in_planes = range(1, PLANE)
    in_lines = range(1, planes)

    def spot_of(distance):
        return lax.rem(spot + distance, PLANE)

    def plane_of(distance):
        return lax.rem(plane + distance, planes)

    def in_plane(distance):
        return (plane * PLANE + spot_of(distance), group)

    def in_line(distance):
        return (plane_of(distance) * PLANE + spot, group)

    def copy(pair, index, src, dst, device):
        return remote(src, dst, pair[0].at[index], pair[1].at[index], device)

    def some(g):
        return pl.ds(g * size, size)

    def scatter_a_plane(d, g):
        return copy(
            a_plane, (d - 1, g), mine_ref.at[spot_of(d), some(g), upper], first.at[d - 1, some(g)], in_plane(d)
        )

    def scatter_a_line(piece):
        d = lax.rem(piece + planes - plane, planes)
        return copy(a_line, (d - 1,), part.at[piece], second.at[d - 1], (piece * PLANE + spot, group))

    def scatter_c_line(d):
        return copy(c_line, (d - 1,), mine_ref.at[:, plane_of(d), lower], line.at[d - 1], in_line(d))

    def scatter_c_plane(d):
        return copy(c_plane, (d - 1,), mixed.at[spot_of(d)], last.at[d - 1], in_plane(d))

    def gather_a_line(d):
        where = out_ref.at[spot, plane, upper]
        return copy(ga_line, (d - 1,), where, where, in_line(d))

    def gather_a_plane(d, g):
        where = out_ref.at[spot, some(g), upper]
        return copy(ga_plane, (d - 1, g), where, where, in_plane(d))

    def gather_c_plane(d):
        where = out_ref.at[spot, plane, lower]
        return copy(gc_plane, (d - 1,), where, where, in_plane(d))

    def gather_c_line(d):
        where = out_ref.at[:, plane, lower]
        return copy(gc_line, (d - 1,), where, where, in_line(d))

    per_block = max(1, half_probes // rows)
    weight = jnp.concatenate(
        [
            jnp.broadcast_to(
                weight_ref[pl.ds(spot * (RB_LOC // PLANE) + plane % size // per_block + extra, 1), :],
                (min(rows, half_probes), BLK),
            )
            for extra in range(max(1, rows // half_probes))
        ],
        axis=0,
    )

    def product(slot, source):
        return lax.dot_general(
            field_ref[source], blocks_ref[slot], (((1,), (1,)), ((), ())), preferred_element_type=F32
        )

    def forward():
        running_sums(plan_ref, 0, blocks_ref.shape[0], product, products, sums)
        step = min(rows, half_probes)
        for block in range(RB_LOC):
            value = block_sum(plan_ref, 0, block, sums)
            for inner in range(2 * half_probes // step):
                half, at = divmod(inner * step, half_probes)
                at += block % 2 * half_probes
                mine_ref[block // 2, half * size + at // rows, at % rows : at % rows + step] = value[
                    inner * step : (inner + 1) * step
                ]

    def begin_group(g):
        for d in in_planes:
            scatter_a_plane(d, g).start()

    def plane_sums(g):
        for d in in_planes:
            scatter_a_plane(d, g).wait_recv()
        for index in range(size):
            piece = g * size + index
            total = mine_ref[spot, piece, 0:cut].astype(F32)
            for other in range(PLANE - 1):
                total = total + first[other, piece].astype(F32)
            part[piece] = total.astype(BF16)

            @pl.when(piece != plane)
            def _():
                scatter_a_line(piece).start()

    def own_rows(g):
        @pl.when(plane // size == g)
        def _():
            for d in in_lines:
                copy(a_line, (d - 1,), part.at[plane], second.at[d - 1], in_line(d)).wait_recv()
            total = part[plane].astype(F32)
            for other in range(planes - 1):
                total = total + second[other].astype(F32)
            out_ref[spot, plane, 0:cut] = (total * weight[0:cut]).astype(BF16)
            for d in in_lines:
                gather_a_line(d).start()

    def spread_group(g):
        for index in range(size):
            piece = g * size + index

            @pl.when(piece != plane)
            def _():
                where = out_ref.at[spot, piece, upper]
                sender = lax.rem(plane + planes - piece, planes) - 1
                copy(ga_line, (sender,), where, where, in_line(1)).wait_recv()

        for d in in_planes:
            gather_a_plane(d, g).start()

    def line_sums():
        for d in in_lines:
            scatter_c_line(d).wait_recv()
        for d in [*in_planes, 0]:
            piece = spot_of(d)
            total = mine_ref[piece, plane, cut:rows].astype(F32)
            for other in range(planes - 1):
                total = total + line[other, piece].astype(F32)
            mixed[piece] = total.astype(BF16)
            if d:
                scatter_c_plane(d).start()

    def own_lower_rows():
        for d in in_planes:
            scatter_c_plane(d).wait_recv()
        total = mixed[spot].astype(F32)
        for other in range(PLANE - 1):
            total = total + last[other].astype(F32)
        out_ref[spot, plane, cut:rows] = (total * weight[cut:rows]).astype(BF16)
        for d in in_planes:
            gather_c_plane(d).start()

    def spread_lower_rows():
        for d in in_planes:
            gather_c_plane(d).wait_recv()
        for d in in_lines:
            gather_c_line(d).start()

    partners = [in_plane(d) for d in in_planes] + [in_line(d) for d in in_lines]
    announce(partners)
    forward()
    await_all(partners)
    begin_group(0)
    for d in in_lines:
        scatter_c_line(d).start()
    begin_group(1)
    plane_sums(0)
    line_sums()
    plane_sums(1)
    own_lower_rows()
    own_rows(0)
    own_rows(1)
    spread_group(0)
    spread_lower_rows()
    spread_group(1)
    for d in in_planes:
        for g in range(groups):
            gather_a_plane(d, g).wait()
            scatter_a_plane(d, g).wait_send()
        scatter_c_plane(d).wait_send()
        gather_c_plane(d).wait_send()
    for d in in_lines:
        gather_c_line(d).wait()
        gather_a_line(d).wait_send()
        scatter_c_line(d).wait_send()
        copy(a_line, (d - 1,), part.at[plane], second.at[d - 1], in_line(d)).wait_send()


def reduce_and_weigh(n_src, plan, field, blocks, weight):
    probes = field.shape[1]
    slots = blocks.shape[0]
    planes = n_src // PLANE
    rows = RB_LOC * probes // (PLANE * planes)
    cut = rows * 3 // 4
    dma = pltpu.SemaphoreType.DMA
    per_spot, per_plane, parts = (PLANE - 1,), (planes - 1,), (PLANE - 1, 2)
    counts = (parts, per_plane, per_plane, per_spot, per_plane, parts, per_spot, per_plane)
    return pl.pallas_call(
        functools.partial(reduce_kernel, planes),
        out_shape=jax.ShapeDtypeStruct((PLANE, planes, rows, BLK), BF16),
        in_specs=[pl.BlockSpec(memory_space=pltpu.SMEM)] + [pl.BlockSpec(memory_space=VMEM)] * 3,
        out_specs=pl.BlockSpec(memory_space=VMEM),
        scratch_shapes=[
            VMEM((min(TOGETHER, slots), probes, BLK), F32),
            VMEM((slots, probes, BLK), BF16),
            VMEM((PLANE, planes, rows, BLK), BF16),
            VMEM((PLANE - 1, planes, cut, BLK), BF16),
            VMEM((planes, cut, BLK), BF16),
            VMEM((planes - 1, cut, BLK), BF16),
            VMEM((planes - 1, PLANE, rows - cut, BLK), BF16),
            VMEM((PLANE, rows - cut, BLK), BF16),
            VMEM((PLANE - 1, rows - cut, BLK), BF16),
        ]
        + [dma(count) for count in counts for _ in range(2)],
        compiler_params=pltpu.CompilerParams(
            collective_id=1, has_side_effects=True, vmem_limit_bytes=VMEM_LIMIT
        ),
        name="reduce_and_weigh",
    )(plan, field, blocks, weight)


def back_kernel(
    n_src, plan_ref, weighted_ref, blocks_ref, probes_ref, kext_ref, out_ref, products, sums, terms_far, terms_near, pair, relayed, joined, far, edge, halo, wide, kwide, keep, flat,
    edge_send, edge_recv, send, recv,
):
    me, group, before, after, twin, opposite = neighbours(n_src)
    lat = kext_ref.shape[0] - 16
    loc, lon = probes_ref.shape[0] // lat, probes_ref.shape[1]
    slabs = loc // SLAB
    high, core = group // 2, group % 2
    partners = [before, after, (me, twin), (me, opposite)]
    announce(partners)

    def view(ref, k, offset=0):
        if isinstance(k, int) and k < 2:
            return ref.at[pl.ds(k * (lat - SMOOTH), SMOOTH), pl.ds(pl.multiple_of(offset, loc), loc), :]
        start = pl.multiple_of(offset + (k - 2) * SLAB, SLAB)
        return ref.at[pl.ds(SMOOTH, lat - 2 * SMOOTH), pl.ds(start, SLAB), :]

    def term(terms, core_of, k):
        return view(terms, k, core_of * loc)

    def adjoint(half, terms):
        def product(slot, place):
            block = weighted_ref[place + half * 2]
            return jnp.dot(block, blocks_ref[slot], preferred_element_type=F32)

        running_sums(plan_ref, 8, blocks_ref.shape[0], product, products, sums)
        for row in range(lat):
            for side in range(2):
                terms[row, :, side * BLK : (side + 1) * BLK] = block_sum(plan_ref, 8, 2 * row + side, sums)

    def for_relay(k):
        return remote(term(terms_far, 1 - core, k), view(relayed, k), send.at[0, k], recv.at[0, k], (me, twin))

    def for_twin(k):
        return remote(term(terms_near, 1 - core, k), view(pair, k), send.at[1, k], recv.at[1, k], (me, twin))

    def across(k):
        return remote(view(joined, k), view(far, k), send.at[2, k], recv.at[2, k], (me, opposite))

    def each(work):
        work(0)
        work(1)
        lax.fori_loop(2, slabs + 2, lambda k, carry: (work(k), carry)[1], 0)

    def join(k):
        for_relay(k).wait_recv()
        view(joined, k)[...] = (
            term(terms_far, core, k)[...].astype(F32) + view(relayed, k)[...].astype(F32)
        ).astype(BF16)
        across(k).start()

    def total(k):
        for_twin(k).wait_recv()
        across(k).wait_recv()
        return term(terms_near, core, k)[...].astype(F32) + view(pair, k)[...].astype(F32) + view(far, k)[...].astype(F32)

    edges = [
        remote(edge.at[0], halo.at[1], edge_send.at[0], edge_recv.at[0], before),
        remote(edge.at[1], halo.at[0], edge_send.at[1], edge_recv.at[1], after),
    ]
    adjoint(1 - high, terms_far)
    await_all(partners)
    each(lambda k: for_relay(k).start())
    spread_kappa(n_src, me, kext_ref, kwide, keep, range(lat + 2 * SMOOTH))
    each(join)
    adjoint(high, terms_near)
    each(lambda k: for_twin(k).start())
    for k, row in ((0, SMOOTH), (1, lat)):
        rows = total(k)
        wide[row : row + SMOOTH] = rows
        edge[k] = rows.astype(BF16)
        edges[k].start()

    def one_slab(slab, carry):
        probes_here = pl.ds(pl.multiple_of(slab * SLAB, SLAB), SLAB)
        wide[2 * SMOOTH : lat, probes_here, :] = total(slab + 2)

        @pl.when(slab == 0)
        def _():
            for copy in edges:
                copy.wait()
            wide[0:SMOOTH] = halo[0].astype(F32)
            wide[lat + SMOOTH :] = halo[1].astype(F32)

        for half in range(SLAB // 8):
            some = pl.ds(pl.multiple_of(slab * SLAB + half * 8, 8), 8)
            value = halves_of(wide, slice(None), some)
            for step in range(SMOOTH):
                rows = slice(step, lat + 2 * SMOOTH - step)
                scaled = [w * v for w, v in zip(halves_of(kwide, rows, slice(None)), value)]
                around = beside(*[v[1:-1] for v in scaled])
                inner = slice(step + 1, lat + 2 * SMOOTH - 1 - step)
                value = [
                    v[1:-1] * k + (g[:-2] + g[2:] + a)
                    for v, k, g, a in zip(value, halves_of(keep, inner, slice(None)), scaled, around)
                ]
            for side in range(2):
                for row in range(lat):
                    flat[side, pl.ds(half * 8 * lat + row, 8, stride=lat), :] = value[side][row]
        some = pl.ds(pl.multiple_of(slab * SLAB * lat, SLAB * lat), SLAB * lat)
        for side in range(2):
            lanes = slice(side * BLK, (side + 1) * BLK)
            out_ref[some, lanes] = flat[side] + probes_ref[some, lanes].astype(F32)
        return carry

    lax.fori_loop(0, slabs, one_slab, 0)

    def finish(k):
        for_relay(k).wait_send()
        for_twin(k).wait_send()
        across(k).wait_send()

    each(finish)


def scatter_and_smooth(n_src, plan, weighted, blocks, probes, kext):
    lat = kext.shape[0] - 16
    loc, lon = probes.shape[0] // lat, probes.shape[1]
    pieces = loc // SLAB + 2
    landing = VMEM((lat, loc, lon), BF16)
    dma = pltpu.SemaphoreType.DMA
    return pl.pallas_call(
        functools.partial(back_kernel, n_src),
        out_shape=jax.ShapeDtypeStruct(probes.shape, F32),
        in_specs=[pl.BlockSpec(memory_space=pltpu.SMEM)] + [pl.BlockSpec(memory_space=VMEM)] * 4,
        out_specs=pl.BlockSpec(memory_space=VMEM),
        scratch_shapes=[
            VMEM((min(TOGETHER, blocks.shape[0]), 2 * loc, BLK), F32),
            VMEM((blocks.shape[0], 2 * loc, BLK), BF16),
            VMEM((lat, 2 * loc, lon), BF16),
            VMEM((lat, 2 * loc, lon), BF16),
            landing,
            landing,
            landing,
            landing,
            VMEM((2, SMOOTH, loc, lon), BF16),
            VMEM((2, SMOOTH, loc, lon), BF16),
            VMEM((lat + 2 * SMOOTH, loc, lon), F32),
            VMEM((lat + 2 * SMOOTH, 8, lon), F32),
            VMEM((lat + 2 * SMOOTH, 8, lon), F32),
            VMEM((lon // BLK, SLAB * lat, BLK), F32),
            dma((2,)),
            dma((2,)),
            dma((3, pieces)),
            dma((3, pieces)),
        ],
        compiler_params=pltpu.CompilerParams(
            collective_id=2, has_side_effects=True, vmem_limit_bytes=VMEM_LIMIT
        ),
        name="scatter_and_smooth",
    )(plan, weighted, blocks, probes, kext)


def per_device(probes, kappa, footprint, block_source, block_receptor, block_count, obs_weight):
    n_src, n_rcv = lax.axis_size("src"), lax.axis_size("rcv")
    loc, lat, lon = probes.shape
    flat = probes.reshape(loc * lat, lon)
    blocks = footprint.reshape(footprint.shape[2:])
    slots = blocks.shape[0]
    sources, receptors = block_source.reshape(1, slots), block_receptor.reshape(1, slots)
    unused = lax.broadcasted_iota(jnp.int32, (1, slots), 1) >= block_count.reshape(1, 1)
    packed = sources + SLOT_BASE * (receptors + SLOT_BASE * unused.astype(jnp.int32))
    field, kext, plan = smooth_and_gather(n_src, n_rcv, flat, kappa, packed)
    weighted = reduce_and_weigh(n_src, plan, field, blocks, obs_weight.reshape(RB_LOC, BLK))
    weighted = weighted.reshape(2 * RB_LOC, loc * n_rcv // 2, BLK)
    out = scatter_and_smooth(n_src, plan, weighted, blocks, flat, kext)
    return out.reshape(loc, lat, lon)


def solution(mesh):
    placed = (
        P("rcv", "src", None),
        P("src", None),
        P("src", "rcv", None, None, None),
        P("src", "rcv", None),
        P("src", "rcv", None),
        P("src", "rcv"),
        P("rcv"),
    )
    return jax.shard_map(
        per_device, mesh=mesh, in_specs=placed, out_specs=P("rcv", "src", None), check_vma=False
    )
```

```python
import functools

import jax
import jax.numpy as jnp
from jax import lax
from jax.experimental import pallas as pl
from jax.experimental.pallas import tpu as pltpu
from jax.sharding import PartitionSpec as P

BLK = 128
RB_LOC = 16
SMOOTH = 4
PLANE = 8
SLAB = 16
SLOT_BASE = 64
TOGETHER = 32
MESH = pl.DeviceIdType.MESH
VMEM = pltpu.VMEM
F32 = jnp.float32
BF16 = jnp.bfloat16
VMEM_LIMIT = 44 * 1024 * 1024


def announce(devices):
    barrier = pltpu.get_barrier_semaphore()
    for device in devices:
        pl.semaphore_signal(barrier, inc=1, device_id=device, device_id_type=MESH)


def await_all(devices):
    pl.semaphore_wait(pltpu.get_barrier_semaphore(), len(devices))


def remote(src, dst, send_sem, recv_sem, device):
    return pltpu.make_async_remote_copy(
        src_ref=src,
        dst_ref=dst,
        send_sem=send_sem,
        recv_sem=recv_sem,
        device_id=device,
        device_id_type=MESH,
    )


def neighbours(n_src):
    me = lax.axis_index("src")
    group = lax.axis_index("rcv")
    high, core = group // 2, group % 2
    before = (lax.rem(me + n_src - 1, n_src), group)
    after = (lax.rem(me + 1, n_src), group)
    twin = high * 2 + (1 - core)
    opposite = (1 - high) * 2 + core
    return me, group, before, after, twin, opposite


def beside(west_half, east_half):
    axis = west_half.ndim - 1
    lane = lax.broadcasted_iota(jnp.int32, west_half.shape, axis)
    first, last = lane == 0, lane == BLK - 1
    up_w, up_e = pltpu.roll(west_half, 1, axis), pltpu.roll(east_half, 1, axis)
    down_w, down_e = pltpu.roll(west_half, BLK - 1, axis), pltpu.roll(east_half, BLK - 1, axis)
    return (
        jnp.where(first, 0.0, up_w) + jnp.where(last, down_e, down_w),
        jnp.where(first, up_w, up_e) + jnp.where(last, 0.0, down_e),
    )


def halves_of(ref, rows, *middle):
    return [ref[(rows, *middle, slice(side * BLK, (side + 1) * BLK))] for side in range(2)]


def spread_kappa(n_src, me, kext_ref, kwide, keep, rows):
    for row in rows:
        value = kext_ref[8 - SMOOTH + row : 8 - SMOOTH + row + 1, :]
        if row < SMOOTH:
            value = jnp.where(me == 0, 0.0, value)
        if row >= kwide.shape[0] - SMOOTH:
            value = jnp.where(me == n_src - 1, 0.0, value)
        wide = jnp.broadcast_to(value, kwide.shape[1:])
        kwide[row] = wide
        keep[row] = 1.0 - 4.0 * wide


def make_plan(lower_pieces, packed, plan_ref):
    slots, lanes = packed.shape[1], plan_ref.shape[1]
    sources, receptors = packed % SLOT_BASE, packed // SLOT_BASE % SLOT_BASE
    row_of = lax.broadcasted_iota(jnp.int32, (slots, slots), 0)
    lane_of = lax.broadcasted_iota(jnp.int32, (slots, slots), 1)
    place = lax.broadcasted_iota(jnp.int32, (slots, lanes), 1)
    slot = lax.broadcasted_iota(jnp.int32, (1, slots), 1)
    used = packed < SLOT_BASE * SLOT_BASE

    def column(row):
        return jnp.sum(jnp.where(row_of == lane_of, row, 0.0), axis=1, keepdims=True)

    first_lane = lax.broadcasted_iota(jnp.int32, (1, lanes), 1) == 0
    for base, owner, other in ((0, receptors, sources), (8, sources, receptors)):
        key = jnp.where(used, owner * 256 + slot, 64 * 256 + slot).astype(F32)
        tall = column(key)
        rank = jnp.sum(jnp.where(key < tall, 1.0, 0.0), axis=1, keepdims=True)
        here = rank.astype(jnp.int32) == place

        def ordered(values):
            return jnp.sum(jnp.where(here, values, 0.0), axis=0, keepdims=True).astype(jnp.int32)

        keys = ordered(tall)
        block = keys // 256
        ends = jnp.sum(
            jnp.where(tall < ((place + 1) * 256).astype(F32), 1.0, 0.0), axis=0, keepdims=True
        ).astype(jnp.int32)
        start = jnp.where(first_lane, 0, pltpu.roll(ends, 1, 1))
        same = (block == pltpu.roll(block, 1, 1)) & jnp.logical_not(first_lane)
        plan_ref[base : base + 1, :] = keys - block * 256
        plan_ref[base + 1 : base + 2, :] = ordered(column(other.astype(F32)))
        plan_ref[base + 2 : base + 3, :] = same.astype(jnp.int32)
        plan_ref[base + 3 : base + 4, :] = jnp.maximum(ends - 1, 0)
        if base:
            lower = other % 2 * (lower_pieces * PLANE) + other // 2
            plan_ref[base + 5 : base + 6, :] = ordered(column(lower.astype(F32)))
        plan_ref[base + 4 : base + 5, :] = (ends > start).astype(jnp.int32)


def smooth_kernel(
    n_src, probes_ref, kappa_ref, slots_ref, field_ref, kext_ref, plan_ref, flat, halo, edge, wide, kwide, keep,
    edge_send, edge_recv, send, recv,
):
    me, group, before, after, twin, opposite = neighbours(n_src)
    lat, lon = kappa_ref.shape
    loc = probes_ref.shape[0] // lat
    slabs = loc // SLAB
    partners = [before, after, (me, twin), (me, opposite)]
    announce(partners)

    top, bottom = range(SMOOTH), range(lat - SMOOTH, lat)
    for side in range(lon // BLK):
        flat[side] = probes_ref[:, side * BLK : (side + 1) * BLK].astype(F32)

    def of_row(row):
        return jnp.concatenate([flat[side, pl.ds(row, loc, stride=lat), :] for side in range(lon // BLK)], axis=1)

    for side, rows in enumerate((top, bottom)):
        for place, row in enumerate(rows):
            value = of_row(row)
            wide[SMOOTH + row] = value
            edge[side, place] = value.astype(BF16)
    for row in range(SMOOTH, lat - SMOOTH):
        wide[SMOOTH + row] = of_row(row)
    kext_ref[8 : lat + 8, :] = kappa_ref[...]
    spread_kappa(n_src, me, kext_ref, kwide, keep, range(SMOOTH, lat + SMOOTH))
    edges = [
        remote(edge.at[1], halo.at[0], edge_send.at[0], edge_recv.at[0], after),
        remote(edge.at[0], halo.at[1], edge_send.at[1], edge_recv.at[1], before),
        remote(kappa_ref.at[pl.ds(lat - 8, 8)], kext_ref.at[pl.ds(0, 8)], edge_send.at[2], edge_recv.at[2], after),
        remote(kappa_ref.at[pl.ds(0, 8)], kext_ref.at[pl.ds(lat + 8, 8)], edge_send.at[3], edge_recv.at[3], before),
    ]

    parts = ((SMOOTH, lat - SMOOTH), (0, SMOOTH), (lat - SMOOTH, lat))

    core = group % 2
    own, far = 2 + core, core

    def place(owner, part, slab):
        first, last = parts[part]
        return field_ref.at[
            pl.ds(2 * first, 2 * (last - first)), pl.ds(pl.multiple_of(owner * loc + slab * SLAB, SLAB), SLAB), :
        ]

    def to_twin(part, slab):
        where = place(own, part, slab)
        return remote(where, where, send.at[0, part, slab], recv.at[0, part, slab], (me, twin))

    def to_opposite(part, slab):
        there = place(far, part, slab)
        return remote(place(own, part, slab), there, send.at[1, part, slab], recv.at[1, part, slab], (me, opposite))

    def relay(part, slab):
        where = place(far, part, slab)
        return remote(where, where, send.at[2, part, slab], recv.at[2, part, slab], (me, twin))

    def smooth_part(part, slab):
        first, last = parts[part]
        groups = []
        for half in range(SLAB // 8):
            some = pl.ds(pl.multiple_of(slab * SLAB + half * 8, 8), 8)
            value = halves_of(wide, slice(first, last + 2 * SMOOTH), some)
            for step in range(SMOOTH):
                rows = slice(first + step + 1, last + 2 * SMOOTH - 1 - step)
                centre = [v[1:-1] for v in value]
                around = beside(*centre)
                value = [
                    c * k + w * (v[:-2] + v[2:] + a)
                    for c, k, w, v, a in zip(
                        centre, halves_of(keep, rows, slice(None)), halves_of(kwide, rows, slice(None)), value, around
                    )
                ]
            groups.append(value)
        mine = pl.ds(pl.multiple_of(own * loc + slab * SLAB, SLAB), SLAB)
        for side in range(2):
            smoothed = jnp.concatenate([g[side] for g in groups], axis=1).astype(BF16)
            for row in range(first, last):
                field_ref[2 * row + side, mine, :] = smoothed[row - first]

    def post(part, slab):
        to_opposite(part, slab).start()
        to_twin(part, slab).start()

    def inner(slab, carry):
        smooth_part(0, slab)
        post(0, slab)
        return carry

    def outer(slab, carry):
        for part in (1, 2):
            smooth_part(part, slab)
            post(part, slab)
        return carry

    smooth_part(0, 0)
    await_all(partners)
    post(0, 0)
    for copy in edges:
        copy.start()
    lax.fori_loop(1, slabs, inner, 0)
    for copy in edges:
        copy.wait()
    wide[0:SMOOTH] = jnp.where(me == 0, 0.0, halo[0].astype(F32))
    wide[lat + SMOOTH :] = jnp.where(me == n_src - 1, 0.0, halo[1].astype(F32))
    spread_kappa(n_src, me, kext_ref, kwide, keep, [*range(SMOOTH), *range(lat + SMOOTH, lat + 2 * SMOOTH)])
    lax.fori_loop(0, slabs, outer, 0)
    make_plan(n_src // PLANE // 4, slots_ref[...], plan_ref)

    def pass_on(parts_here):
        def one(slab, carry):
            for part in parts_here:
                to_opposite(part, slab).wait_recv()
                relay(part, slab).start()
            return carry

        lax.fori_loop(0, slabs, one, 0)

    pass_on((0,))
    pass_on((1, 2))

    def finish(slab, carry):
        for part in range(3):
            to_opposite(part, slab).wait_send()
            to_twin(part, slab).wait()
            relay(part, slab).wait()
        return carry

    lax.fori_loop(0, slabs, finish, 0)


def smooth_and_gather(n_src, n_rcv, probes, kappa, packed):
    lat, lon = kappa.shape
    loc = probes.shape[0] // lat
    slabs = loc // SLAB
    dma = pltpu.SemaphoreType.DMA
    return pl.pallas_call(
        functools.partial(smooth_kernel, n_src),
        out_shape=(
            jax.ShapeDtypeStruct((lat * lon // BLK, loc * n_rcv, BLK), BF16),
            jax.ShapeDtypeStruct((lat + 16, lon), F32),
            jax.ShapeDtypeStruct((16, 256), jnp.int32),
        ),
        in_specs=[pl.BlockSpec(memory_space=VMEM)] * 3,
        out_specs=(pl.BlockSpec(memory_space=VMEM),) * 3,
        scratch_shapes=[
            VMEM((lon // BLK, loc * lat, BLK), F32),
            VMEM((2, SMOOTH, loc, lon), BF16),
            VMEM((2, SMOOTH, loc, lon), BF16),
            VMEM((lat + 2 * SMOOTH, loc, lon), F32),
            VMEM((lat + 2 * SMOOTH, 8, lon), F32),
            VMEM((lat + 2 * SMOOTH, 8, lon), F32),
            dma((4,)),
            dma((4,)),
            dma((3, 3, slabs)),
            dma((3, 3, slabs)),
        ],
        compiler_params=pltpu.CompilerParams(
            collective_id=0, has_side_effects=True, vmem_limit_bytes=VMEM_LIMIT
        ),
        cost_estimate=pl.CostEstimate(flops=20_000_000_000, bytes_accessed=64_000_000, transcendentals=0),
        name="smooth_and_gather",
    )(probes, kappa, packed)


def running_sums(plan_ref, base, slots, product, products, sums):
    together = products.shape[0]

    def several(turn, total):
        for step in range(together):
            k = turn * together + step
            products[step] = product(k)
        for step in range(together):
            k = turn * together + step
            total = products[step] + total * plan_ref[base + 2, k].astype(F32)
            sums[k] = total.astype(BF16)
        return total

    lax.fori_loop(0, slots // together, several, jnp.zeros(sums.shape[1:], F32))


def block_sum(plan_ref, base, block, sums):
    value = sums[plan_ref[base + 3, block]]
    return (value.astype(F32) * plan_ref[base + 4, block].astype(F32)).astype(BF16)


def reduction(planes, plan_ref, field_ref, blocks_ref, weight_ref, products, sums, mine_ref, first, part, second, line, mixed, last, upper, lower, *sems):
    me = lax.axis_index("src")
    group = lax.axis_index("rcv")
    plane, spot = me // PLANE, me % PLANE
    pairs = iter(sems)
    a_plane, a_line, c_line, c_plane, ga_line, ga_plane, gc_plane, gc_line = zip(pairs, pairs)
    rows = mine_ref.shape[2]
    cut = rows * 3 // 4
    upper_rows, lower_rows = pl.ds(0, cut), pl.ds(cut, rows - cut)
    half_probes = field_ref.shape[1] // 2
    groups = 2
    size = planes // groups
    in_planes = range(1, PLANE)
    in_lines = range(1, planes)

    def spot_of(distance):
        return lax.rem(spot + distance, PLANE)

    def plane_of(distance):
        return lax.rem(plane + distance, planes)

    def in_plane(distance):
        return (plane * PLANE + spot_of(distance), group)

    def in_line(distance):
        return (plane_of(distance) * PLANE + spot, group)

    def copy(pair, index, src, dst, device):
        return remote(src, dst, pair[0].at[index], pair[1].at[index], device)

    def some(g):
        return pl.ds(g * size, size)

    def scatter_a_plane(d, g):
        return copy(
            a_plane, (d - 1, g), mine_ref.at[spot_of(d), some(g), upper_rows], first.at[d - 1, some(g)], in_plane(d)
        )

    def scatter_a_line(piece):
        d = lax.rem(piece + planes - plane, planes)
        return copy(a_line, (d - 1,), part.at[piece], second.at[d - 1], (piece * PLANE + spot, group))

    def scatter_c_line(d):
        return copy(c_line, (d - 1,), mine_ref.at[:, plane_of(d), lower_rows], line.at[d - 1], in_line(d))

    def scatter_c_plane(d):
        return copy(c_plane, (d - 1,), mixed.at[spot_of(d)], last.at[d - 1], in_plane(d))

    own_index = plane % size

    def gather_a_line(d, g):
        where = upper[g].at[spot * size + own_index]
        return copy(ga_line, (d - 1,), where, where, in_line(d))

    def gather_a_plane(d, g):
        where = upper[g].at[pl.ds(spot * size, size)]
        return copy(ga_plane, (d - 1, g), where, where, in_plane(d))

    def gather_c_plane(d, g):
        where = lower[g].at[own_index * PLANE + spot]
        return copy(gc_plane, (d - 1,), where, where, in_plane(d))

    def gather_c_line(d, g):
        where = lower[g].at[pl.ds(own_index * PLANE, PLANE)]
        return copy(gc_line, (d - 1,), where, where, in_line(d))

    def sender(piece):
        return lax.rem(plane + planes - piece, planes)

    def on_own_group(work):
        for g in range(groups):
            pl.when(plane // size == g)(functools.partial(work, g))

    def others_of(g, work):
        for index in range(size):
            piece = g * size + index
            pl.when(piece != plane)(functools.partial(work, piece))

    weight = weight_ref[pl.ds(spot * (RB_LOC // PLANE) + own_index // (half_probes // rows), 1), :]

    def product(k):
        return lax.dot_general(
            field_ref[plan_ref[1, k]], blocks_ref[plan_ref[0, k]], (((1,), (1,)), ((), ())), preferred_element_type=F32
        )

    def forward():
        running_sums(plan_ref, 0, blocks_ref.shape[0], product, products, sums)
        for block in range(RB_LOC):
            value = block_sum(plan_ref, 0, block, sums)
            for start in range(0, 2 * half_probes, rows):
                half, at = divmod(start, half_probes)
                piece = half * size + (block % 2 * half_probes + at) // rows
                mine_ref[block // 2, piece] = value[start : start + rows]

    def begin_group(g):
        for d in in_planes:
            scatter_a_plane(d, g).start()

    def plane_sums(g):
        for d in in_planes:
            scatter_a_plane(d, g).wait_recv()
        for index in range(size):
            piece = g * size + index
            total = mine_ref[spot, piece, 0:cut].astype(F32)
            for other in range(PLANE - 1):
                total = total + first[other, piece].astype(F32)
            part[piece] = total.astype(BF16)

            @pl.when(piece != plane)
            def _():
                scatter_a_line(piece).start()

    def own_rows(g):
        for d in in_lines:
            copy(a_line, (d - 1,), part.at[plane], second.at[d - 1], in_line(d)).wait_recv()
        total = part[plane].astype(F32)
        for other in range(planes - 1):
            total = total + second[other].astype(F32)
        upper[g][spot * size + own_index] = (total * weight).astype(BF16)
        for d in in_lines:
            gather_a_line(d, g).start()

    def spread_group(g):
        def landed(piece):
            where = upper[g].at[spot * size + piece % size]
            copy(ga_line, (sender(piece) - 1,), where, where, in_line(1)).wait_recv()

        others_of(g, landed)
        for d in in_planes:
            gather_a_plane(d, g).start()

    def line_sums():
        for d in in_lines:
            scatter_c_line(d).wait_recv()
        for d in [*in_planes, 0]:
            piece = spot_of(d)
            total = mine_ref[piece, plane, cut:rows].astype(F32)
            for other in range(planes - 1):
                total = total + line[other, piece].astype(F32)
            mixed[piece] = total.astype(BF16)
            if d:
                scatter_c_plane(d).start()

    def own_lower_rows(g):
        for d in in_planes:
            scatter_c_plane(d).wait_recv()
        total = mixed[spot].astype(F32)
        for other in range(PLANE - 1):
            total = total + last[other].astype(F32)
        lower[g][own_index * PLANE + spot] = (total * weight).astype(BF16)
        for d in in_planes:
            gather_c_plane(d, g).start()

    def spread_lower_rows(g):
        for d in in_planes:
            gather_c_plane(d, g).wait_recv()
        for d in in_lines:
            gather_c_line(d, g).start()

    def run():
        begin_group(0)
        for d in in_lines:
            scatter_c_line(d).start()
        begin_group(1)
        plane_sums(0)
        line_sums()
        plane_sums(1)
        on_own_group(own_lower_rows)
        on_own_group(own_rows)
        spread_group(0)
        on_own_group(spread_lower_rows)
        spread_group(1)

    def ready(g):
        for d in in_planes:
            gather_a_plane(d, g).wait_recv()

        def landed(piece):
            where = lower[g].at[pl.ds(piece % size * PLANE, PLANE)]
            copy(gc_line, (sender(piece) - 1,), where, where, in_line(1)).wait_recv()

        others_of(g, landed)

    def finish():
        for d in in_planes:
            for g in range(groups):
                gather_a_plane(d, g).wait_send()
                scatter_a_plane(d, g).wait_send()
            scatter_c_plane(d).wait_send()
            gather_c_plane(d, 0).wait_send()
        for d in in_lines:
            gather_c_line(d, 0).wait_send()
            gather_a_line(d, 0).wait_send()
            scatter_c_line(d).wait_send()
            copy(a_line, (d - 1,), part.at[plane], second.at[d - 1], in_line(d)).wait_send()

    partners = [in_plane(d) for d in in_planes] + [in_line(d) for d in in_lines]
    return partners, forward, run, ready, finish


def hessian_kernel(n_src, plan_ref, field_ref, blocks_ref, weight_ref, probes_ref, kext_ref, out_ref, *scratch):
    (
        products, sums, back_products, back_sums, mine, first, part, second, line, mixed, last,
        upper_far, upper_near, lower_far, lower_near, terms_far, terms_near, pair, relayed, joined, far,
        edge, halo, wide, kwide, keep, flat, edge_send, edge_recv, send, recv, *sems,
    ) = scratch
    upper, lower = (upper_far, upper_near), (lower_far, lower_near)
    reduce_partners, forward, run, ready, finish_reduction = reduction(
        n_src // PLANE, plan_ref, field_ref, blocks_ref, weight_ref, products, sums, mine, first, part, second, line, mixed,
        last, upper, lower, *sems,
    )
    me, group, before, after, twin, opposite = neighbours(n_src)
    lat = kext_ref.shape[0] - 16
    loc, lon = probes_ref.shape[0] // lat, probes_ref.shape[1]
    slabs = loc // SLAB
    core = group % 2
    partners = [before, after, (me, twin), (me, opposite), *reduce_partners]
    announce(partners)
    forward()
    await_all(partners)
    run()

    def view(ref, k, offset=0):
        if isinstance(k, int) and k < 2:
            return ref.at[pl.ds(k * (lat - SMOOTH), SMOOTH), pl.ds(pl.multiple_of(offset, loc), loc), :]
        start = pl.multiple_of(offset + (k - 2) * SLAB, SLAB)
        return ref.at[pl.ds(SMOOTH, lat - 2 * SMOOTH), pl.ds(start, SLAB), :]

    def term(terms, core_of, k):
        return view(terms, k, core_of * loc)

    def adjoint(half, terms):
        pieces = upper_far.shape[0] // RB_LOC

        def product(k):
            receptor, low = plan_ref[9, k], plan_ref[13, k]
            rows = []
            for piece in range(pieces):
                rows += [upper[half][receptor * pieces + piece], lower[half][low + piece * PLANE]]
            return jnp.dot(jnp.concatenate(rows, axis=0), blocks_ref[plan_ref[8, k]], preferred_element_type=F32)

        running_sums(plan_ref, 8, blocks_ref.shape[0], product, back_products, back_sums)
        for row in range(lat):
            for side in range(2):
                terms[row, :, side * BLK : (side + 1) * BLK] = block_sum(plan_ref, 8, 2 * row + side, back_sums)

    def for_relay(k):
        return remote(term(terms_far, 1 - core, k), view(relayed, k), send.at[0, k], recv.at[0, k], (me, twin))

    def for_twin(k):
        return remote(term(terms_near, 1 - core, k), view(pair, k), send.at[1, k], recv.at[1, k], (me, twin))

    def across(k):
        return remote(view(joined, k), view(far, k), send.at[2, k], recv.at[2, k], (me, opposite))

    def each(work):
        work(0)
        work(1)
        lax.fori_loop(2, slabs + 2, lambda k, carry: (work(k), carry)[1], 0)

    def join(k):
        for_relay(k).wait_recv()
        view(joined, k)[...] = (
            term(terms_far, core, k)[...].astype(F32) + view(relayed, k)[...].astype(F32)
        ).astype(BF16)
        across(k).start()

    def total(k):
        for_twin(k).wait_recv()
        across(k).wait_recv()
        return term(terms_near, core, k)[...].astype(F32) + view(pair, k)[...].astype(F32) + view(far, k)[...].astype(F32)

    edges = [
        remote(edge.at[0], halo.at[1], edge_send.at[0], edge_recv.at[0], before),
        remote(edge.at[1], halo.at[0], edge_send.at[1], edge_recv.at[1], after),
    ]
    ready(0)
    adjoint(0, terms_far)
    each(lambda k: for_relay(k).start())
    spread_kappa(n_src, me, kext_ref, kwide, keep, range(lat + 2 * SMOOTH))
    each(join)
    ready(1)
    adjoint(1, terms_near)
    each(lambda k: for_twin(k).start())
    for k, row in ((0, SMOOTH), (1, lat)):
        rows = total(k)
        wide[row : row + SMOOTH] = rows
        edge[k] = rows.astype(BF16)
        edges[k].start()

    def one_slab(slab, carry):
        probes_here = pl.ds(pl.multiple_of(slab * SLAB, SLAB), SLAB)
        wide[2 * SMOOTH : lat, probes_here, :] = total(slab + 2)

        @pl.when(slab == 0)
        def _():
            for copy in edges:
                copy.wait()
            wide[0:SMOOTH] = halo[0].astype(F32)
            wide[lat + SMOOTH :] = halo[1].astype(F32)

        for half in range(SLAB // 8):
            some = pl.ds(pl.multiple_of(slab * SLAB + half * 8, 8), 8)
            value = halves_of(wide, slice(None), some)
            for step in range(SMOOTH):
                rows = slice(step, lat + 2 * SMOOTH - step)
                scaled = [w * v for w, v in zip(halves_of(kwide, rows, slice(None)), value)]
                around = beside(*[v[1:-1] for v in scaled])
                inner = slice(step + 1, lat + 2 * SMOOTH - 1 - step)
                value = [
                    v[1:-1] * k + (g[:-2] + g[2:] + a)
                    for v, k, g, a in zip(value, halves_of(keep, inner, slice(None)), scaled, around)
                ]
            for side in range(2):
                for row in range(lat):
                    flat[side, pl.ds(half * 8 * lat + row, 8, stride=lat), :] = value[side][row]
        some = pl.ds(pl.multiple_of(slab * SLAB * lat, SLAB * lat), SLAB * lat)
        for side in range(2):
            lanes = slice(side * BLK, (side + 1) * BLK)
            out_ref[some, lanes] = flat[side] + probes_ref[some, lanes].astype(F32)
        return carry

    lax.fori_loop(0, slabs, one_slab, 0)

    def finish(k):
        for_relay(k).wait_send()
        for_twin(k).wait_send()
        across(k).wait_send()

    each(finish)
    finish_reduction()


def hessian_part(n_src, plan, field, blocks, weight, probes, kext):
    lat = kext.shape[0] - 16
    loc, lon = probes.shape[0] // lat, probes.shape[1]
    total, slots = field.shape[1], blocks.shape[0]
    half = total // 2
    planes = n_src // PLANE
    rows = RB_LOC * total // (PLANE * planes)
    cut = rows * 3 // 4
    rest = rows - cut
    pieces = loc // SLAB + 2
    together = min(TOGETHER, slots)
    dma = pltpu.SemaphoreType.DMA
    per_spot, per_plane, parts = (PLANE - 1,), (planes - 1,), (PLANE - 1, 2)
    counts = (parts, per_plane, per_plane, per_spot, per_plane, parts, per_spot, per_plane)
    held = [
        (slots, total, BLK),
        (PLANE, planes, rows, BLK),
        (PLANE - 1, planes, cut, BLK),
        (planes, cut, BLK),
        (planes - 1, cut, BLK),
        (planes - 1, PLANE, rest, BLK),
        (PLANE, rest, BLK),
        (PLANE - 1, rest, BLK),
        *[(PLANE * planes // 2, cut, BLK)] * 2,
        *[(PLANE * planes // 2, rest, BLK)] * 2,
        *[(lat, half, lon)] * 2,
        *[(lat, loc, lon)] * 4,
        *[(2, SMOOTH, loc, lon)] * 2,
    ]
    return pl.pallas_call(
        functools.partial(hessian_kernel, n_src),
        out_shape=jax.ShapeDtypeStruct(probes.shape, F32),
        in_specs=[pl.BlockSpec(memory_space=pltpu.SMEM)] + [pl.BlockSpec(memory_space=VMEM)] * 5,
        out_specs=pl.BlockSpec(memory_space=VMEM),
        scratch_shapes=[
            VMEM((together, total, BLK), F32),
            VMEM(held[0], BF16),
            VMEM((together, half, BLK), F32),
            VMEM((slots, half, BLK), BF16),
            *[VMEM(shape, BF16) for shape in held[1:]],
            VMEM((lat + 2 * SMOOTH, loc, lon), F32),
            VMEM((lat + 2 * SMOOTH, 8, lon), F32),
            VMEM((lat + 2 * SMOOTH, 8, lon), F32),
            VMEM((lon // BLK, SLAB * lat, BLK), F32),
            dma((2,)),
            dma((2,)),
            dma((3, pieces)),
            dma((3, pieces)),
        ]
        + [dma(count) for count in counts for _ in range(2)],
        compiler_params=pltpu.CompilerParams(
            collective_id=1, has_side_effects=True, vmem_limit_bytes=VMEM_LIMIT
        ),
        name="hessian_part",
    )(plan, field, blocks, weight, probes, kext)


def per_device(probes, kappa, footprint, block_source, block_receptor, block_count, obs_weight):
    n_src, n_rcv = lax.axis_size("src"), lax.axis_size("rcv")
    loc, lat, lon = probes.shape
    flat = probes.reshape(loc * lat, lon)
    blocks = footprint.reshape(footprint.shape[2:])
    slots = blocks.shape[0]
    sources, receptors = block_source.reshape(1, slots), block_receptor.reshape(1, slots)
    unused = lax.broadcasted_iota(jnp.int32, (1, slots), 1) >= block_count.reshape(1, 1)
    packed = sources + SLOT_BASE * (receptors + SLOT_BASE * unused.astype(jnp.int32))
    field, kext, plan = smooth_and_gather(n_src, n_rcv, flat, kappa, packed)
    out = hessian_part(n_src, plan, field, blocks, obs_weight.reshape(RB_LOC, BLK), flat, kext)
    return out.reshape(loc, lat, lon)


def solution(mesh):
    placed = (
        P("rcv", "src", None),
        P("src", None),
        P("src", "rcv", None, None, None),
        P("src", "rcv", None),
        P("src", "rcv", None),
        P("src", "rcv"),
        P("rcv"),
    )
    return jax.shard_map(
        per_device, mesh=mesh, in_specs=placed, out_specs=P("rcv", "src", None), check_vma=False
    )
```

```python
import functools

import jax
import jax.numpy as jnp
from jax import lax
from jax.experimental import pallas as pl
from jax.experimental.pallas import tpu as pltpu
from jax.sharding import PartitionSpec as P

BLK = 128
RB_LOC = 16
SMOOTH = 4
PLANE = 8
SLAB = 16
SLOT_BASE = 64
TOGETHER = 64
MESH = pl.DeviceIdType.MESH
VMEM = pltpu.VMEM
F32 = jnp.float32
BF16 = jnp.bfloat16
VMEM_LIMIT = 40 * 1024 * 1024


def announce(devices):
    barrier = pltpu.get_barrier_semaphore()
    for device in devices:
        pl.semaphore_signal(barrier, inc=1, device_id=device, device_id_type=MESH)


def await_all(devices):
    pl.semaphore_wait(pltpu.get_barrier_semaphore(), len(devices))


def remote(src, dst, send_sem, recv_sem, device):
    return pltpu.make_async_remote_copy(
        src_ref=src,
        dst_ref=dst,
        send_sem=send_sem,
        recv_sem=recv_sem,
        device_id=device,
        device_id_type=MESH,
    )


def neighbours(n_src):
    me = lax.axis_index("src")
    group = lax.axis_index("rcv")
    high, core = group // 2, group % 2
    before = (lax.rem(me + n_src - 1, n_src), group)
    after = (lax.rem(me + 1, n_src), group)
    twin = high * 2 + (1 - core)
    opposite = (1 - high) * 2 + core
    return me, group, before, after, twin, opposite


def beside(west_half, east_half):
    axis = west_half.ndim - 1
    lane = lax.broadcasted_iota(jnp.int32, west_half.shape, axis)
    first, last = lane == 0, lane == BLK - 1
    up_w, up_e = pltpu.roll(west_half, 1, axis), pltpu.roll(east_half, 1, axis)
    down_w, down_e = pltpu.roll(west_half, BLK - 1, axis), pltpu.roll(east_half, BLK - 1, axis)
    return (
        jnp.where(first, 0.0, up_w) + jnp.where(last, down_e, down_w),
        jnp.where(first, up_w, up_e) + jnp.where(last, 0.0, down_e),
    )


def halves_of(ref, rows, *middle):
    return [ref[(rows, *middle, slice(side * BLK, (side + 1) * BLK))] for side in range(2)]


def spread_kappa(n_src, me, kext_ref, kwide, keep, rows):
    for row in rows:
        value = kext_ref[8 - SMOOTH + row : 8 - SMOOTH + row + 1, :]
        if row < SMOOTH:
            value = jnp.where(me == 0, 0.0, value)
        if row >= kwide.shape[0] - SMOOTH:
            value = jnp.where(me == n_src - 1, 0.0, value)
        wide = jnp.broadcast_to(value, kwide.shape[1:])
        kwide[row] = wide
        keep[row] = 1.0 - 4.0 * wide


def make_plan(lower_pieces, packed, plan_ref):
    slots, lanes = packed.shape[1], plan_ref.shape[1]
    sources, receptors = packed % SLOT_BASE, packed // SLOT_BASE % SLOT_BASE
    row_of = lax.broadcasted_iota(jnp.int32, (slots, slots), 0)
    lane_of = lax.broadcasted_iota(jnp.int32, (slots, slots), 1)
    place = lax.broadcasted_iota(jnp.int32, (slots, lanes), 1)
    slot = lax.broadcasted_iota(jnp.int32, (1, slots), 1)
    used = packed < SLOT_BASE * SLOT_BASE

    def column(row):
        return jnp.sum(jnp.where(row_of == lane_of, row, 0.0), axis=1, keepdims=True)

    first_lane = lax.broadcasted_iota(jnp.int32, (1, lanes), 1) == 0
    for base, owner, other in ((0, receptors, sources), (8, sources, receptors)):
        key = jnp.where(used, owner * 256 + slot, 64 * 256 + slot).astype(F32)
        tall = column(key)
        rank = jnp.sum(jnp.where(key < tall, 1.0, 0.0), axis=1, keepdims=True)
        here = rank.astype(jnp.int32) == place

        def ordered(values):
            return jnp.sum(jnp.where(here, values, 0.0), axis=0, keepdims=True).astype(jnp.int32)

        keys = ordered(tall)
        block = keys // 256
        ends = jnp.sum(
            jnp.where(tall < ((place + 1) * 256).astype(F32), 1.0, 0.0), axis=0, keepdims=True
        ).astype(jnp.int32)
        start = jnp.where(first_lane, 0, pltpu.roll(ends, 1, 1))
        same = (block == pltpu.roll(block, 1, 1)) & jnp.logical_not(first_lane)
        plan_ref[base : base + 1, :] = keys - block * 256
        plan_ref[base + 1 : base + 2, :] = ordered(column(other.astype(F32)))
        plan_ref[base + 2 : base + 3, :] = same.astype(jnp.int32)
        plan_ref[base + 3 : base + 4, :] = jnp.maximum(ends - 1, 0)
        if base:
            lower = other % 2 * (lower_pieces * PLANE) + other // 2
            plan_ref[base + 5 : base + 6, :] = ordered(column(lower.astype(F32)))
        plan_ref[base + 4 : base + 5, :] = (ends > start).astype(jnp.int32)


def smooth_kernel(
    n_src, probes_ref, kappa_ref, slots_ref, field_ref, kext_ref, plan_ref, flat, halo, edge, wide, kwide, keep,
    edge_send, edge_recv, send, recv,
):
    me, group, before, after, twin, opposite = neighbours(n_src)
    lat, lon = kappa_ref.shape
    loc = probes_ref.shape[0] // lat
    slabs = loc // SLAB
    partners = [before, after, (me, twin), (me, opposite)]
    announce(partners)

    def prepare(slab):
        here = pl.ds(pl.multiple_of(slab * SLAB * lat, SLAB * lat), SLAB * lat)
        some = pl.ds(pl.multiple_of(slab * SLAB, SLAB), SLAB)
        for side in range(2):
            flat[side] = probes_ref[here, side * BLK : (side + 1) * BLK].astype(F32)
        for row in range(lat):
            value = jnp.concatenate([flat[side, pl.ds(row, SLAB, stride=lat), :] for side in range(2)], axis=1)
            wide[SMOOTH + row, some, :] = value
            if row < SMOOTH:
                edge[0, row, some, :] = value.astype(BF16)
            if row >= lat - SMOOTH:
                edge[1, row - lat + SMOOTH, some, :] = value.astype(BF16)

    kext_ref[8 : lat + 8, :] = kappa_ref[...]
    spread_kappa(n_src, me, kext_ref, kwide, keep, range(SMOOTH, lat + SMOOTH))
    edges = [
        remote(edge.at[1], halo.at[0], edge_send.at[0], edge_recv.at[0], after),
        remote(edge.at[0], halo.at[1], edge_send.at[1], edge_recv.at[1], before),
        remote(kappa_ref.at[pl.ds(lat - 8, 8)], kext_ref.at[pl.ds(0, 8)], edge_send.at[2], edge_recv.at[2], after),
        remote(kappa_ref.at[pl.ds(0, 8)], kext_ref.at[pl.ds(lat + 8, 8)], edge_send.at[3], edge_recv.at[3], before),
    ]

    parts = ((SMOOTH, lat - SMOOTH), (0, SMOOTH), (lat - SMOOTH, lat))

    core = group % 2
    own, far = 2 + core, core

    def place(owner, part, slab):
        first, last = parts[part]
        return field_ref.at[
            pl.ds(2 * first, 2 * (last - first)), pl.ds(pl.multiple_of(owner * loc + slab * SLAB, SLAB), SLAB), :
        ]

    def to_twin(part, slab):
        where = place(own, part, slab)
        return remote(where, where, send.at[0, part, slab], recv.at[0, part, slab], (me, twin))

    def to_opposite(part, slab):
        there = place(far, part, slab)
        return remote(place(own, part, slab), there, send.at[1, part, slab], recv.at[1, part, slab], (me, opposite))

    def relay(part, slab):
        where = place(far, part, slab)
        return remote(where, where, send.at[2, part, slab], recv.at[2, part, slab], (me, twin))

    def smooth_part(part, slab):
        first, last = parts[part]
        groups = []
        for half in range(SLAB // 8):
            some = pl.ds(pl.multiple_of(slab * SLAB + half * 8, 8), 8)
            value = halves_of(wide, slice(first, last + 2 * SMOOTH), some)
            for step in range(SMOOTH):
                rows = slice(first + step + 1, last + 2 * SMOOTH - 1 - step)
                centre = [v[1:-1] for v in value]
                around = beside(*centre)
                value = [
                    c * k + w * (v[:-2] + v[2:] + a)
                    for c, k, w, v, a in zip(
                        centre, halves_of(keep, rows, slice(None)), halves_of(kwide, rows, slice(None)), value, around
                    )
                ]
            groups.append(value)
        mine = pl.ds(pl.multiple_of(own * loc + slab * SLAB, SLAB), SLAB)
        for side in range(2):
            smoothed = jnp.concatenate([g[side] for g in groups], axis=1).astype(BF16)
            for row in range(first, last):
                field_ref[2 * row + side, mine, :] = smoothed[row - first]

    def post(part, slab):
        to_opposite(part, slab).start()
        to_twin(part, slab).start()

    def inner(slab, carry):
        smooth_part(0, slab)
        post(0, slab)
        return carry

    def outer(slab, carry):
        for part in (1, 2):
            smooth_part(part, slab)
            post(part, slab)
        return carry

    prepare(0)
    smooth_part(0, 0)
    await_all(partners)
    post(0, 0)
    lax.fori_loop(1, slabs, lambda slab, carry: (prepare(slab), carry)[1], 0)
    for copy in edges:
        copy.start()
    lax.fori_loop(1, slabs, inner, 0)
    for copy in edges:
        copy.wait()
    wide[0:SMOOTH] = jnp.where(me == 0, 0.0, halo[0].astype(F32))
    wide[lat + SMOOTH :] = jnp.where(me == n_src - 1, 0.0, halo[1].astype(F32))
    spread_kappa(n_src, me, kext_ref, kwide, keep, [*range(SMOOTH), *range(lat + SMOOTH, lat + 2 * SMOOTH)])
    lax.fori_loop(0, slabs, outer, 0)
    make_plan(n_src // PLANE // 4, slots_ref[...], plan_ref)

    def pass_on(parts_here):
        def one(slab, carry):
            for part in parts_here:
                to_opposite(part, slab).wait_recv()
                relay(part, slab).start()
            return carry

        lax.fori_loop(0, slabs, one, 0)

    pass_on((0,))
    pass_on((1, 2))

    def finish(slab, carry):
        for part in range(3):
            to_opposite(part, slab).wait_send()
            to_twin(part, slab).wait()
            relay(part, slab).wait()
        return carry

    lax.fori_loop(0, slabs, finish, 0)


def smooth_and_gather(n_src, n_rcv, probes, kappa, packed):
    lat, lon = kappa.shape
    loc = probes.shape[0] // lat
    slabs = loc // SLAB
    dma = pltpu.SemaphoreType.DMA
    return pl.pallas_call(
        functools.partial(smooth_kernel, n_src),
        out_shape=(
            jax.ShapeDtypeStruct((lat * lon // BLK, loc * n_rcv, BLK), BF16),
            jax.ShapeDtypeStruct((lat + 16, lon), F32),
            jax.ShapeDtypeStruct((16, 256), jnp.int32),
        ),
        in_specs=[pl.BlockSpec(memory_space=VMEM)] * 3,
        out_specs=(pl.BlockSpec(memory_space=VMEM),) * 3,
        scratch_shapes=[
            VMEM((lon // BLK, SLAB * lat, BLK), F32),
            VMEM((2, SMOOTH, loc, lon), BF16),
            VMEM((2, SMOOTH, loc, lon), BF16),
            VMEM((lat + 2 * SMOOTH, loc, lon), F32),
            VMEM((lat + 2 * SMOOTH, 8, lon), F32),
            VMEM((lat + 2 * SMOOTH, 8, lon), F32),
            dma((4,)),
            dma((4,)),
            dma((3, 3, slabs)),
            dma((3, 3, slabs)),
        ],
        compiler_params=pltpu.CompilerParams(
            collective_id=0, has_side_effects=True, vmem_limit_bytes=VMEM_LIMIT
        ),
        cost_estimate=pl.CostEstimate(flops=20_000_000_000, bytes_accessed=64_000_000, transcendentals=0),
        name="smooth_and_gather",
    )(probes, kappa, packed)


def running_sums(plan_ref, base, slots, product, products, sums):
    together = products.shape[0]

    def several(turn, total):
        for step in range(together):
            k = turn * together + step
            products[step] = product(k)
        for step in range(together):
            k = turn * together + step
            total = products[step] + total * plan_ref[base + 2, k].astype(F32)
            sums[k] = total.astype(BF16)
        return total

    lax.fori_loop(0, slots // together, several, jnp.zeros(sums.shape[1:], F32))


def block_sum(plan_ref, base, block, sums):
    value = sums[plan_ref[base + 3, block]]
    return (value.astype(F32) * plan_ref[base + 4, block].astype(F32)).astype(BF16)


def reduction(planes, plan_ref, field_ref, blocks_ref, weight_ref, products, sums, mine_ref, first, part, second, line, mixed, last, upper, lower, *sems):
    me = lax.axis_index("src")
    group = lax.axis_index("rcv")
    plane, spot = me // PLANE, me % PLANE
    pairs = iter(sems)
    a_plane, a_line, c_line, c_plane, ga_line, ga_plane, gc_plane, gc_line = zip(pairs, pairs)
    rows = mine_ref.shape[2]
    cut = rows * 3 // 4
    upper_rows, lower_rows = pl.ds(0, cut), pl.ds(cut, rows - cut)
    half_probes = field_ref.shape[1] // 2
    groups = 2
    size = planes // groups
    in_planes = range(1, PLANE)
    in_lines = range(1, planes)

    def spot_of(distance):
        return lax.rem(spot + distance, PLANE)

    def plane_of(distance):
        return lax.rem(plane + distance, planes)

    def in_plane(distance):
        return (plane * PLANE + spot_of(distance), group)

    def in_line(distance):
        return (plane_of(distance) * PLANE + spot, group)

    def copy(pair, index, src, dst, device):
        return remote(src, dst, pair[0].at[index], pair[1].at[index], device)

    def some(g):
        return pl.ds(g * size, size)

    def scatter_a_plane(d, g):
        return copy(
            a_plane, (d - 1, g), mine_ref.at[spot_of(d), some(g), upper_rows], first.at[d - 1, some(g)], in_plane(d)
        )

    def scatter_a_line(piece):
        d = lax.rem(piece + planes - plane, planes)
        return copy(a_line, (d - 1,), part.at[piece], second.at[d - 1], (piece * PLANE + spot, group))

    def scatter_c_line(d):
        return copy(c_line, (d - 1,), mine_ref.at[:, plane_of(d), lower_rows], line.at[d - 1], in_line(d))

    def scatter_c_plane(d):
        return copy(c_plane, (d - 1,), mixed.at[spot_of(d)], last.at[d - 1], in_plane(d))

    own_index = plane % size

    def gather_a_line(d, g):
        where = upper[g].at[spot * size + own_index]
        return copy(ga_line, (d - 1,), where, where, in_line(d))

    def gather_a_plane(d, g):
        where = upper[g].at[pl.ds(spot * size, size)]
        return copy(ga_plane, (d - 1, g), where, where, in_plane(d))

    def gather_c_plane(d, g):
        where = lower[g].at[own_index * PLANE + spot]
        return copy(gc_plane, (d - 1,), where, where, in_plane(d))

    def gather_c_line(d, g):
        where = lower[g].at[pl.ds(own_index * PLANE, PLANE)]
        return copy(gc_line, (d - 1,), where, where, in_line(d))

    def sender(piece):
        return lax.rem(plane + planes - piece, planes)

    def on_own_group(work):
        for g in range(groups):
            pl.when(plane // size == g)(functools.partial(work, g))

    def others_of(g, work):
        for index in range(size):
            piece = g * size + index
            pl.when(piece != plane)(functools.partial(work, piece))

    weight = weight_ref[pl.ds(spot * (RB_LOC // PLANE) + own_index // (half_probes // rows), 1), :]

    def product(k):
        return lax.dot_general(
            field_ref[plan_ref[1, k]], blocks_ref[plan_ref[0, k]], (((1,), (1,)), ((), ())), preferred_element_type=F32
        )

    def forward():
        running_sums(plan_ref, 0, blocks_ref.shape[0], product, products, sums)
        for block in range(RB_LOC):
            value = block_sum(plan_ref, 0, block, sums)
            for start in range(0, 2 * half_probes, rows):
                half, at = divmod(start, half_probes)
                piece = half * size + (block % 2 * half_probes + at) // rows
                mine_ref[block // 2, piece] = value[start : start + rows]

    def begin_group(g):
        for d in in_planes:
            scatter_a_plane(d, g).start()

    def plane_sums(g):
        for d in in_planes:
            scatter_a_plane(d, g).wait_recv()
        for index in range(size):
            piece = g * size + index
            total = mine_ref[spot, piece, 0:cut].astype(F32)
            for other in range(PLANE - 1):
                total = total + first[other, piece].astype(F32)
            part[piece] = total.astype(BF16)

            @pl.when(piece != plane)
            def _():
                scatter_a_line(piece).start()

    def own_rows(g):
        for d in in_lines:
            copy(a_line, (d - 1,), part.at[plane], second.at[d - 1], in_line(d)).wait_recv()
        total = part[plane].astype(F32)
        for other in range(planes - 1):
            total = total + second[other].astype(F32)
        upper[g][spot * size + own_index] = (total * weight).astype(BF16)
        for d in in_lines:
            gather_a_line(d, g).start()

    def spread_group(g):
        def landed(piece):
            where = upper[g].at[spot * size + piece % size]
            copy(ga_line, (sender(piece) - 1,), where, where, in_line(1)).wait_recv()

        others_of(g, landed)
        for d in in_planes:
            gather_a_plane(d, g).start()

    def line_sums():
        for d in in_lines:
            scatter_c_line(d).wait_recv()
        for d in [*in_planes, 0]:
            piece = spot_of(d)
            total = mine_ref[piece, plane, cut:rows].astype(F32)
            for other in range(planes - 1):
                total = total + line[other, piece].astype(F32)
            mixed[piece] = total.astype(BF16)
            if d:
                scatter_c_plane(d).start()

    def own_lower_rows(g):
        for d in in_planes:
            scatter_c_plane(d).wait_recv()
        total = mixed[spot].astype(F32)
        for other in range(PLANE - 1):
            total = total + last[other].astype(F32)
        lower[g][own_index * PLANE + spot] = (total * weight).astype(BF16)
        for d in in_planes:
            gather_c_plane(d, g).start()

    def spread_lower_rows(g):
        for d in in_planes:
            gather_c_plane(d, g).wait_recv()
        for d in in_lines:
            gather_c_line(d, g).start()

    def run():
        begin_group(0)
        for d in in_lines:
            scatter_c_line(d).start()
        begin_group(1)
        plane_sums(0)
        line_sums()
        plane_sums(1)
        on_own_group(own_lower_rows)
        on_own_group(own_rows)
        spread_group(0)
        on_own_group(spread_lower_rows)
        spread_group(1)

    def ready(g):
        for d in in_planes:
            gather_a_plane(d, g).wait_recv()

        def landed(piece):
            where = lower[g].at[pl.ds(piece % size * PLANE, PLANE)]
            copy(gc_line, (sender(piece) - 1,), where, where, in_line(1)).wait_recv()

        others_of(g, landed)

    def finish():
        for d in in_planes:
            for g in range(groups):
                gather_a_plane(d, g).wait_send()
                scatter_a_plane(d, g).wait_send()
            scatter_c_plane(d).wait_send()
            gather_c_plane(d, 0).wait_send()
        for d in in_lines:
            gather_c_line(d, 0).wait_send()
            gather_a_line(d, 0).wait_send()
            scatter_c_line(d).wait_send()
            copy(a_line, (d - 1,), part.at[plane], second.at[d - 1], in_line(d)).wait_send()

    partners = [in_plane(d) for d in in_planes] + [in_line(d) for d in in_lines]
    return partners, forward, run, ready, finish


def hessian_kernel(n_src, plan_ref, field_ref, blocks_ref, weight_ref, probes_ref, kext_ref, out_ref, *scratch):
    (
        products, sums, mine, first, part, second, line, mixed, last,
        upper_far, upper_near, lower_far, lower_near, terms_far, terms_near, pair, relayed, joined, far,
        edge, halo, wide, kwide, keep, flat, edge_send, edge_recv, send, recv, *sems,
    ) = scratch
    upper, lower = (upper_far, upper_near), (lower_far, lower_near)
    half_probes = pl.ds(0, field_ref.shape[1] // 2)
    back_products, back_sums = products.at[:, half_probes], sums.at[:, half_probes]
    reduce_partners, forward, run, ready, finish_reduction = reduction(
        n_src // PLANE, plan_ref, field_ref, blocks_ref, weight_ref, products, sums, mine, first, part, second, line, mixed,
        last, upper, lower, *sems,
    )
    me, group, before, after, twin, opposite = neighbours(n_src)
    lat = kext_ref.shape[0] - 16
    loc, lon = probes_ref.shape[0] // lat, probes_ref.shape[1]
    slabs = loc // SLAB
    core = group % 2
    partners = [before, after, (me, twin), (me, opposite), *reduce_partners]
    announce(partners)
    forward()
    await_all(partners)
    run()

    def view(ref, k, offset=0):
        if isinstance(k, int) and k < 2:
            return ref.at[pl.ds(k * (lat - SMOOTH), SMOOTH), pl.ds(pl.multiple_of(offset, loc), loc), :]
        start = pl.multiple_of(offset + (k - 2) * SLAB, SLAB)
        return ref.at[pl.ds(SMOOTH, lat - 2 * SMOOTH), pl.ds(start, SLAB), :]

    def term(terms, core_of, k):
        return view(terms, k, core_of * loc)

    def adjoint(half, terms):
        pieces = upper_far.shape[0] // RB_LOC

        def product(k):
            receptor, low = plan_ref[9, k], plan_ref[13, k]
            rows = []
            for piece in range(pieces):
                rows += [upper[half][receptor * pieces + piece], lower[half][low + piece * PLANE]]
            return jnp.dot(jnp.concatenate(rows, axis=0), blocks_ref[plan_ref[8, k]], preferred_element_type=F32)

        running_sums(plan_ref, 8, blocks_ref.shape[0], product, back_products, back_sums)
        for row in range(lat):
            for side in range(2):
                terms[row, :, side * BLK : (side + 1) * BLK] = block_sum(plan_ref, 8, 2 * row + side, back_sums)

    def for_relay(k):
        return remote(term(terms_far, 1 - core, k), view(relayed, k), send.at[0, k], recv.at[0, k], (me, twin))

    def for_twin(k):
        return remote(term(terms_near, 1 - core, k), view(pair, k), send.at[1, k], recv.at[1, k], (me, twin))

    def across(k):
        return remote(view(joined, k), view(far, k), send.at[2, k], recv.at[2, k], (me, opposite))

    def each(work):
        work(0)
        work(1)
        lax.fori_loop(2, slabs + 2, lambda k, carry: (work(k), carry)[1], 0)

    def join(k):
        for_relay(k).wait_recv()
        view(joined, k)[...] = (
            term(terms_far, core, k)[...].astype(F32) + view(relayed, k)[...].astype(F32)
        ).astype(BF16)
        across(k).start()

    def total(k):
        for_twin(k).wait_recv()
        across(k).wait_recv()
        return term(terms_near, core, k)[...].astype(F32) + view(pair, k)[...].astype(F32) + view(far, k)[...].astype(F32)

    edges = [
        remote(edge.at[0], halo.at[1], edge_send.at[0], edge_recv.at[0], before),
        remote(edge.at[1], halo.at[0], edge_send.at[1], edge_recv.at[1], after),
    ]
    ready(0)
    adjoint(0, terms_far)
    each(lambda k: for_relay(k).start())
    spread_kappa(n_src, me, kext_ref, kwide, keep, range(lat + 2 * SMOOTH))
    each(join)
    ready(1)
    adjoint(1, terms_near)
    each(lambda k: for_twin(k).start())
    for k, row in ((0, SMOOTH), (1, lat)):
        rows = total(k)
        wide[row : row + SMOOTH] = rows
        edge[k] = rows.astype(BF16)
        edges[k].start()

    def one_slab(slab, carry):
        probes_here = pl.ds(pl.multiple_of(slab * SLAB, SLAB), SLAB)
        wide[2 * SMOOTH : lat, probes_here, :] = total(slab + 2)

        @pl.when(slab == 0)
        def _():
            for copy in edges:
                copy.wait()
            wide[0:SMOOTH] = halo[0].astype(F32)
            wide[lat + SMOOTH :] = halo[1].astype(F32)

        for half in range(SLAB // 8):
            some = pl.ds(pl.multiple_of(slab * SLAB + half * 8, 8), 8)
            value = halves_of(wide, slice(None), some)
            for step in range(SMOOTH):
                rows = slice(step, lat + 2 * SMOOTH - step)
                scaled = [w * v for w, v in zip(halves_of(kwide, rows, slice(None)), value)]
                around = beside(*[v[1:-1] for v in scaled])
                inner = slice(step + 1, lat + 2 * SMOOTH - 1 - step)
                value = [
                    v[1:-1] * k + (g[:-2] + g[2:] + a)
                    for v, k, g, a in zip(value, halves_of(keep, inner, slice(None)), scaled, around)
                ]
            for side in range(2):
                for row in range(lat):
                    flat[side, pl.ds(half * 8 * lat + row, 8, stride=lat), :] = value[side][row]
        some = pl.ds(pl.multiple_of(slab * SLAB * lat, SLAB * lat), SLAB * lat)
        for side in range(2):
            lanes = slice(side * BLK, (side + 1) * BLK)
            out_ref[some, lanes] = flat[side] + probes_ref[some, lanes].astype(F32)
        return carry

    lax.fori_loop(0, slabs, one_slab, 0)

    def finish(k):
        for_relay(k).wait_send()
        for_twin(k).wait_send()
        across(k).wait_send()

    each(finish)
    finish_reduction()


def hessian_part(n_src, plan, field, blocks, weight, probes, kext):
    lat = kext.shape[0] - 16
    loc, lon = probes.shape[0] // lat, probes.shape[1]
    total, slots = field.shape[1], blocks.shape[0]
    half = total // 2
    planes = n_src // PLANE
    rows = RB_LOC * total // (PLANE * planes)
    cut = rows * 3 // 4
    rest = rows - cut
    pieces = loc // SLAB + 2
    together = min(TOGETHER, slots)
    dma = pltpu.SemaphoreType.DMA
    per_spot, per_plane, parts = (PLANE - 1,), (planes - 1,), (PLANE - 1, 2)
    counts = (parts, per_plane, per_plane, per_spot, per_plane, parts, per_spot, per_plane)
    held = [
        (slots, total, BLK),
        (PLANE, planes, rows, BLK),
        (PLANE - 1, planes, cut, BLK),
        (planes, cut, BLK),
        (planes - 1, cut, BLK),
        (planes - 1, PLANE, rest, BLK),
        (PLANE, rest, BLK),
        (PLANE - 1, rest, BLK),
        *[(PLANE * planes // 2, cut, BLK)] * 2,
        *[(PLANE * planes // 2, rest, BLK)] * 2,
        *[(lat, half, lon)] * 2,
        *[(lat, loc, lon)] * 4,
        *[(2, SMOOTH, loc, lon)] * 2,
    ]
    return pl.pallas_call(
        functools.partial(hessian_kernel, n_src),
        out_shape=jax.ShapeDtypeStruct(probes.shape, F32),
        in_specs=[pl.BlockSpec(memory_space=pltpu.SMEM)] + [pl.BlockSpec(memory_space=VMEM)] * 5,
        out_specs=pl.BlockSpec(memory_space=VMEM),
        scratch_shapes=[
            VMEM((together, total, BLK), F32),
            VMEM(held[0], BF16),
            *[VMEM(shape, BF16) for shape in held[1:]],
            VMEM((lat + 2 * SMOOTH, loc, lon), F32),
            VMEM((lat + 2 * SMOOTH, 8, lon), F32),
            VMEM((lat + 2 * SMOOTH, 8, lon), F32),
            VMEM((lon // BLK, SLAB * lat, BLK), F32),
            dma((2,)),
            dma((2,)),
            dma((3, pieces)),
            dma((3, pieces)),
        ]
        + [dma(count) for count in counts for _ in range(2)],
        compiler_params=pltpu.CompilerParams(
            collective_id=1, has_side_effects=True, vmem_limit_bytes=VMEM_LIMIT
        ),
        name="hessian_part",
    )(plan, field, blocks, weight, probes, kext)


def per_device(probes, kappa, footprint, block_source, block_receptor, block_count, obs_weight):
    n_src, n_rcv = lax.axis_size("src"), lax.axis_size("rcv")
    loc, lat, lon = probes.shape
    flat = probes.reshape(loc * lat, lon)
    blocks = footprint.reshape(footprint.shape[2:])
    slots = blocks.shape[0]
    sources, receptors = block_source.reshape(1, slots), block_receptor.reshape(1, slots)
    unused = lax.broadcasted_iota(jnp.int32, (1, slots), 1) >= block_count.reshape(1, 1)
    packed = sources + SLOT_BASE * (receptors + SLOT_BASE * unused.astype(jnp.int32))
    field, kext, plan = smooth_and_gather(n_src, n_rcv, flat, kappa, packed)
    out = hessian_part(n_src, plan, field, blocks, obs_weight.reshape(RB_LOC, BLK), flat, kext)
    return out.reshape(loc, lat, lon)


def solution(mesh):
    placed = (
        P("rcv", "src", None),
        P("src", None),
        P("src", "rcv", None, None, None),
        P("src", "rcv", None),
        P("src", "rcv", None),
        P("src", "rcv"),
        P("rcv"),
    )
    return jax.shard_map(
        per_device, mesh=mesh, in_specs=placed, out_specs=P("rcv", "src", None), check_vma=False
    )
```

```python
import functools

import jax
import jax.numpy as jnp
from jax import lax
from jax.experimental import pallas as pl
from jax.experimental.pallas import tpu as pltpu
from jax.sharding import PartitionSpec as P

BLK = 128
RB_LOC = 16
SMOOTH = 4
PLANE = 8
SLAB = 16
SLOT_BASE = 64
TOGETHER = 64
MESH = pl.DeviceIdType.MESH
VMEM = pltpu.VMEM
F32 = jnp.float32
BF16 = jnp.bfloat16
VMEM_LIMIT = 40 * 1024 * 1024


def announce(devices):
    barrier = pltpu.get_barrier_semaphore()
    for device in devices:
        pl.semaphore_signal(barrier, inc=1, device_id=device, device_id_type=MESH)


def await_all(devices):
    pl.semaphore_wait(pltpu.get_barrier_semaphore(), len(devices))


def remote(src, dst, send_sem, recv_sem, device):
    return pltpu.make_async_remote_copy(
        src_ref=src,
        dst_ref=dst,
        send_sem=send_sem,
        recv_sem=recv_sem,
        device_id=device,
        device_id_type=MESH,
    )


def neighbours(n_src):
    me = lax.axis_index("src")
    group = lax.axis_index("rcv")
    high, core = group // 2, group % 2
    before = (lax.rem(me + n_src - 1, n_src), group)
    after = (lax.rem(me + 1, n_src), group)
    twin = high * 2 + (1 - core)
    opposite = (1 - high) * 2 + core
    return me, group, before, after, twin, opposite


def beside(west_half, east_half):
    axis = west_half.ndim - 1
    lane = lax.broadcasted_iota(jnp.int32, west_half.shape, axis)
    first, last = lane == 0, lane == BLK - 1
    up_w, up_e = pltpu.roll(west_half, 1, axis), pltpu.roll(east_half, 1, axis)
    down_w, down_e = pltpu.roll(west_half, BLK - 1, axis), pltpu.roll(east_half, BLK - 1, axis)
    return (
        jnp.where(first, 0.0, up_w) + jnp.where(last, down_e, down_w),
        jnp.where(first, up_w, up_e) + jnp.where(last, 0.0, down_e),
    )


def halves_of(ref, rows, *middle):
    return [ref[(rows, *middle, slice(side * BLK, (side + 1) * BLK))] for side in range(2)]


def spread_kappa(n_src, me, kext_ref, kwide, keep, rows):
    for row in rows:
        value = kext_ref[8 - SMOOTH + row : 8 - SMOOTH + row + 1, :]
        if row < SMOOTH:
            value = jnp.where(me == 0, 0.0, value)
        if row >= kwide.shape[0] - SMOOTH:
            value = jnp.where(me == n_src - 1, 0.0, value)
        wide = jnp.broadcast_to(value, kwide.shape[1:])
        kwide[row] = wide
        keep[row] = 1.0 - 4.0 * wide


def make_plan(lower_pieces, packed, plan_ref):
    slots, lanes = packed.shape[1], plan_ref.shape[1]
    sources, receptors = packed % SLOT_BASE, packed // SLOT_BASE % SLOT_BASE
    row_of = lax.broadcasted_iota(jnp.int32, (slots, slots), 0)
    lane_of = lax.broadcasted_iota(jnp.int32, (slots, slots), 1)
    place = lax.broadcasted_iota(jnp.int32, (slots, lanes), 1)
    slot = lax.broadcasted_iota(jnp.int32, (1, slots), 1)
    used = packed < SLOT_BASE * SLOT_BASE

    def column(row):
        return jnp.sum(jnp.where(row_of == lane_of, row, 0.0), axis=1, keepdims=True)

    first_lane = lax.broadcasted_iota(jnp.int32, (1, lanes), 1) == 0
    for base, owner, other in ((0, receptors, sources), (8, sources, receptors)):
        key = jnp.where(used, owner * 256 + slot, 64 * 256 + slot).astype(F32)
        tall = column(key)
        rank = jnp.sum(jnp.where(key < tall, 1.0, 0.0), axis=1, keepdims=True)
        here = rank.astype(jnp.int32) == place

        def ordered(values):
            return jnp.sum(jnp.where(here, values, 0.0), axis=0, keepdims=True).astype(jnp.int32)

        keys = ordered(tall)
        block = keys // 256
        ends = jnp.sum(
            jnp.where(tall < ((place + 1) * 256).astype(F32), 1.0, 0.0), axis=0, keepdims=True
        ).astype(jnp.int32)
        start = jnp.where(first_lane, 0, pltpu.roll(ends, 1, 1))
        same = (block == pltpu.roll(block, 1, 1)) & jnp.logical_not(first_lane)
        plan_ref[base : base + 1, :] = keys - block * 256
        plan_ref[base + 1 : base + 2, :] = ordered(column(other.astype(F32)))
        plan_ref[base + 2 : base + 3, :] = same.astype(jnp.int32)
        plan_ref[base + 3 : base + 4, :] = jnp.maximum(ends - 1, 0)
        if base:
            lower = other % 2 * (lower_pieces * PLANE) + other // 2
            plan_ref[base + 5 : base + 6, :] = ordered(column(lower.astype(F32)))
        plan_ref[base + 4 : base + 5, :] = (ends > start).astype(jnp.int32)


def smooth_kernel(
    n_src, probes_ref, kappa_ref, slots_ref, field_ref, kext_ref, plan_ref, flat, halo, edge, wide, kwide, keep,
    edge_send, edge_recv, send, recv,
):
    me, group, before, after, twin, opposite = neighbours(n_src)
    lat, lon = kappa_ref.shape
    loc = probes_ref.shape[0] // lat
    slabs = loc // SLAB
    partners = [before, after, (me, twin), (me, opposite)]
    announce(partners)

    top, bottom = range(SMOOTH), range(lat - SMOOTH, lat)
    for side in range(lon // BLK):
        flat[side] = probes_ref[:, side * BLK : (side + 1) * BLK].astype(F32)

    def of_row(row):
        return jnp.concatenate([flat[side, pl.ds(row, loc, stride=lat), :] for side in range(lon // BLK)], axis=1)

    for side, rows in enumerate((top, bottom)):
        for place, row in enumerate(rows):
            value = of_row(row)
            wide[SMOOTH + row] = value
            edge[side, place] = value.astype(BF16)
    for row in range(SMOOTH, lat - SMOOTH):
        wide[SMOOTH + row] = of_row(row)
    kext_ref[8 : lat + 8, :] = kappa_ref[...]
    spread_kappa(n_src, me, kext_ref, kwide, keep, range(SMOOTH, lat + SMOOTH))
    edges = [
        remote(edge.at[1], halo.at[0], edge_send.at[0], edge_recv.at[0], after),
        remote(edge.at[0], halo.at[1], edge_send.at[1], edge_recv.at[1], before),
        remote(kappa_ref.at[pl.ds(lat - 8, 8)], kext_ref.at[pl.ds(0, 8)], edge_send.at[2], edge_recv.at[2], after),
        remote(kappa_ref.at[pl.ds(0, 8)], kext_ref.at[pl.ds(lat + 8, 8)], edge_send.at[3], edge_recv.at[3], before),
    ]

    parts = ((SMOOTH, lat - SMOOTH), (0, SMOOTH), (lat - SMOOTH, lat))

    core = group % 2
    own, far = 2 + core, core

    def place(owner, part, slab):
        first, last = parts[part]
        return field_ref.at[
            pl.ds(2 * first, 2 * (last - first)), pl.ds(pl.multiple_of(owner * loc + slab * SLAB, SLAB), SLAB), :
        ]

    def to_twin(part, slab):
        where = place(own, part, slab)
        return remote(where, where, send.at[0, part, slab], recv.at[0, part, slab], (me, twin))

    def to_opposite(part, slab):
        there = place(far, part, slab)
        return remote(place(own, part, slab), there, send.at[1, part, slab], recv.at[1, part, slab], (me, opposite))

    def relay(part, slab):
        where = place(far, part, slab)
        return remote(where, where, send.at[2, part, slab], recv.at[2, part, slab], (me, twin))

    def smooth_part(part, slab):
        first, last = parts[part]
        groups = []
        for half in range(SLAB // 8):
            some = pl.ds(pl.multiple_of(slab * SLAB + half * 8, 8), 8)
            value = halves_of(wide, slice(first, last + 2 * SMOOTH), some)
            for step in range(SMOOTH):
                rows = slice(first + step + 1, last + 2 * SMOOTH - 1 - step)
                centre = [v[1:-1] for v in value]
                around = beside(*centre)
                value = [
                    c * k + w * (v[:-2] + v[2:] + a)
                    for c, k, w, v, a in zip(
                        centre, halves_of(keep, rows, slice(None)), halves_of(kwide, rows, slice(None)), value, around
                    )
                ]
            groups.append(value)
        mine = pl.ds(pl.multiple_of(own * loc + slab * SLAB, SLAB), SLAB)
        for side in range(2):
            smoothed = jnp.concatenate([g[side] for g in groups], axis=1).astype(BF16)
            for row in range(first, last):
                field_ref[2 * row + side, mine, :] = smoothed[row - first]

    def post(part, slab):
        to_opposite(part, slab).start()
        to_twin(part, slab).start()

    def inner(slab, carry):
        smooth_part(0, slab)
        post(0, slab)
        return carry

    def outer(slab, carry):
        for part in (1, 2):
            smooth_part(part, slab)
            post(part, slab)
        return carry

    smooth_part(0, 0)
    await_all(partners)
    post(0, 0)
    for copy in edges:
        copy.start()
    lax.fori_loop(1, slabs, inner, 0)
    for copy in edges:
        copy.wait()
    wide[0:SMOOTH] = jnp.where(me == 0, 0.0, halo[0].astype(F32))
    wide[lat + SMOOTH :] = jnp.where(me == n_src - 1, 0.0, halo[1].astype(F32))
    spread_kappa(n_src, me, kext_ref, kwide, keep, [*range(SMOOTH), *range(lat + SMOOTH, lat + 2 * SMOOTH)])
    lax.fori_loop(0, slabs, outer, 0)
    make_plan(n_src // PLANE // 4, slots_ref[...], plan_ref)

    def pass_on(parts_here):
        def one(slab, carry):
            for part in parts_here:
                to_opposite(part, slab).wait_recv()
                relay(part, slab).start()
            return carry

        lax.fori_loop(0, slabs, one, 0)

    pass_on((0,))
    pass_on((1, 2))

    def finish(slab, carry):
        for part in range(3):
            to_opposite(part, slab).wait_send()
            to_twin(part, slab).wait()
            relay(part, slab).wait()
        return carry

    lax.fori_loop(0, slabs, finish, 0)


def smooth_and_gather(n_src, n_rcv, probes, kappa, packed):
    lat, lon = kappa.shape
    loc = probes.shape[0] // lat
    slabs = loc // SLAB
    dma = pltpu.SemaphoreType.DMA
    return pl.pallas_call(
        functools.partial(smooth_kernel, n_src),
        out_shape=(
            jax.ShapeDtypeStruct((lat * lon // BLK, loc * n_rcv, BLK), BF16),
            jax.ShapeDtypeStruct((lat + 16, lon), F32),
            jax.ShapeDtypeStruct((16, 256), jnp.int32),
        ),
        in_specs=[pl.BlockSpec(memory_space=VMEM)] * 3,
        out_specs=(pl.BlockSpec(memory_space=VMEM),) * 3,
        scratch_shapes=[
            VMEM((lon // BLK, loc * lat, BLK), F32),
            VMEM((2, SMOOTH, loc, lon), BF16),
            VMEM((2, SMOOTH, loc, lon), BF16),
            VMEM((lat + 2 * SMOOTH, loc, lon), F32),
            VMEM((lat + 2 * SMOOTH, 8, lon), F32),
            VMEM((lat + 2 * SMOOTH, 8, lon), F32),
            dma((4,)),
            dma((4,)),
            dma((3, 3, slabs)),
            dma((3, 3, slabs)),
        ],
        compiler_params=pltpu.CompilerParams(
            collective_id=0, has_side_effects=True, vmem_limit_bytes=VMEM_LIMIT
        ),
        cost_estimate=pl.CostEstimate(flops=20_000_000_000, bytes_accessed=64_000_000, transcendentals=0),
        name="smooth_and_gather",
    )(probes, kappa, packed)


def running_sums(plan_ref, base, slots, product, products, sums):
    together = products.shape[0]

    def several(turn, total):
        for step in range(together):
            k = turn * together + step
            products[step] = product(k)
        for step in range(together):
            k = turn * together + step
            total = products[step] + total * plan_ref[base + 2, k].astype(F32)
            sums[k] = total.astype(BF16)
        return total

    lax.fori_loop(0, slots // together, several, jnp.zeros(sums.shape[1:], F32))


def block_sum(plan_ref, base, block, sums):
    value = sums[plan_ref[base + 3, block]]
    return (value.astype(F32) * plan_ref[base + 4, block].astype(F32)).astype(BF16)


def reduction(planes, plan_ref, field_ref, blocks_ref, weight_ref, products, sums, mine_ref, first, part, second, line, mixed, last, upper, lower, *sems):
    me = lax.axis_index("src")
    group = lax.axis_index("rcv")
    plane, spot = me // PLANE, me % PLANE
    pairs = iter(sems)
    a_plane, a_line, c_line, c_plane, ga_line, ga_plane, gc_plane, gc_line = zip(pairs, pairs)
    rows = mine_ref.shape[2]
    cut = rows * 3 // 4
    upper_rows, lower_rows = pl.ds(0, cut), pl.ds(cut, rows - cut)
    half_probes = field_ref.shape[1] // 2
    groups = 2
    size = planes // groups
    in_planes = range(1, PLANE)
    in_lines = range(1, planes)

    def spot_of(distance):
        return lax.rem(spot + distance, PLANE)

    def plane_of(distance):
        return lax.rem(plane + distance, planes)

    def in_plane(distance):
        return (plane * PLANE + spot_of(distance), group)

    def in_line(distance):
        return (plane_of(distance) * PLANE + spot, group)

    def copy(pair, index, src, dst, device):
        return remote(src, dst, pair[0].at[index], pair[1].at[index], device)

    def some(g):
        return pl.ds(g * size, size)

    def scatter_a_plane(d, g):
        return copy(
            a_plane, (d - 1, g), mine_ref.at[spot_of(d), some(g), upper_rows], first.at[d - 1, some(g)], in_plane(d)
        )

    def scatter_a_line(piece):
        d = lax.rem(piece + planes - plane, planes)
        return copy(a_line, (d - 1,), part.at[piece], second.at[d - 1], (piece * PLANE + spot, group))

    def scatter_c_line(d):
        return copy(c_line, (d - 1,), mine_ref.at[:, plane_of(d), lower_rows], line.at[d - 1], in_line(d))

    def scatter_c_plane(d):
        return copy(c_plane, (d - 1,), mixed.at[spot_of(d)], last.at[d - 1], in_plane(d))

    own_index = plane % size

    def gather_a_line(d, g):
        where = upper[g].at[spot * size + own_index]
        return copy(ga_line, (d - 1,), where, where, in_line(d))

    def gather_a_plane(d, g):
        where = upper[g].at[pl.ds(spot * size, size)]
        return copy(ga_plane, (d - 1, g), where, where, in_plane(d))

    def gather_c_plane(d, g):
        where = lower[g].at[own_index * PLANE + spot]
        return copy(gc_plane, (d - 1,), where, where, in_plane(d))

    def gather_c_line(d, g):
        where = lower[g].at[pl.ds(own_index * PLANE, PLANE)]
        return copy(gc_line, (d - 1,), where, where, in_line(d))

    def sender(piece):
        return lax.rem(plane + planes - piece, planes)

    def on_own_group(work, which=(0, 1)):
        for g in which:
            pl.when(plane // size == g)(functools.partial(work, g))

    def others_of(g, work):
        for index in range(size):
            piece = g * size + index
            pl.when(piece != plane)(functools.partial(work, piece))

    weight = weight_ref[pl.ds(spot * (RB_LOC // PLANE) + own_index // (half_probes // rows), 1), :]

    def product(k):
        return lax.dot_general(
            field_ref[plan_ref[1, k]], blocks_ref[plan_ref[0, k]], (((1,), (1,)), ((), ())), preferred_element_type=F32
        )

    def forward():
        running_sums(plan_ref, 0, blocks_ref.shape[0], product, products, sums)
        for block in range(RB_LOC):
            value = block_sum(plan_ref, 0, block, sums)
            for start in range(0, 2 * half_probes, rows):
                half, at = divmod(start, half_probes)
                piece = half * size + (block % 2 * half_probes + at) // rows
                mine_ref[block // 2, piece] = value[start : start + rows]

    def begin_group(g):
        for d in in_planes:
            scatter_a_plane(d, g).start()

    def plane_sums(g):
        for d in in_planes:
            scatter_a_plane(d, g).wait_recv()
        for index in range(size):
            piece = g * size + index
            total = mine_ref[spot, piece, 0:cut].astype(F32)
            for other in range(PLANE - 1):
                total = total + first[other, piece].astype(F32)
            part[piece] = total.astype(BF16)

            @pl.when(piece != plane)
            def _():
                scatter_a_line(piece).start()

    def own_rows(g):
        for d in in_lines:
            copy(a_line, (d - 1,), part.at[plane], second.at[d - 1], in_line(d)).wait_recv()
        total = part[plane].astype(F32)
        for other in range(planes - 1):
            total = total + second[other].astype(F32)
        upper[g][spot * size + own_index] = (total * weight).astype(BF16)
        for d in in_lines:
            gather_a_line(d, g).start()

    def spread_group(g):
        def landed(piece):
            where = upper[g].at[spot * size + piece % size]
            copy(ga_line, (sender(piece) - 1,), where, where, in_line(1)).wait_recv()

        others_of(g, landed)
        for d in in_planes:
            gather_a_plane(d, g).start()

    def line_sums():
        for d in in_lines:
            scatter_c_line(d).wait_recv()
        for d in [*in_planes, 0]:
            piece = spot_of(d)
            total = mine_ref[piece, plane, cut:rows].astype(F32)
            for other in range(planes - 1):
                total = total + line[other, piece].astype(F32)
            mixed[piece] = total.astype(BF16)
            if d:
                scatter_c_plane(d).start()

    def own_lower_rows(g):
        for d in in_planes:
            scatter_c_plane(d).wait_recv()
        total = mixed[spot].astype(F32)
        for other in range(PLANE - 1):
            total = total + last[other].astype(F32)
        lower[g][own_index * PLANE + spot] = (total * weight).astype(BF16)
        for d in in_planes:
            gather_c_plane(d, g).start()

    def spread_lower_rows(g):
        for d in in_planes:
            gather_c_plane(d, g).wait_recv()
        for d in in_lines:
            gather_c_line(d, g).start()

    def run():
        begin_group(0)
        for d in in_lines:
            scatter_c_line(d).start()
        begin_group(1)
        plane_sums(0)
        line_sums()
        plane_sums(1)
        on_own_group(own_rows, (0,))
        on_own_group(own_lower_rows)
        on_own_group(own_rows, (1,))
        spread_group(0)
        on_own_group(spread_lower_rows, (0,))
        spread_group(1)
        on_own_group(spread_lower_rows, (1,))

    def ready(g):
        for d in in_planes:
            gather_a_plane(d, g).wait_recv()

        def landed(piece):
            where = lower[g].at[pl.ds(piece % size * PLANE, PLANE)]
            copy(gc_line, (sender(piece) - 1,), where, where, in_line(1)).wait_recv()

        others_of(g, landed)

    def finish():
        for d in in_planes:
            for g in range(groups):
                gather_a_plane(d, g).wait_send()
                scatter_a_plane(d, g).wait_send()
            scatter_c_plane(d).wait_send()
            gather_c_plane(d, 0).wait_send()
        for d in in_lines:
            gather_c_line(d, 0).wait_send()
            gather_a_line(d, 0).wait_send()
            scatter_c_line(d).wait_send()
            copy(a_line, (d - 1,), part.at[plane], second.at[d - 1], in_line(d)).wait_send()

    partners = [in_plane(d) for d in in_planes] + [in_line(d) for d in in_lines]
    return partners, forward, run, ready, finish


def hessian_kernel(n_src, plan_ref, field_ref, blocks_ref, weight_ref, probes_ref, kext_ref, out_ref, *scratch):
    (
        products, sums, mine, first, part, second, line, mixed, last,
        upper_far, upper_near, lower_far, lower_near, terms_far, terms_near, pair, relayed, joined, far,
        edge, halo, wide, kwide, keep, flat, edge_send, edge_recv, send, recv, *sems,
    ) = scratch
    upper, lower = (upper_far, upper_near), (lower_far, lower_near)
    half_probes = pl.ds(0, field_ref.shape[1] // 2)
    back_products, back_sums = products.at[:, half_probes], sums.at[:, half_probes]
    reduce_partners, forward, run, ready, finish_reduction = reduction(
        n_src // PLANE, plan_ref, field_ref, blocks_ref, weight_ref, products, sums, mine, first, part, second, line, mixed,
        last, upper, lower, *sems,
    )
    me, group, before, after, twin, opposite = neighbours(n_src)
    lat = kext_ref.shape[0] - 16
    loc, lon = probes_ref.shape[0] // lat, probes_ref.shape[1]
    slabs = loc // SLAB
    core = group % 2
    partners = [before, after, (me, twin), (me, opposite), *reduce_partners]
    announce(partners)
    forward()
    await_all(partners)
    run()

    def view(ref, k, offset=0):
        if isinstance(k, int) and k < 2:
            return ref.at[pl.ds(k * (lat - SMOOTH), SMOOTH), pl.ds(pl.multiple_of(offset, loc), loc), :]
        start = pl.multiple_of(offset + (k - 2) * SLAB, SLAB)
        return ref.at[pl.ds(SMOOTH, lat - 2 * SMOOTH), pl.ds(start, SLAB), :]

    def term(terms, core_of, k):
        return view(terms, k, core_of * loc)

    def adjoint(half, terms):
        pieces = upper_far.shape[0] // RB_LOC

        def product(k):
            receptor, low = plan_ref[9, k], plan_ref[13, k]
            rows = []
            for piece in range(pieces):
                rows += [upper[half][receptor * pieces + piece], lower[half][low + piece * PLANE]]
            return jnp.dot(jnp.concatenate(rows, axis=0), blocks_ref[plan_ref[8, k]], preferred_element_type=F32)

        running_sums(plan_ref, 8, blocks_ref.shape[0], product, back_products, back_sums)
        for row in range(lat):
            for side in range(2):
                terms[row, :, side * BLK : (side + 1) * BLK] = block_sum(plan_ref, 8, 2 * row + side, back_sums)

    def for_relay(k):
        return remote(term(terms_far, 1 - core, k), view(relayed, k), send.at[0, k], recv.at[0, k], (me, twin))

    def for_twin(k):
        return remote(term(terms_near, 1 - core, k), view(pair, k), send.at[1, k], recv.at[1, k], (me, twin))

    def across(k):
        return remote(view(joined, k), view(far, k), send.at[2, k], recv.at[2, k], (me, opposite))

    def each(work):
        work(0)
        work(1)
        lax.fori_loop(2, slabs + 2, lambda k, carry: (work(k), carry)[1], 0)

    def join(k):
        for_relay(k).wait_recv()
        view(joined, k)[...] = (
            term(terms_far, core, k)[...].astype(F32) + view(relayed, k)[...].astype(F32)
        ).astype(BF16)
        across(k).start()

    def total(k):
        for_twin(k).wait_recv()
        across(k).wait_recv()
        return term(terms_near, core, k)[...].astype(F32) + view(pair, k)[...].astype(F32) + view(far, k)[...].astype(F32)

    edges = [
        remote(edge.at[0], halo.at[1], edge_send.at[0], edge_recv.at[0], before),
        remote(edge.at[1], halo.at[0], edge_send.at[1], edge_recv.at[1], after),
    ]
    ready(0)
    adjoint(0, terms_far)
    each(lambda k: for_relay(k).start())
    spread_kappa(n_src, me, kext_ref, kwide, keep, range(lat + 2 * SMOOTH))
    each(join)
    ready(1)
    adjoint(1, terms_near)
    each(lambda k: for_twin(k).start())
    for k, row in ((0, SMOOTH), (1, lat)):
        rows = total(k)
        wide[row : row + SMOOTH] = rows
        edge[k] = rows.astype(BF16)
        edges[k].start()

    def one_slab(slab, carry):
        probes_here = pl.ds(pl.multiple_of(slab * SLAB, SLAB), SLAB)
        wide[2 * SMOOTH : lat, probes_here, :] = total(slab + 2)

        @pl.when(slab == 0)
        def _():
            for copy in edges:
                copy.wait()
            wide[0:SMOOTH] = halo[0].astype(F32)
            wide[lat + SMOOTH :] = halo[1].astype(F32)

        for half in range(SLAB // 8):
            some = pl.ds(pl.multiple_of(slab * SLAB + half * 8, 8), 8)
            value = halves_of(wide, slice(None), some)
            for step in range(SMOOTH):
                rows = slice(step, lat + 2 * SMOOTH - step)
                scaled = [w * v for w, v in zip(halves_of(kwide, rows, slice(None)), value)]
                around = beside(*[v[1:-1] for v in scaled])
                inner = slice(step + 1, lat + 2 * SMOOTH - 1 - step)
                value = [
                    v[1:-1] * k + (g[:-2] + g[2:] + a)
                    for v, k, g, a in zip(value, halves_of(keep, inner, slice(None)), scaled, around)
                ]
            for side in range(2):
                for row in range(lat):
                    flat[side, pl.ds(half * 8 * lat + row, 8, stride=lat), :] = value[side][row]
        some = pl.ds(pl.multiple_of(slab * SLAB * lat, SLAB * lat), SLAB * lat)
        for side in range(2):
            lanes = slice(side * BLK, (side + 1) * BLK)
            out_ref[some, lanes] = flat[side] + probes_ref[some, lanes].astype(F32)
        return carry

    lax.fori_loop(0, slabs, one_slab, 0)

    def finish(k):
        for_relay(k).wait_send()
        for_twin(k).wait_send()
        across(k).wait_send()

    each(finish)
    finish_reduction()


def hessian_part(n_src, plan, field, blocks, weight, probes, kext):
    lat = kext.shape[0] - 16
    loc, lon = probes.shape[0] // lat, probes.shape[1]
    total, slots = field.shape[1], blocks.shape[0]
    half = total // 2
    planes = n_src // PLANE
    rows = RB_LOC * total // (PLANE * planes)
    cut = rows * 3 // 4
    rest = rows - cut
    pieces = loc // SLAB + 2
    together = min(TOGETHER, slots)
    dma = pltpu.SemaphoreType.DMA
    per_spot, per_plane, parts = (PLANE - 1,), (planes - 1,), (PLANE - 1, 2)
    counts = (parts, per_plane, per_plane, per_spot, per_plane, parts, per_spot, per_plane)
    held = [
        (slots, total, BLK),
        (PLANE, planes, rows, BLK),
        (PLANE - 1, planes, cut, BLK),
        (planes, cut, BLK),
        (planes - 1, cut, BLK),
        (planes - 1, PLANE, rest, BLK),
        (PLANE, rest, BLK),
        (PLANE - 1, rest, BLK),
        *[(PLANE * planes // 2, cut, BLK)] * 2,
        *[(PLANE * planes // 2, rest, BLK)] * 2,
        *[(lat, half, lon)] * 2,
        *[(lat, loc, lon)] * 4,
        *[(2, SMOOTH, loc, lon)] * 2,
    ]
    return pl.pallas_call(
        functools.partial(hessian_kernel, n_src),
        out_shape=jax.ShapeDtypeStruct(probes.shape, F32),
        in_specs=[pl.BlockSpec(memory_space=pltpu.SMEM)] + [pl.BlockSpec(memory_space=VMEM)] * 5,
        out_specs=pl.BlockSpec(memory_space=VMEM),
        scratch_shapes=[
            VMEM((together, total, BLK), F32),
            VMEM(held[0], BF16),
            *[VMEM(shape, BF16) for shape in held[1:]],
            VMEM((lat + 2 * SMOOTH, loc, lon), F32),
            VMEM((lat + 2 * SMOOTH, 8, lon), F32),
            VMEM((lat + 2 * SMOOTH, 8, lon), F32),
            VMEM((lon // BLK, SLAB * lat, BLK), F32),
            dma((2,)),
            dma((2,)),
            dma((3, pieces)),
            dma((3, pieces)),
        ]
        + [dma(count) for count in counts for _ in range(2)],
        compiler_params=pltpu.CompilerParams(
            collective_id=1, has_side_effects=True, vmem_limit_bytes=VMEM_LIMIT
        ),
        name="hessian_part",
    )(plan, field, blocks, weight, probes, kext)


def per_device(probes, kappa, footprint, block_source, block_receptor, block_count, obs_weight):
    n_src, n_rcv = lax.axis_size("src"), lax.axis_size("rcv")
    loc, lat, lon = probes.shape
    flat = probes.reshape(loc * lat, lon)
    blocks = footprint.reshape(footprint.shape[2:])
    slots = blocks.shape[0]
    sources, receptors = block_source.reshape(1, slots), block_receptor.reshape(1, slots)
    unused = lax.broadcasted_iota(jnp.int32, (1, slots), 1) >= block_count.reshape(1, 1)
    packed = sources + SLOT_BASE * (receptors + SLOT_BASE * unused.astype(jnp.int32))
    field, kext, plan = smooth_and_gather(n_src, n_rcv, flat, kappa, packed)
    out = hessian_part(n_src, plan, field, blocks, obs_weight.reshape(RB_LOC, BLK), flat, kext)
    return out.reshape(loc, lat, lon)


def solution(mesh):
    placed = (
        P("rcv", "src", None),
        P("src", None),
        P("src", "rcv", None, None, None),
        P("src", "rcv", None),
        P("src", "rcv", None),
        P("src", "rcv"),
        P("rcv"),
    )
    return jax.shard_map(
        per_device, mesh=mesh, in_specs=placed, out_specs=P("rcv", "src", None), check_vma=False
    )
```

```python
import functools

import jax
import jax.numpy as jnp
from jax import lax
from jax.experimental import pallas as pl
from jax.experimental.pallas import tpu as pltpu
from jax.sharding import PartitionSpec as P

BLK = 128
RB_LOC = 16
SMOOTH = 4
PLANE = 8
SLAB = 16
SLOT_BASE = 64
TOGETHER = 64
MESH = pl.DeviceIdType.MESH
VMEM = pltpu.VMEM
F32 = jnp.float32
BF16 = jnp.bfloat16
VMEM_LIMIT = 40 * 1024 * 1024


def announce(devices):
    barrier = pltpu.get_barrier_semaphore()
    for device in devices:
        pl.semaphore_signal(barrier, inc=1, device_id=device, device_id_type=MESH)


def await_all(devices):
    pl.semaphore_wait(pltpu.get_barrier_semaphore(), len(devices))


def remote(src, dst, send_sem, recv_sem, device):
    return pltpu.make_async_remote_copy(
        src_ref=src,
        dst_ref=dst,
        send_sem=send_sem,
        recv_sem=recv_sem,
        device_id=device,
        device_id_type=MESH,
    )


def neighbours(n_src):
    me = lax.axis_index("src")
    group = lax.axis_index("rcv")
    high, core = group // 2, group % 2
    before = (lax.rem(me + n_src - 1, n_src), group)
    after = (lax.rem(me + 1, n_src), group)
    twin = high * 2 + (1 - core)
    opposite = (1 - high) * 2 + core
    return me, group, before, after, twin, opposite


def beside(west_half, east_half):
    axis = west_half.ndim - 1
    lane = lax.broadcasted_iota(jnp.int32, west_half.shape, axis)
    first, last = lane == 0, lane == BLK - 1
    up_w, up_e = pltpu.roll(west_half, 1, axis), pltpu.roll(east_half, 1, axis)
    down_w, down_e = pltpu.roll(west_half, BLK - 1, axis), pltpu.roll(east_half, BLK - 1, axis)
    return (
        jnp.where(first, 0.0, up_w) + jnp.where(last, down_e, down_w),
        jnp.where(first, up_w, up_e) + jnp.where(last, 0.0, down_e),
    )


def halves_of(ref, rows, *middle):
    return [ref[(rows, *middle, slice(side * BLK, (side + 1) * BLK))] for side in range(2)]


def spread_kappa(n_src, me, kext_ref, kwide, keep, rows):
    for row in rows:
        value = kext_ref[8 - SMOOTH + row : 8 - SMOOTH + row + 1, :]
        if row < SMOOTH:
            value = jnp.where(me == 0, 0.0, value)
        if row >= kwide.shape[0] - SMOOTH:
            value = jnp.where(me == n_src - 1, 0.0, value)
        wide = jnp.broadcast_to(value, kwide.shape[1:])
        kwide[row] = wide
        keep[row] = 1.0 - 4.0 * wide


def make_plan(lower_pieces, packed, plan_ref):
    slots, lanes = packed.shape[1], plan_ref.shape[1]
    sources, receptors = packed % SLOT_BASE, packed // SLOT_BASE % SLOT_BASE
    row_of = lax.broadcasted_iota(jnp.int32, (slots, slots), 0)
    lane_of = lax.broadcasted_iota(jnp.int32, (slots, slots), 1)
    place = lax.broadcasted_iota(jnp.int32, (slots, lanes), 1)
    slot = lax.broadcasted_iota(jnp.int32, (1, slots), 1)
    used = packed < SLOT_BASE * SLOT_BASE

    def column(row):
        return jnp.sum(jnp.where(row_of == lane_of, row, 0.0), axis=1, keepdims=True)

    first_lane = lax.broadcasted_iota(jnp.int32, (1, lanes), 1) == 0
    for base, owner, other in ((0, receptors, sources), (8, sources, receptors)):
        key = jnp.where(used, owner * 256 + slot, 64 * 256 + slot).astype(F32)
        tall = column(key)
        rank = jnp.sum(jnp.where(key < tall, 1.0, 0.0), axis=1, keepdims=True)
        here = rank.astype(jnp.int32) == place

        def ordered(values):
            return jnp.sum(jnp.where(here, values, 0.0), axis=0, keepdims=True).astype(jnp.int32)

        keys = ordered(tall)
        block = keys // 256
        ends = jnp.sum(
            jnp.where(tall < ((place + 1) * 256).astype(F32), 1.0, 0.0), axis=0, keepdims=True
        ).astype(jnp.int32)
        start = jnp.where(first_lane, 0, pltpu.roll(ends, 1, 1))
        same = (block == pltpu.roll(block, 1, 1)) & jnp.logical_not(first_lane)
        plan_ref[base : base + 1, :] = keys - block * 256
        plan_ref[base + 1 : base + 2, :] = ordered(column(other.astype(F32)))
        plan_ref[base + 2 : base + 3, :] = same.astype(jnp.int32)
        plan_ref[base + 3 : base + 4, :] = jnp.maximum(ends - 1, 0)
        if base:
            lower = other % 2 * (lower_pieces * PLANE) + other // 2
            plan_ref[base + 5 : base + 6, :] = ordered(column(lower.astype(F32)))
        plan_ref[base + 4 : base + 5, :] = (ends > start).astype(jnp.int32)


def smooth_kernel(
    n_src, probes_ref, kappa_ref, slots_ref, field_ref, kext_ref, plan_ref, flat, halo, edge, wide, kwide, keep,
    edge_send, edge_recv, send, recv,
):
    me, group, before, after, twin, opposite = neighbours(n_src)
    lat, lon = kappa_ref.shape
    loc = probes_ref.shape[0] // lat
    slabs = loc // SLAB
    partners = [before, after, (me, twin), (me, opposite)]
    announce(partners)

    top, bottom = range(SMOOTH), range(lat - SMOOTH, lat)
    for side in range(lon // BLK):
        flat[side] = probes_ref[:, side * BLK : (side + 1) * BLK].astype(F32)

    def of_row(row):
        return jnp.concatenate([flat[side, pl.ds(row, loc, stride=lat), :] for side in range(lon // BLK)], axis=1)

    for side, rows in enumerate((top, bottom)):
        for place, row in enumerate(rows):
            value = of_row(row)
            wide[SMOOTH + row] = value
            edge[side, place] = value.astype(BF16)
    for row in range(SMOOTH, lat - SMOOTH):
        wide[SMOOTH + row] = of_row(row)
    kext_ref[8 : lat + 8, :] = kappa_ref[...]
    spread_kappa(n_src, me, kext_ref, kwide, keep, range(SMOOTH, lat + SMOOTH))
    edges = [
        remote(edge.at[1], halo.at[0], edge_send.at[0], edge_recv.at[0], after),
        remote(edge.at[0], halo.at[1], edge_send.at[1], edge_recv.at[1], before),
        remote(kappa_ref.at[pl.ds(lat - 8, 8)], kext_ref.at[pl.ds(0, 8)], edge_send.at[2], edge_recv.at[2], after),
        remote(kappa_ref.at[pl.ds(0, 8)], kext_ref.at[pl.ds(lat + 8, 8)], edge_send.at[3], edge_recv.at[3], before),
    ]

    parts = ((SMOOTH, lat - SMOOTH), (0, SMOOTH), (lat - SMOOTH, lat))

    core = group % 2
    own, far = 2 + core, core

    def place(owner, part, slab):
        first, last = parts[part]
        return field_ref.at[
            pl.ds(2 * first, 2 * (last - first)), pl.ds(pl.multiple_of(owner * loc + slab * SLAB, SLAB), SLAB), :
        ]

    def to_twin(part, slab):
        where = place(own, part, slab)
        return remote(where, where, send.at[0, part, slab], recv.at[0, part, slab], (me, twin))

    def to_opposite(part, slab):
        there = place(far, part, slab)
        return remote(place(own, part, slab), there, send.at[1, part, slab], recv.at[1, part, slab], (me, opposite))

    def relay(part, slab):
        where = place(far, part, slab)
        return remote(where, where, send.at[2, part, slab], recv.at[2, part, slab], (me, twin))

    def smooth_part(part, slab):
        first, last = parts[part]
        groups = []
        for half in range(SLAB // 8):
            some = pl.ds(pl.multiple_of(slab * SLAB + half * 8, 8), 8)
            value = halves_of(wide, slice(first, last + 2 * SMOOTH), some)
            for step in range(SMOOTH):
                rows = slice(first + step + 1, last + 2 * SMOOTH - 1 - step)
                centre = [v[1:-1] for v in value]
                around = beside(*centre)
                value = [
                    c * k + w * (v[:-2] + v[2:] + a)
                    for c, k, w, v, a in zip(
                        centre, halves_of(keep, rows, slice(None)), halves_of(kwide, rows, slice(None)), value, around
                    )
                ]
            groups.append(value)
        mine = pl.ds(pl.multiple_of(own * loc + slab * SLAB, SLAB), SLAB)
        for side in range(2):
            smoothed = jnp.concatenate([g[side] for g in groups], axis=1).astype(BF16)
            for row in range(first, last):
                field_ref[2 * row + side, mine, :] = smoothed[row - first]

    def post(part, slab):
        to_opposite(part, slab).start()
        to_twin(part, slab).start()

    def inner(slab, carry):
        smooth_part(0, slab)
        post(0, slab)
        return carry

    def outer(slab, carry):
        for part in (1, 2):
            smooth_part(part, slab)
            post(part, slab)
        return carry

    smooth_part(0, 0)
    await_all(partners)
    post(0, 0)
    for copy in edges:
        copy.start()
    lax.fori_loop(1, slabs, inner, 0)
    for copy in edges:
        copy.wait()
    wide[0:SMOOTH] = jnp.where(me == 0, 0.0, halo[0].astype(F32))
    wide[lat + SMOOTH :] = jnp.where(me == n_src - 1, 0.0, halo[1].astype(F32))
    spread_kappa(n_src, me, kext_ref, kwide, keep, [*range(SMOOTH), *range(lat + SMOOTH, lat + 2 * SMOOTH)])
    lax.fori_loop(0, slabs, outer, 0)
    make_plan(n_src // PLANE // 4, slots_ref[...], plan_ref)

    def pass_on(parts_here):
        def one(slab, carry):
            for part in parts_here:
                to_opposite(part, slab).wait_recv()
                relay(part, slab).start()
            return carry

        lax.fori_loop(0, slabs, one, 0)

    pass_on((0,))
    pass_on((1, 2))

    def finish(slab, carry):
        for part in range(3):
            to_opposite(part, slab).wait_send()
            to_twin(part, slab).wait()
            relay(part, slab).wait()
        return carry

    lax.fori_loop(0, slabs, finish, 0)


def smooth_and_gather(n_src, n_rcv, probes, kappa, packed):
    lat, lon = kappa.shape
    loc = probes.shape[0] // lat
    slabs = loc // SLAB
    dma = pltpu.SemaphoreType.DMA
    return pl.pallas_call(
        functools.partial(smooth_kernel, n_src),
        out_shape=(
            jax.ShapeDtypeStruct((lat * lon // BLK, loc * n_rcv, BLK), BF16),
            jax.ShapeDtypeStruct((lat + 16, lon), F32),
            jax.ShapeDtypeStruct((16, 256), jnp.int32),
        ),
        in_specs=[pl.BlockSpec(memory_space=VMEM)] * 3,
        out_specs=(pl.BlockSpec(memory_space=VMEM),) * 3,
        scratch_shapes=[
            VMEM((lon // BLK, loc * lat, BLK), F32),
            VMEM((2, SMOOTH, loc, lon), BF16),
            VMEM((2, SMOOTH, loc, lon), BF16),
            VMEM((lat + 2 * SMOOTH, loc, lon), F32),
            VMEM((lat + 2 * SMOOTH, 8, lon), F32),
            VMEM((lat + 2 * SMOOTH, 8, lon), F32),
            dma((4,)),
            dma((4,)),
            dma((3, 3, slabs)),
            dma((3, 3, slabs)),
        ],
        compiler_params=pltpu.CompilerParams(
            collective_id=0, has_side_effects=True, vmem_limit_bytes=VMEM_LIMIT
        ),
        cost_estimate=pl.CostEstimate(flops=20_000_000_000, bytes_accessed=64_000_000, transcendentals=0),
        name="smooth_and_gather",
    )(probes, kappa, packed)


def running_sums(plan_ref, base, slots, product, products, sums):
    together = products.shape[0]

    def several(turn, total):
        for step in range(together):
            k = turn * together + step
            products[step] = product(k)
        for step in range(together):
            k = turn * together + step
            total = products[step] + total * plan_ref[base + 2, k].astype(F32)
            sums[k] = total.astype(BF16)
        return total

    lax.fori_loop(0, slots // together, several, jnp.zeros(sums.shape[1:], F32))


def block_sum(plan_ref, base, block, sums):
    value = sums[plan_ref[base + 3, block]]
    return (value.astype(F32) * plan_ref[base + 4, block].astype(F32)).astype(BF16)


def reduction(planes, plan_ref, field_ref, blocks_ref, weight_ref, products, sums, mine_ref, first, part, second, line, mixed, last, upper, lower, *sems):
    me = lax.axis_index("src")
    group = lax.axis_index("rcv")
    plane, spot = me // PLANE, me % PLANE
    pairs = iter(sems)
    a_plane, a_line, c_line, c_plane, ga_line, ga_plane, gc_plane, gc_line = zip(pairs, pairs)
    rows = mine_ref.shape[2]
    cut = rows * 3 // 4
    upper_rows, lower_rows = pl.ds(0, cut), pl.ds(cut, rows - cut)
    half_probes = field_ref.shape[1] // 2
    groups = 2
    size = planes // groups
    in_planes = range(1, PLANE)
    in_lines = range(1, planes)

    def spot_of(distance):
        return lax.rem(spot + distance, PLANE)

    def plane_of(distance):
        return lax.rem(plane + distance, planes)

    def in_plane(distance):
        return (plane * PLANE + spot_of(distance), group)

    def in_line(distance):
        return (plane_of(distance) * PLANE + spot, group)

    def copy(pair, index, src, dst, device):
        return remote(src, dst, pair[0].at[index], pair[1].at[index], device)

    def some(g):
        return pl.ds(g * size, size)

    def scatter_a_plane(d, g):
        return copy(
            a_plane, (d - 1, g), mine_ref.at[spot_of(d), some(g), upper_rows], first.at[d - 1, some(g)], in_plane(d)
        )

    def scatter_a_line(piece):
        d = lax.rem(piece + planes - plane, planes)
        return copy(a_line, (d - 1,), part.at[piece], second.at[d - 1], (piece * PLANE + spot, group))

    def scatter_c_line(d):
        return copy(c_line, (d - 1,), mine_ref.at[:, plane_of(d), lower_rows], line.at[d - 1], in_line(d))

    def scatter_c_plane(d):
        return copy(c_plane, (d - 1,), mixed.at[spot_of(d)], last.at[d - 1], in_plane(d))

    own_index = plane % size

    def gather_a_line(d, g):
        where = upper[g].at[spot * size + own_index]
        return copy(ga_line, (d - 1,), where, where, in_line(d))

    def gather_a_plane(d, g, index):
        where = upper[g].at[spot * size + index]
        return copy(ga_plane, (d - 1, g * size + index), where, where, in_plane(d))

    def gather_c_plane(d, g):
        where = lower[g].at[own_index * PLANE + spot]
        return copy(gc_plane, (d - 1,), where, where, in_plane(d))

    def gather_c_line(d, g):
        where = lower[g].at[pl.ds(own_index * PLANE, PLANE)]
        return copy(gc_line, (d - 1,), where, where, in_line(d))

    def sender(piece):
        return lax.rem(plane + planes - piece, planes)

    def on_own_group(work, which=(0, 1)):
        for g in which:
            pl.when(plane // size == g)(functools.partial(work, g))

    def others_of(g, work):
        for index in range(size):
            piece = g * size + index
            pl.when(piece != plane)(functools.partial(work, piece))

    weight = weight_ref[pl.ds(spot * (RB_LOC // PLANE) + own_index // (half_probes // rows), 1), :]

    def product(k):
        return lax.dot_general(
            field_ref[plan_ref[1, k]], blocks_ref[plan_ref[0, k]], (((1,), (1,)), ((), ())), preferred_element_type=F32
        )

    def forward():
        running_sums(plan_ref, 0, blocks_ref.shape[0], product, products, sums)
        for block in range(RB_LOC):
            value = block_sum(plan_ref, 0, block, sums)
            for start in range(0, 2 * half_probes, rows):
                half, at = divmod(start, half_probes)
                piece = half * size + (block % 2 * half_probes + at) // rows
                mine_ref[block // 2, piece] = value[start : start + rows]

    def begin_group(g):
        for d in in_planes:
            scatter_a_plane(d, g).start()

    def plane_sums(g):
        for d in in_planes:
            scatter_a_plane(d, g).wait_recv()
        for index in range(size):
            piece = g * size + index
            total = mine_ref[spot, piece, 0:cut].astype(F32)
            for other in range(PLANE - 1):
                total = total + first[other, piece].astype(F32)
            part[piece] = total.astype(BF16)

            @pl.when(piece != plane)
            def _():
                scatter_a_line(piece).start()

    def own_rows(g):
        for d in in_lines:
            copy(a_line, (d - 1,), part.at[plane], second.at[d - 1], in_line(d)).wait_recv()
        total = part[plane].astype(F32)
        for other in range(planes - 1):
            total = total + second[other].astype(F32)
        upper[g][spot * size + own_index] = (total * weight).astype(BF16)
        for d in in_lines:
            gather_a_line(d, g).start()

    def spread_group(g):
        for turn in range(size):
            index = lax.rem(own_index + turn, size)
            piece = g * size + index

            @pl.when(piece != plane)
            def _():
                where = upper[g].at[spot * size + index]
                copy(ga_line, (sender(piece) - 1,), where, where, in_line(1)).wait_recv()

            for d in in_planes:
                gather_a_plane(d, g, index).start()

    def line_sums():
        for d in in_lines:
            scatter_c_line(d).wait_recv()
        for d in [*in_planes, 0]:
            piece = spot_of(d)
            total = mine_ref[piece, plane, cut:rows].astype(F32)
            for other in range(planes - 1):
                total = total + line[other, piece].astype(F32)
            mixed[piece] = total.astype(BF16)
            if d:
                scatter_c_plane(d).start()

    def own_lower_rows(g):
        for d in in_planes:
            scatter_c_plane(d).wait_recv()
        total = mixed[spot].astype(F32)
        for other in range(PLANE - 1):
            total = total + last[other].astype(F32)
        lower[g][own_index * PLANE + spot] = (total * weight).astype(BF16)
        for d in in_planes:
            gather_c_plane(d, g).start()

    def spread_lower_rows(g):
        for d in in_planes:
            gather_c_plane(d, g).wait_recv()
        for d in in_lines:
            gather_c_line(d, g).start()

    def run():
        begin_group(0)
        for d in in_lines:
            scatter_c_line(d).start()
        begin_group(1)
        plane_sums(0)
        line_sums()
        plane_sums(1)
        on_own_group(own_rows, (0,))
        on_own_group(own_lower_rows)
        on_own_group(own_rows, (1,))
        spread_group(0)
        on_own_group(spread_lower_rows, (0,))
        spread_group(1)
        on_own_group(spread_lower_rows, (1,))

    def ready(g):
        for d in in_planes:
            for index in range(size):
                gather_a_plane(d, g, index).wait_recv()

        def landed(piece):
            where = lower[g].at[pl.ds(piece % size * PLANE, PLANE)]
            copy(gc_line, (sender(piece) - 1,), where, where, in_line(1)).wait_recv()

        others_of(g, landed)

    def finish():
        for d in in_planes:
            for g in range(groups):
                scatter_a_plane(d, g).wait_send()
                for index in range(size):
                    gather_a_plane(d, g, index).wait_send()
            scatter_c_plane(d).wait_send()
            gather_c_plane(d, 0).wait_send()
        for d in in_lines:
            gather_c_line(d, 0).wait_send()
            gather_a_line(d, 0).wait_send()
            scatter_c_line(d).wait_send()
            copy(a_line, (d - 1,), part.at[plane], second.at[d - 1], in_line(d)).wait_send()

    partners = [in_plane(d) for d in in_planes] + [in_line(d) for d in in_lines]
    return partners, forward, run, ready, finish


def hessian_kernel(n_src, plan_ref, field_ref, blocks_ref, weight_ref, probes_ref, kext_ref, out_ref, *scratch):
    (
        products, sums, mine, first, part, second, line, mixed, last,
        upper_far, upper_near, lower_far, lower_near, terms_far, terms_near, pair, relayed, joined, far,
        edge, halo, wide, kwide, keep, flat, edge_send, edge_recv, send, recv, *sems,
    ) = scratch
    upper, lower = (upper_far, upper_near), (lower_far, lower_near)
    half_probes = pl.ds(0, field_ref.shape[1] // 2)
    back_products, back_sums = products.at[:, half_probes], sums.at[:, half_probes]
    reduce_partners, forward, run, ready, finish_reduction = reduction(
        n_src // PLANE, plan_ref, field_ref, blocks_ref, weight_ref, products, sums, mine, first, part, second, line, mixed,
        last, upper, lower, *sems,
    )
    me, group, before, after, twin, opposite = neighbours(n_src)
    lat = kext_ref.shape[0] - 16
    loc, lon = probes_ref.shape[0] // lat, probes_ref.shape[1]
    slabs = loc // SLAB
    core = group % 2
    partners = [before, after, (me, twin), (me, opposite), *reduce_partners]
    announce(partners)
    forward()
    await_all(partners)
    run()

    def view(ref, k, offset=0):
        if isinstance(k, int) and k < 2:
            return ref.at[pl.ds(k * (lat - SMOOTH), SMOOTH), pl.ds(pl.multiple_of(offset, loc), loc), :]
        start = pl.multiple_of(offset + (k - 2) * SLAB, SLAB)
        return ref.at[pl.ds(SMOOTH, lat - 2 * SMOOTH), pl.ds(start, SLAB), :]

    def term(terms, core_of, k):
        return view(terms, k, core_of * loc)

    def adjoint(half, terms):
        pieces = upper_far.shape[0] // RB_LOC

        def product(k):
            receptor, low = plan_ref[9, k], plan_ref[13, k]
            rows = []
            for piece in range(pieces):
                rows += [upper[half][receptor * pieces + piece], lower[half][low + piece * PLANE]]
            return jnp.dot(jnp.concatenate(rows, axis=0), blocks_ref[plan_ref[8, k]], preferred_element_type=F32)

        running_sums(plan_ref, 8, blocks_ref.shape[0], product, back_products, back_sums)
        for row in range(lat):
            for side in range(2):
                terms[row, :, side * BLK : (side + 1) * BLK] = block_sum(plan_ref, 8, 2 * row + side, back_sums)

    def for_relay(k):
        return remote(term(terms_far, 1 - core, k), view(relayed, k), send.at[0, k], recv.at[0, k], (me, twin))

    def for_twin(k):
        return remote(term(terms_near, 1 - core, k), view(pair, k), send.at[1, k], recv.at[1, k], (me, twin))

    def across(k):
        return remote(view(joined, k), view(far, k), send.at[2, k], recv.at[2, k], (me, opposite))

    def each(work):
        work(0)
        work(1)
        lax.fori_loop(2, slabs + 2, lambda k, carry: (work(k), carry)[1], 0)

    def join(k):
        for_relay(k).wait_recv()
        view(joined, k)[...] = (
            term(terms_far, core, k)[...].astype(F32) + view(relayed, k)[...].astype(F32)
        ).astype(BF16)
        across(k).start()

    def total(k):
        for_twin(k).wait_recv()
        across(k).wait_recv()
        return term(terms_near, core, k)[...].astype(F32) + view(pair, k)[...].astype(F32) + view(far, k)[...].astype(F32)

    edges = [
        remote(edge.at[0], halo.at[1], edge_send.at[0], edge_recv.at[0], before),
        remote(edge.at[1], halo.at[0], edge_send.at[1], edge_recv.at[1], after),
    ]
    ready(0)
    adjoint(0, terms_far)
    each(lambda k: for_relay(k).start())
    spread_kappa(n_src, me, kext_ref, kwide, keep, range(lat + 2 * SMOOTH))
    each(join)
    ready(1)
    adjoint(1, terms_near)
    each(lambda k: for_twin(k).start())
    for k, row in ((0, SMOOTH), (1, lat)):
        rows = total(k)
        wide[row : row + SMOOTH] = rows
        edge[k] = rows.astype(BF16)
        edges[k].start()

    def one_slab(slab, carry):
        probes_here = pl.ds(pl.multiple_of(slab * SLAB, SLAB), SLAB)
        wide[2 * SMOOTH : lat, probes_here, :] = total(slab + 2)

        @pl.when(slab == 0)
        def _():
            for copy in edges:
                copy.wait()
            wide[0:SMOOTH] = halo[0].astype(F32)
            wide[lat + SMOOTH :] = halo[1].astype(F32)

        for half in range(SLAB // 8):
            some = pl.ds(pl.multiple_of(slab * SLAB + half * 8, 8), 8)
            value = halves_of(wide, slice(None), some)
            for step in range(SMOOTH):
                rows = slice(step, lat + 2 * SMOOTH - step)
                scaled = [w * v for w, v in zip(halves_of(kwide, rows, slice(None)), value)]
                around = beside(*[v[1:-1] for v in scaled])
                inner = slice(step + 1, lat + 2 * SMOOTH - 1 - step)
                value = [
                    v[1:-1] * k + (g[:-2] + g[2:] + a)
                    for v, k, g, a in zip(value, halves_of(keep, inner, slice(None)), scaled, around)
                ]
            for side in range(2):
                for row in range(lat):
                    flat[side, pl.ds(half * 8 * lat + row, 8, stride=lat), :] = value[side][row]
        some = pl.ds(pl.multiple_of(slab * SLAB * lat, SLAB * lat), SLAB * lat)
        for side in range(2):
            lanes = slice(side * BLK, (side + 1) * BLK)
            out_ref[some, lanes] = flat[side] + probes_ref[some, lanes].astype(F32)
        return carry

    lax.fori_loop(0, slabs, one_slab, 0)

    def finish(k):
        for_relay(k).wait_send()
        for_twin(k).wait_send()
        across(k).wait_send()

    each(finish)
    finish_reduction()


def hessian_part(n_src, plan, field, blocks, weight, probes, kext):
    lat = kext.shape[0] - 16
    loc, lon = probes.shape[0] // lat, probes.shape[1]
    total, slots = field.shape[1], blocks.shape[0]
    half = total // 2
    planes = n_src // PLANE
    rows = RB_LOC * total // (PLANE * planes)
    cut = rows * 3 // 4
    rest = rows - cut
    pieces = loc // SLAB + 2
    together = min(TOGETHER, slots)
    dma = pltpu.SemaphoreType.DMA
    per_spot, per_plane, parts = (PLANE - 1,), (planes - 1,), (PLANE - 1, 2)
    each = (PLANE - 1, planes)
    counts = (parts, per_plane, per_plane, per_spot, per_plane, each, per_spot, per_plane)
    held = [
        (slots, total, BLK),
        (PLANE, planes, rows, BLK),
        (PLANE - 1, planes, cut, BLK),
        (planes, cut, BLK),
        (planes - 1, cut, BLK),
        (planes - 1, PLANE, rest, BLK),
        (PLANE, rest, BLK),
        (PLANE - 1, rest, BLK),
        *[(PLANE * planes // 2, cut, BLK)] * 2,
        *[(PLANE * planes // 2, rest, BLK)] * 2,
        *[(lat, half, lon)] * 2,
        *[(lat, loc, lon)] * 4,
        *[(2, SMOOTH, loc, lon)] * 2,
    ]
    return pl.pallas_call(
        functools.partial(hessian_kernel, n_src),
        out_shape=jax.ShapeDtypeStruct(probes.shape, F32),
        in_specs=[pl.BlockSpec(memory_space=pltpu.SMEM)] + [pl.BlockSpec(memory_space=VMEM)] * 5,
        out_specs=pl.BlockSpec(memory_space=VMEM),
        scratch_shapes=[
            VMEM((together, total, BLK), F32),
            VMEM(held[0], BF16),
            *[VMEM(shape, BF16) for shape in held[1:]],
            VMEM((lat + 2 * SMOOTH, loc, lon), F32),
            VMEM((lat + 2 * SMOOTH, 8, lon), F32),
            VMEM((lat + 2 * SMOOTH, 8, lon), F32),
            VMEM((lon // BLK, SLAB * lat, BLK), F32),
            dma((2,)),
            dma((2,)),
            dma((3, pieces)),
            dma((3, pieces)),
        ]
        + [dma(count) for count in counts for _ in range(2)],
        compiler_params=pltpu.CompilerParams(
            collective_id=1, has_side_effects=True, vmem_limit_bytes=VMEM_LIMIT
        ),
        name="hessian_part",
    )(plan, field, blocks, weight, probes, kext)


def per_device(probes, kappa, footprint, block_source, block_receptor, block_count, obs_weight):
    n_src, n_rcv = lax.axis_size("src"), lax.axis_size("rcv")
    loc, lat, lon = probes.shape
    flat = probes.reshape(loc * lat, lon)
    blocks = footprint.reshape(footprint.shape[2:])
    slots = blocks.shape[0]
    sources, receptors = block_source.reshape(1, slots), block_receptor.reshape(1, slots)
    unused = lax.broadcasted_iota(jnp.int32, (1, slots), 1) >= block_count.reshape(1, 1)
    packed = sources + SLOT_BASE * (receptors + SLOT_BASE * unused.astype(jnp.int32))
    field, kext, plan = smooth_and_gather(n_src, n_rcv, flat, kappa, packed)
    out = hessian_part(n_src, plan, field, blocks, obs_weight.reshape(RB_LOC, BLK), flat, kext)
    return out.reshape(loc, lat, lon)


def solution(mesh):
    placed = (
        P("rcv", "src", None),
        P("src", None),
        P("src", "rcv", None, None, None),
        P("src", "rcv", None),
        P("src", "rcv", None),
        P("src", "rcv"),
        P("rcv"),
    )
    return jax.shard_map(
        per_device, mesh=mesh, in_specs=placed, out_specs=P("rcv", "src", None), check_vma=False
    )
```

```python
import functools

import jax
import jax.numpy as jnp
from jax import lax
from jax.experimental import pallas as pl
from jax.experimental.pallas import tpu as pltpu
from jax.sharding import PartitionSpec as P

BLK = 128
RB_LOC = 16
SMOOTH = 4
PLANE = 8
SLAB = 16
SLOT_BASE = 64
TOGETHER = 64
SHIFTS = ((0, 0), (1, 2), (1, 1), (1, 3), (0, 2), (1, 0), (0, 1), (0, 3))
MESH = pl.DeviceIdType.MESH
VMEM = pltpu.VMEM
F32 = jnp.float32
BF16 = jnp.bfloat16
VMEM_LIMIT = 40 * 1024 * 1024


def announce(devices):
    barrier = pltpu.get_barrier_semaphore()
    for device in devices:
        pl.semaphore_signal(barrier, inc=1, device_id=device, device_id_type=MESH)


def await_all(devices):
    pl.semaphore_wait(pltpu.get_barrier_semaphore(), len(devices))


def remote(src, dst, send_sem, recv_sem, device):
    return pltpu.make_async_remote_copy(
        src_ref=src,
        dst_ref=dst,
        send_sem=send_sem,
        recv_sem=recv_sem,
        device_id=device,
        device_id_type=MESH,
    )


def neighbours(n_src):
    me = lax.axis_index("src")
    group = lax.axis_index("rcv")
    high, core = group // 2, group % 2
    before = (lax.rem(me + n_src - 1, n_src), group)
    after = (lax.rem(me + 1, n_src), group)
    twin = high * 2 + (1 - core)
    opposite = (1 - high) * 2 + core
    return me, group, before, after, twin, opposite


def beside(west_half, east_half):
    axis = west_half.ndim - 1
    lane = lax.broadcasted_iota(jnp.int32, west_half.shape, axis)
    first, last = lane == 0, lane == BLK - 1
    up_w, up_e = pltpu.roll(west_half, 1, axis), pltpu.roll(east_half, 1, axis)
    down_w, down_e = pltpu.roll(west_half, BLK - 1, axis), pltpu.roll(east_half, BLK - 1, axis)
    return (
        jnp.where(first, 0.0, up_w) + jnp.where(last, down_e, down_w),
        jnp.where(first, up_w, up_e) + jnp.where(last, 0.0, down_e),
    )


def halves_of(ref, rows, *middle):
    return [ref[(rows, *middle, slice(side * BLK, (side + 1) * BLK))] for side in range(2)]


def spread_kappa(n_src, me, kext_ref, kwide, keep, rows):
    for row in rows:
        value = kext_ref[8 - SMOOTH + row : 8 - SMOOTH + row + 1, :]
        if row < SMOOTH:
            value = jnp.where(me == 0, 0.0, value)
        if row >= kwide.shape[0] - SMOOTH:
            value = jnp.where(me == n_src - 1, 0.0, value)
        wide = jnp.broadcast_to(value, kwide.shape[1:])
        kwide[row] = wide
        keep[row] = 1.0 - 4.0 * wide


def make_plan(lower_pieces, packed, plan_ref):
    slots, lanes = packed.shape[1], plan_ref.shape[1]
    sources, receptors = packed % SLOT_BASE, packed // SLOT_BASE % SLOT_BASE
    row_of = lax.broadcasted_iota(jnp.int32, (slots, slots), 0)
    lane_of = lax.broadcasted_iota(jnp.int32, (slots, slots), 1)
    place = lax.broadcasted_iota(jnp.int32, (slots, lanes), 1)
    slot = lax.broadcasted_iota(jnp.int32, (1, slots), 1)
    used = packed < SLOT_BASE * SLOT_BASE

    def column(row):
        return jnp.sum(jnp.where(row_of == lane_of, row, 0.0), axis=1, keepdims=True)

    first_lane = lax.broadcasted_iota(jnp.int32, (1, lanes), 1) == 0
    for base, owner, other in ((0, receptors, sources), (8, sources, receptors)):
        key = jnp.where(used, owner * 256 + slot, 64 * 256 + slot).astype(F32)
        tall = column(key)
        rank = jnp.sum(jnp.where(key < tall, 1.0, 0.0), axis=1, keepdims=True)
        here = rank.astype(jnp.int32) == place

        def ordered(values):
            return jnp.sum(jnp.where(here, values, 0.0), axis=0, keepdims=True).astype(jnp.int32)

        keys = ordered(tall)
        block = keys // 256
        ends = jnp.sum(
            jnp.where(tall < ((place + 1) * 256).astype(F32), 1.0, 0.0), axis=0, keepdims=True
        ).astype(jnp.int32)
        start = jnp.where(first_lane, 0, pltpu.roll(ends, 1, 1))
        same = (block == pltpu.roll(block, 1, 1)) & jnp.logical_not(first_lane)
        plan_ref[base : base + 1, :] = keys - block * 256
        plan_ref[base + 1 : base + 2, :] = ordered(column(other.astype(F32)))
        plan_ref[base + 2 : base + 3, :] = same.astype(jnp.int32)
        plan_ref[base + 3 : base + 4, :] = jnp.maximum(ends - 1, 0)
        if base:
            lower = other % 2 * (lower_pieces * PLANE) + other // 2
            plan_ref[base + 5 : base + 6, :] = ordered(column(lower.astype(F32)))
        plan_ref[base + 4 : base + 5, :] = (ends > start).astype(jnp.int32)


def smooth_kernel(
    n_src, probes_ref, kappa_ref, slots_ref, field_ref, kext_ref, plan_ref, flat, halo, edge, wide, kwide, keep,
    edge_send, edge_recv, send, recv,
):
    me, group, before, after, twin, opposite = neighbours(n_src)
    lat, lon = kappa_ref.shape
    loc = probes_ref.shape[0] // lat
    slabs = loc // SLAB
    partners = [before, after, (me, twin), (me, opposite)]
    announce(partners)

    top, bottom = range(SMOOTH), range(lat - SMOOTH, lat)
    for side in range(lon // BLK):
        flat[side] = probes_ref[:, side * BLK : (side + 1) * BLK].astype(F32)

    def of_row(row):
        return jnp.concatenate([flat[side, pl.ds(row, loc, stride=lat), :] for side in range(lon // BLK)], axis=1)

    for side, rows in enumerate((top, bottom)):
        for place, row in enumerate(rows):
            value = of_row(row)
            wide[SMOOTH + row] = value
            edge[side, place] = value.astype(BF16)
    for row in range(SMOOTH, lat - SMOOTH):
        wide[SMOOTH + row] = of_row(row)
    kext_ref[8 : lat + 8, :] = kappa_ref[...]
    spread_kappa(n_src, me, kext_ref, kwide, keep, range(SMOOTH, lat + SMOOTH))
    edges = [
        remote(edge.at[1], halo.at[0], edge_send.at[0], edge_recv.at[0], after),
        remote(edge.at[0], halo.at[1], edge_send.at[1], edge_recv.at[1], before),
        remote(kappa_ref.at[pl.ds(lat - 8, 8)], kext_ref.at[pl.ds(0, 8)], edge_send.at[2], edge_recv.at[2], after),
        remote(kappa_ref.at[pl.ds(0, 8)], kext_ref.at[pl.ds(lat + 8, 8)], edge_send.at[3], edge_recv.at[3], before),
    ]

    parts = ((SMOOTH, lat - SMOOTH), (0, SMOOTH), (lat - SMOOTH, lat))

    core = group % 2
    own, far = 2 + core, core

    def place(owner, part, slab):
        first, last = parts[part]
        return field_ref.at[
            pl.ds(2 * first, 2 * (last - first)), pl.ds(pl.multiple_of(owner * loc + slab * SLAB, SLAB), SLAB), :
        ]

    def to_twin(part, slab):
        where = place(own, part, slab)
        return remote(where, where, send.at[0, part, slab], recv.at[0, part, slab], (me, twin))

    def to_opposite(part, slab):
        there = place(far, part, slab)
        return remote(place(own, part, slab), there, send.at[1, part, slab], recv.at[1, part, slab], (me, opposite))

    def relay(part, slab):
        where = place(far, part, slab)
        return remote(where, where, send.at[2, part, slab], recv.at[2, part, slab], (me, twin))

    def smooth_part(part, slab):
        first, last = parts[part]
        groups = []
        for half in range(SLAB // 8):
            some = pl.ds(pl.multiple_of(slab * SLAB + half * 8, 8), 8)
            value = halves_of(wide, slice(first, last + 2 * SMOOTH), some)
            for step in range(SMOOTH):
                rows = slice(first + step + 1, last + 2 * SMOOTH - 1 - step)
                centre = [v[1:-1] for v in value]
                around = beside(*centre)
                value = [
                    c * k + w * (v[:-2] + v[2:] + a)
                    for c, k, w, v, a in zip(
                        centre, halves_of(keep, rows, slice(None)), halves_of(kwide, rows, slice(None)), value, around
                    )
                ]
            groups.append(value)
        mine = pl.ds(pl.multiple_of(own * loc + slab * SLAB, SLAB), SLAB)
        for side in range(2):
            smoothed = jnp.concatenate([g[side] for g in groups], axis=1).astype(BF16)
            for row in range(first, last):
                field_ref[2 * row + side, mine, :] = smoothed[row - first]

    def post(part, slab):
        to_opposite(part, slab).start()
        to_twin(part, slab).start()

    def inner(slab, carry):
        smooth_part(0, slab)
        post(0, slab)
        return carry

    def outer(slab, carry):
        for part in (1, 2):
            smooth_part(part, slab)
            post(part, slab)
        return carry

    smooth_part(0, 0)
    await_all(partners)
    post(0, 0)
    for copy in edges:
        copy.start()
    lax.fori_loop(1, slabs, inner, 0)
    for copy in edges:
        copy.wait()
    wide[0:SMOOTH] = jnp.where(me == 0, 0.0, halo[0].astype(F32))
    wide[lat + SMOOTH :] = jnp.where(me == n_src - 1, 0.0, halo[1].astype(F32))
    spread_kappa(n_src, me, kext_ref, kwide, keep, [*range(SMOOTH), *range(lat + SMOOTH, lat + 2 * SMOOTH)])
    lax.fori_loop(0, slabs, outer, 0)
    make_plan(n_src // PLANE // 4, slots_ref[...], plan_ref)

    def pass_on(parts_here):
        def one(slab, carry):
            for part in parts_here:
                to_opposite(part, slab).wait_recv()
                relay(part, slab).start()
            return carry

        lax.fori_loop(0, slabs, one, 0)

    pass_on((0,))
    pass_on((1, 2))

    def finish(slab, carry):
        for part in range(3):
            to_opposite(part, slab).wait_send()
            to_twin(part, slab).wait()
            relay(part, slab).wait()
        return carry

    lax.fori_loop(0, slabs, finish, 0)


def smooth_and_gather(n_src, n_rcv, probes, kappa, packed):
    lat, lon = kappa.shape
    loc = probes.shape[0] // lat
    slabs = loc // SLAB
    dma = pltpu.SemaphoreType.DMA
    return pl.pallas_call(
        functools.partial(smooth_kernel, n_src),
        out_shape=(
            jax.ShapeDtypeStruct((lat * lon // BLK, loc * n_rcv, BLK), BF16),
            jax.ShapeDtypeStruct((lat + 16, lon), F32),
            jax.ShapeDtypeStruct((16, 256), jnp.int32),
        ),
        in_specs=[pl.BlockSpec(memory_space=VMEM)] * 3,
        out_specs=(pl.BlockSpec(memory_space=VMEM),) * 3,
        scratch_shapes=[
            VMEM((lon // BLK, loc * lat, BLK), F32),
            VMEM((2, SMOOTH, loc, lon), BF16),
            VMEM((2, SMOOTH, loc, lon), BF16),
            VMEM((lat + 2 * SMOOTH, loc, lon), F32),
            VMEM((lat + 2 * SMOOTH, 8, lon), F32),
            VMEM((lat + 2 * SMOOTH, 8, lon), F32),
            dma((4,)),
            dma((4,)),
            dma((3, 3, slabs)),
            dma((3, 3, slabs)),
        ],
        compiler_params=pltpu.CompilerParams(
            collective_id=0, has_side_effects=True, vmem_limit_bytes=VMEM_LIMIT
        ),
        cost_estimate=pl.CostEstimate(flops=20_000_000_000, bytes_accessed=64_000_000, transcendentals=0),
        name="smooth_and_gather",
    )(probes, kappa, packed)


def running_sums(plan_ref, base, slots, product, products, sums):
    together = products.shape[0]

    def several(turn, total):
        for step in range(together):
            k = turn * together + step
            products[step] = product(k)
        for step in range(together):
            k = turn * together + step
            total = products[step] + total * plan_ref[base + 2, k].astype(F32)
            sums[k] = total.astype(BF16)
        return total

    lax.fori_loop(0, slots // together, several, jnp.zeros(sums.shape[1:], F32))


def block_sum(plan_ref, base, block, sums):
    value = sums[plan_ref[base + 3, block]]
    return (value.astype(F32) * plan_ref[base + 4, block].astype(F32)).astype(BF16)


def reduction(planes, plan_ref, field_ref, blocks_ref, weight_ref, products, sums, mine_ref, first, part, second, line, mixed, last, upper, lower, *sems):
    me = lax.axis_index("src")
    group = lax.axis_index("rcv")
    plane, spot = me // PLANE, me % PLANE
    pairs = iter(sems)
    a_plane, a_line, c_line, c_plane, ga_line, ga_plane, gc_plane, gc_line = zip(pairs, pairs)
    rows = mine_ref.shape[2]
    cut = rows * 3 // 4
    upper_rows, lower_rows = pl.ds(0, cut), pl.ds(cut, rows - cut)
    half_probes = field_ref.shape[1] // 2
    groups = 2
    size = planes // groups
    in_planes = range(1, PLANE)
    in_lines = range(1, planes)

    def spot_of(distance):
        across, along = SHIFTS[distance]
        return lax.rem(spot // 4 + across, 2) * 4 + lax.rem(spot % 4 + along, 4)

    def plane_of(distance):
        return lax.rem(plane + distance, planes)

    def in_plane(distance):
        return (plane * PLANE + spot_of(distance), group)

    def in_line(distance):
        return (plane_of(distance) * PLANE + spot, group)

    def copy(pair, index, src, dst, device):
        return remote(src, dst, pair[0].at[index], pair[1].at[index], device)

    def some(g):
        return pl.ds(g * size, size)

    def scatter_a_plane(d, g):
        return copy(
            a_plane, (d - 1, g), mine_ref.at[spot_of(d), some(g), upper_rows], first.at[d - 1, some(g)], in_plane(d)
        )

    def scatter_a_line(piece):
        d = lax.rem(piece + planes - plane, planes)
        return copy(a_line, (d - 1,), part.at[piece], second.at[d - 1], (piece * PLANE + spot, group))

    def scatter_c_line(d):
        return copy(c_line, (d - 1,), mine_ref.at[:, plane_of(d), lower_rows], line.at[d - 1], in_line(d))

    def scatter_c_plane(d):
        return copy(c_plane, (d - 1,), mixed.at[spot_of(d)], last.at[d - 1], in_plane(d))

    own_index = plane % size

    def gather_a_line(d, g):
        where = upper[g].at[spot * size + own_index]
        return copy(ga_line, (d - 1,), where, where, in_line(d))

    def gather_a_plane(d, g):
        where = upper[g].at[pl.ds(spot * size, size)]
        return copy(ga_plane, (d - 1, g), where, where, in_plane(d))

    def gather_c_plane(d, g):
        where = lower[g].at[own_index * PLANE + spot]
        return copy(gc_plane, (d - 1,), where, where, in_plane(d))

    def gather_c_line(d, g):
        where = lower[g].at[pl.ds(own_index * PLANE, PLANE)]
        return copy(gc_line, (d - 1,), where, where, in_line(d))

    def sender(piece):
        return lax.rem(plane + planes - piece, planes)

    def on_own_group(work, which=(0, 1)):
        for g in which:
            pl.when(plane // size == g)(functools.partial(work, g))

    def others_of(g, work):
        for index in range(size):
            piece = g * size + index
            pl.when(piece != plane)(functools.partial(work, piece))

    weight = weight_ref[pl.ds(spot * (RB_LOC // PLANE) + own_index // (half_probes // rows), 1), :]

    def product(k):
        return lax.dot_general(
            field_ref[plan_ref[1, k]], blocks_ref[plan_ref[0, k]], (((1,), (1,)), ((), ())), preferred_element_type=F32
        )

    def forward():
        running_sums(plan_ref, 0, blocks_ref.shape[0], product, products, sums)
        for block in range(RB_LOC):
            value = block_sum(plan_ref, 0, block, sums)
            for start in range(0, 2 * half_probes, rows):
                half, at = divmod(start, half_probes)
                piece = half * size + (block % 2 * half_probes + at) // rows
                mine_ref[block // 2, piece] = value[start : start + rows]

    def begin_group(g):
        for d in in_planes:
            scatter_a_plane(d, g).start()

    def plane_sums(g):
        for d in in_planes:
            scatter_a_plane(d, g).wait_recv()
        for index in range(size):
            piece = g * size + index
            total = mine_ref[spot, piece, 0:cut].astype(F32)
            for other in range(PLANE - 1):
                total = total + first[other, piece].astype(F32)
            part[piece] = total.astype(BF16)

            @pl.when(piece != plane)
            def _():
                scatter_a_line(piece).start()

    def own_rows(g):
        for d in in_lines:
            copy(a_line, (d - 1,), part.at[plane], second.at[d - 1], in_line(d)).wait_recv()
        total = part[plane].astype(F32)
        for other in range(planes - 1):
            total = total + second[other].astype(F32)
        upper[g][spot * size + own_index] = (total * weight).astype(BF16)
        for d in in_lines:
            gather_a_line(d, g).start()

    def spread_group(g):
        def landed(piece):
            where = upper[g].at[spot * size + piece % size]
            copy(ga_line, (sender(piece) - 1,), where, where, in_line(1)).wait_recv()

        others_of(g, landed)
        for d in in_planes:
            gather_a_plane(d, g).start()

    def line_sums():
        for d in in_lines:
            scatter_c_line(d).wait_recv()
        for d in [*in_planes, 0]:
            piece = spot_of(d)
            total = mine_ref[piece, plane, cut:rows].astype(F32)
            for other in range(planes - 1):
                total = total + line[other, piece].astype(F32)
            mixed[piece] = total.astype(BF16)
            if d:
                scatter_c_plane(d).start()

    def own_lower_rows(g):
        for d in in_planes:
            scatter_c_plane(d).wait_recv()
        total = mixed[spot].astype(F32)
        for other in range(PLANE - 1):
            total = total + last[other].astype(F32)
        lower[g][own_index * PLANE + spot] = (total * weight).astype(BF16)
        for d in in_planes:
            gather_c_plane(d, g).start()

    def spread_lower_rows(g):
        for d in in_planes:
            gather_c_plane(d, g).wait_recv()
        for d in in_lines:
            gather_c_line(d, g).start()

    def run():
        begin_group(0)
        for d in in_lines:
            scatter_c_line(d).start()
        begin_group(1)
        plane_sums(0)
        line_sums()
        plane_sums(1)
        on_own_group(own_rows, (0,))
        on_own_group(own_lower_rows)
        on_own_group(own_rows, (1,))
        spread_group(0)
        on_own_group(spread_lower_rows, (0,))
        spread_group(1)
        on_own_group(spread_lower_rows, (1,))

    def ready(g):
        for d in in_planes:
            gather_a_plane(d, g).wait_recv()

        def landed(piece):
            where = lower[g].at[pl.ds(piece % size * PLANE, PLANE)]
            copy(gc_line, (sender(piece) - 1,), where, where, in_line(1)).wait_recv()

        others_of(g, landed)

    def finish():
        for d in in_planes:
            for g in range(groups):
                gather_a_plane(d, g).wait_send()
                scatter_a_plane(d, g).wait_send()
            scatter_c_plane(d).wait_send()
            gather_c_plane(d, 0).wait_send()
        for d in in_lines:
            gather_c_line(d, 0).wait_send()
            gather_a_line(d, 0).wait_send()
            scatter_c_line(d).wait_send()
            copy(a_line, (d - 1,), part.at[plane], second.at[d - 1], in_line(d)).wait_send()

    partners = [in_plane(d) for d in in_planes] + [in_line(d) for d in in_lines]
    return partners, forward, run, ready, finish


def hessian_kernel(n_src, plan_ref, field_ref, blocks_ref, weight_ref, probes_ref, kext_ref, out_ref, *scratch):
    (
        products, sums, mine, first, part, second, line, mixed, last,
        upper_far, upper_near, lower_far, lower_near, terms_far, terms_near, pair, relayed, joined, far,
        edge, halo, wide, kwide, keep, flat, edge_send, edge_recv, send, recv, *sems,
    ) = scratch
    upper, lower = (upper_far, upper_near), (lower_far, lower_near)
    half_probes = pl.ds(0, field_ref.shape[1] // 2)
    back_products, back_sums = products.at[:, half_probes], sums.at[:, half_probes]
    reduce_partners, forward, run, ready, finish_reduction = reduction(
        n_src // PLANE, plan_ref, field_ref, blocks_ref, weight_ref, products, sums, mine, first, part, second, line, mixed,
        last, upper, lower, *sems,
    )
    me, group, before, after, twin, opposite = neighbours(n_src)
    lat = kext_ref.shape[0] - 16
    loc, lon = probes_ref.shape[0] // lat, probes_ref.shape[1]
    slabs = loc // SLAB
    core = group % 2
    partners = [before, after, (me, twin), (me, opposite), *reduce_partners]
    announce(partners)
    forward()
    await_all(partners)
    run()

    def view(ref, k, offset=0):
        if isinstance(k, int) and k < 2:
            return ref.at[pl.ds(k * (lat - SMOOTH), SMOOTH), pl.ds(pl.multiple_of(offset, loc), loc), :]
        start = pl.multiple_of(offset + (k - 2) * SLAB, SLAB)
        return ref.at[pl.ds(SMOOTH, lat - 2 * SMOOTH), pl.ds(start, SLAB), :]

    def term(terms, core_of, k):
        return view(terms, k, core_of * loc)

    def adjoint(half, terms):
        pieces = upper_far.shape[0] // RB_LOC

        def product(k):
            receptor, low = plan_ref[9, k], plan_ref[13, k]
            rows = []
            for piece in range(pieces):
                rows += [upper[half][receptor * pieces + piece], lower[half][low + piece * PLANE]]
            return jnp.dot(jnp.concatenate(rows, axis=0), blocks_ref[plan_ref[8, k]], preferred_element_type=F32)

        running_sums(plan_ref, 8, blocks_ref.shape[0], product, back_products, back_sums)
        for row in range(lat):
            for side in range(2):
                terms[row, :, side * BLK : (side + 1) * BLK] = block_sum(plan_ref, 8, 2 * row + side, back_sums)

    def for_relay(k):
        return remote(term(terms_far, 1 - core, k), view(relayed, k), send.at[0, k], recv.at[0, k], (me, twin))

    def for_twin(k):
        return remote(term(terms_near, 1 - core, k), view(pair, k), send.at[1, k], recv.at[1, k], (me, twin))

    def across(k):
        return remote(view(joined, k), view(far, k), send.at[2, k], recv.at[2, k], (me, opposite))

    def each(work):
        work(0)
        work(1)
        lax.fori_loop(2, slabs + 2, lambda k, carry: (work(k), carry)[1], 0)

    def join(k):
        for_relay(k).wait_recv()
        view(joined, k)[...] = (
            term(terms_far, core, k)[...].astype(F32) + view(relayed, k)[...].astype(F32)
        ).astype(BF16)
        across(k).start()

    def total(k):
        for_twin(k).wait_recv()
        across(k).wait_recv()
        return term(terms_near, core, k)[...].astype(F32) + view(pair, k)[...].astype(F32) + view(far, k)[...].astype(F32)

    edges = [
        remote(edge.at[0], halo.at[1], edge_send.at[0], edge_recv.at[0], before),
        remote(edge.at[1], halo.at[0], edge_send.at[1], edge_recv.at[1], after),
    ]
    ready(0)
    adjoint(0, terms_far)
    each(lambda k: for_relay(k).start())
    spread_kappa(n_src, me, kext_ref, kwide, keep, range(lat + 2 * SMOOTH))
    each(join)
    ready(1)
    adjoint(1, terms_near)
    each(lambda k: for_twin(k).start())
    for k, row in ((0, SMOOTH), (1, lat)):
        rows = total(k)
        wide[row : row + SMOOTH] = rows
        edge[k] = rows.astype(BF16)
        edges[k].start()

    def one_slab(slab, carry):
        probes_here = pl.ds(pl.multiple_of(slab * SLAB, SLAB), SLAB)
        wide[2 * SMOOTH : lat, probes_here, :] = total(slab + 2)

        @pl.when(slab == 0)
        def _():
            for copy in edges:
                copy.wait()
            wide[0:SMOOTH] = halo[0].astype(F32)
            wide[lat + SMOOTH :] = halo[1].astype(F32)

        for half in range(SLAB // 8):
            some = pl.ds(pl.multiple_of(slab * SLAB + half * 8, 8), 8)
            value = halves_of(wide, slice(None), some)
            for step in range(SMOOTH):
                rows = slice(step, lat + 2 * SMOOTH - step)
                scaled = [w * v for w, v in zip(halves_of(kwide, rows, slice(None)), value)]
                around = beside(*[v[1:-1] for v in scaled])
                inner = slice(step + 1, lat + 2 * SMOOTH - 1 - step)
                value = [
                    v[1:-1] * k + (g[:-2] + g[2:] + a)
                    for v, k, g, a in zip(value, halves_of(keep, inner, slice(None)), scaled, around)
                ]
            for side in range(2):
                for row in range(lat):
                    flat[side, pl.ds(half * 8 * lat + row, 8, stride=lat), :] = value[side][row]
        some = pl.ds(pl.multiple_of(slab * SLAB * lat, SLAB * lat), SLAB * lat)
        for side in range(2):
            lanes = slice(side * BLK, (side + 1) * BLK)
            out_ref[some, lanes] = flat[side] + probes_ref[some, lanes].astype(F32)
        return carry

    lax.fori_loop(0, slabs, one_slab, 0)

    def finish(k):
        for_relay(k).wait_send()
        for_twin(k).wait_send()
        across(k).wait_send()

    each(finish)
    finish_reduction()


def hessian_part(n_src, plan, field, blocks, weight, probes, kext):
    lat = kext.shape[0] - 16
    loc, lon = probes.shape[0] // lat, probes.shape[1]
    total, slots = field.shape[1], blocks.shape[0]
    half = total // 2
    planes = n_src // PLANE
    rows = RB_LOC * total // (PLANE * planes)
    cut = rows * 3 // 4
    rest = rows - cut
    pieces = loc // SLAB + 2
    together = min(TOGETHER, slots)
    dma = pltpu.SemaphoreType.DMA
    per_spot, per_plane, parts = (PLANE - 1,), (planes - 1,), (PLANE - 1, 2)
    counts = (parts, per_plane, per_plane, per_spot, per_plane, parts, per_spot, per_plane)
    held = [
        (slots, total, BLK),
        (PLANE, planes, rows, BLK),
        (PLANE - 1, planes, cut, BLK),
        (planes, cut, BLK),
        (planes - 1, cut, BLK),
        (planes - 1, PLANE, rest, BLK),
        (PLANE, rest, BLK),
        (PLANE - 1, rest, BLK),
        *[(PLANE * planes // 2, cut, BLK)] * 2,
        *[(PLANE * planes // 2, rest, BLK)] * 2,
        *[(lat, half, lon)] * 2,
        *[(lat, loc, lon)] * 4,
        *[(2, SMOOTH, loc, lon)] * 2,
    ]
    return pl.pallas_call(
        functools.partial(hessian_kernel, n_src),
        out_shape=jax.ShapeDtypeStruct(probes.shape, F32),
        in_specs=[pl.BlockSpec(memory_space=pltpu.SMEM)] + [pl.BlockSpec(memory_space=VMEM)] * 5,
        out_specs=pl.BlockSpec(memory_space=VMEM),
        scratch_shapes=[
            VMEM((together, total, BLK), F32),
            VMEM(held[0], BF16),
            *[VMEM(shape, BF16) for shape in held[1:]],
            VMEM((lat + 2 * SMOOTH, loc, lon), F32),
            VMEM((lat + 2 * SMOOTH, 8, lon), F32),
            VMEM((lat + 2 * SMOOTH, 8, lon), F32),
            VMEM((lon // BLK, SLAB * lat, BLK), F32),
            dma((2,)),
            dma((2,)),
            dma((3, pieces)),
            dma((3, pieces)),
        ]
        + [dma(count) for count in counts for _ in range(2)],
        compiler_params=pltpu.CompilerParams(
            collective_id=1, has_side_effects=True, vmem_limit_bytes=VMEM_LIMIT
        ),
        name="hessian_part",
    )(plan, field, blocks, weight, probes, kext)


def per_device(probes, kappa, footprint, block_source, block_receptor, block_count, obs_weight):
    n_src, n_rcv = lax.axis_size("src"), lax.axis_size("rcv")
    loc, lat, lon = probes.shape
    flat = probes.reshape(loc * lat, lon)
    blocks = footprint.reshape(footprint.shape[2:])
    slots = blocks.shape[0]
    sources, receptors = block_source.reshape(1, slots), block_receptor.reshape(1, slots)
    unused = lax.broadcasted_iota(jnp.int32, (1, slots), 1) >= block_count.reshape(1, 1)
    packed = sources + SLOT_BASE * (receptors + SLOT_BASE * unused.astype(jnp.int32))
    field, kext, plan = smooth_and_gather(n_src, n_rcv, flat, kappa, packed)
    out = hessian_part(n_src, plan, field, blocks, obs_weight.reshape(RB_LOC, BLK), flat, kext)
    return out.reshape(loc, lat, lon)


def solution(mesh):
    placed = (
        P("rcv", "src", None),
        P("src", None),
        P("src", "rcv", None, None, None),
        P("src", "rcv", None),
        P("src", "rcv", None),
        P("src", "rcv"),
        P("rcv"),
    )
    return jax.shard_map(
        per_device, mesh=mesh, in_specs=placed, out_specs=P("rcv", "src", None), check_vma=False
    )
```
